32 devices in a mesh: dp: 8 (over z, y), tensor: 4 (over x, core).
Axes of the slice: x: 2, y: 2, z: 4, core: 2. Of those that a mesh axis runs over, the one named last changes fastest.
Arguments:
- patches: bfloat16 [128, 196, 384], P('dp'), may hold values from -6 to 6
- image_count: int32 [8], P('dp'), may hold values from 8 to 16, as said below
- routes: int32 [128, 196], P('dp'), may hold values from 0 to 7
- slot_index: int32 [128, 196], P('dp'), may hold values from -1 to 511, as said below
- norm1_gain: float32 [384], replicated, may hold values from 0.5 to 1.5
- norm1_bias: float32 [384], replicated, may hold values from -1.25 to 1.25
- input_proj: bfloat16 [384, 3, 384], P(None, None, 'tensor'), may hold values from -0.3125 to 0.3125
- query_value_bias: float32 [2, 384], P(None, 'tensor'), may hold values from -1.25 to 1.25
- position_bias: float32 [169, 12], P(None, 'tensor'), may hold values from -6 to 6
- output_proj: bfloat16 [384, 384], P('tensor'), may hold values from -0.875 to 0.875
- output_bias: float32 [384], replicated, may hold values from -1.25 to 1.25
- norm2_gain: float32 [384], replicated, may hold values from 0.5 to 1.5
- norm2_bias: float32 [384], replicated, may hold values from -1.25 to 1.25
- router_weight: bfloat16 [384, 8], replicated, may hold values from -0.21875 to 0.21875
- up_weight: bfloat16 [8, 384, 1536], P(None, None, 'tensor'), may hold values from -0.3125 to 0.3125
- up_bias: float32 [8, 1536], P(None, 'tensor'), may hold values from -1.25 to 1.25
- down_weight: bfloat16 [8, 1536, 384], P(None, 'tensor'), may hold values from -1.25 to 1.25
- down_bias: float32 [8, 384], replicated, may hold values from -6 to 6
- cotangent: bfloat16 [128, 196, 384], P('dp'), may hold values from -6 to 6
Outputs:
- block_out: bfloat16 [128, 196, 384], P('dp')
- grad_patches: float32 [128, 196, 384], P('dp')
- grad_norm1_gain: float32 [384], replicated
- grad_norm1_bias: float32 [384], replicated
- grad_input_proj: float32 [384, 3, 384], P(None, None, 'tensor')
- grad_query_value_bias: float32 [2, 384], P(None, 'tensor')
- grad_position_bias: float32 [169, 12], P(None, 'tensor')
- grad_output_proj: float32 [384, 384], P('tensor')
- grad_output_bias: float32 [384], replicated
- grad_norm2_gain: float32 [384], replicated
- grad_norm2_bias: float32 [384], replicated
- grad_router_weight: float32 [384, 8], replicated
- grad_up_weight: float32 [8, 384, 1536], P(None, None, 'tensor')
- grad_up_bias: float32 [8, 1536], P(None, 'tensor')
- grad_down_weight: float32 [8, 1536, 384], P(None, 'tensor')
- grad_down_bias: float32 [8, 384], replicated
The draws below stay inside these ranges and needn't reach their ends.
Inputs may be any that keep to these rules, and one draw needn't show every extreme that they name: `image_count`: valid images come first within each index of dp; the first index is full and the last holds 8. `slot_index`: within one index of dp, the patches of valid images that go to one expert take slots 0, 1, 2, ... in patch order; those past 512 - 1 and all patches of padded images hold -1; some expert is full on the first index of dp.
All inputs are finite; a program needn't handle non-finite values.
Results may differ from the reference program's by a relative error of at most 0.011.
Values sent between devices are 32-bit elements; how exact they have to be, the bound alone decides.
No kernel may reach another device: no remote copies, remote signals or barrier semaphores. Data moves between devices by JAX's collectives and lax.ppermute only.
A program may use at most 192 MiB of HBM per device.

```python
import jax
import jax.numpy as jnp
from jax import lax

D = 384
HEADS = 12
HD = 32
FF = 1536
WIN = 7
SIDE = 14
SHIFT = 3
E = 8
IMG = 16
LEN = 196
CAP = 512
IMAGES = 128
TABLE = 169
N_DP = 8


def route_plan(key):
    base_key = jax.random.fold_in(key, 11)
    count_key, busy_key, route_key, order_key = jax.random.split(base_key, 4)
    per_device = IMG * LEN
    counts = jax.random.randint(count_key, (N_DP,), IMG // 2, IMG + 1)
    counts = counts.at[0].set(IMG).at[N_DP - 1].set(IMG // 2)
    image_of = jnp.arange(per_device) // LEN
    usable = image_of[None, :] < counts[:, None]
    busiest = jax.random.randint(busy_key, (N_DP,), 0, E)
    chosen = jax.random.randint(route_key, (N_DP, per_device), 0, E)
    order_keys = jax.random.split(order_key, N_DP)
    order_rank = jax.vmap(lambda single: jnp.argsort(jax.random.permutation(single, per_device)))(order_keys)
    forced = (order_rank < CAP) & usable
    chosen_routes = jnp.where(forced, busiest[:, None], chosen)
    onehot = (chosen_routes[:, :, None] == jnp.arange(E)[None, None, :]) & usable[:, :, None]
    running = jnp.cumsum(onehot.astype(jnp.int32), axis=1) - 1
    position = jnp.sum(jnp.where(onehot, running, 0), axis=2)
    slots = jnp.where(usable & (position < CAP), position, -1)
    return (counts.astype(jnp.int32), chosen_routes.reshape(N_DP * IMG, LEN).astype(jnp.int32), slots.reshape(N_DP * IMG, LEN).astype(jnp.int32))


def draw_image_count(key, part):
    return route_plan(key)[0]


def draw_routes(key, part):
    return route_plan(key)[1]


def draw_slot_index(key, part):
    return route_plan(key)[2]


def block_levels(own_key, dims, pieces, least, largest):
    loudness, own = 1.0, jax.random.fold_in(own_key, 6)
    for dim, parts in pieces:
        steps = jnp.exp(jax.random.uniform(jax.random.fold_in(own, dim), (parts,), jnp.float32, least / len(pieces), largest / len(pieces)))
        loudness = loudness * jnp.repeat(steps, dims[dim] // parts).reshape([-1 if axis == dim else 1 for axis in range(len(dims))])
    return loudness


def normal_values(rng, dims, spread, reach, cuts=(), held_as=jnp.bfloat16):
    entries = spread * jax.random.normal(rng, dims, jnp.float32)
    if cuts:
        entries = entries * block_levels(rng, dims, cuts, -0.22, 0.18)
    return jnp.clip(entries, -reach, reach).astype(held_as)


def setup_inputs(seed: int = 0) -> dict:
    key_of = jax.random.split(jax.random.key(seed), 20)
    patches = normal_values(key_of[0], (IMAGES, LEN, D), 1.0, 6.0, ((0, 8),))
    image_count = draw_image_count(jax.random.fold_in(key_of[19], 71), 0)
    routes = draw_routes(jax.random.fold_in(key_of[19], 71), 0)
    slot_index = draw_slot_index(jax.random.fold_in(key_of[19], 71), 0)
    norm1_gain = jnp.clip(1.0 + 0.1 * jax.random.normal(key_of[4], (D,), jnp.float32), 0.5, 1.5)
    norm1_bias = normal_values(key_of[5], (D,), 0.2, 1.25, (), jnp.float32)
    input_proj = normal_values(key_of[6], (D, 3, D), D ** -0.5, 0.3125, ((2, 4),))
    query_value_bias = normal_values(key_of[7], (2, D), 0.2, 1.25, ((1, 4),), jnp.float32)
    position_bias = normal_values(key_of[8], (TABLE, HEADS), 1.0, 6.0, ((1, 4),), jnp.float32)
    output_proj = normal_values(key_of[9], (D, D), (D // 8) ** -0.5, 0.875, ((0, 4),))
    output_bias = normal_values(key_of[10], (D,), 0.2, 1.25, (), jnp.float32)
    norm2_gain = jnp.clip(1.0 + 0.1 * jax.random.normal(key_of[11], (D,), jnp.float32), 0.5, 1.5)
    norm2_bias = normal_values(key_of[12], (D,), 0.2, 1.25, (), jnp.float32)
    router_weight = normal_values(key_of[13], (D, E), (2 * D) ** -0.5, 0.21875)
    up_weight = normal_values(key_of[14], (E, D, FF), D ** -0.5, 0.3125, ((2, 4),))
    up_bias = normal_values(key_of[15], (E, FF), 0.2, 1.25, ((1, 4),), jnp.float32)
    down_weight = normal_values(key_of[16], (E, FF, D), (FF // 64) ** -0.5, 1.25, ((1, 4),))
    down_bias = normal_values(key_of[17], (E, D), 1.0, 6.0, (), jnp.float32)
    cotangent = normal_values(key_of[18], (IMAGES, LEN, D), 1.0, 6.0, ((0, 8),))
    return dict(patches=patches, image_count=image_count, routes=routes, slot_index=slot_index, norm1_gain=norm1_gain, norm1_bias=norm1_bias, input_proj=input_proj, query_value_bias=query_value_bias, position_bias=position_bias, output_proj=output_proj, output_bias=output_bias, norm2_gain=norm2_gain, norm2_bias=norm2_bias, router_weight=router_weight, up_weight=up_weight, up_bias=up_bias, down_weight=down_weight, down_bias=down_bias, cotangent=cotangent)


@jax.custom_vjp
def low(v):
    return lax.optimization_barrier(v.astype(jnp.bfloat16)).astype(jnp.float32)

@jax.custom_vjp
def low_back(v):
    return v

def low_keep(v):
    return (low(v), None)

def low_pass(kept, grad):
    return (grad,)

def back_keep(v):
    return (v, None)

def back_low(kept, grad):
    return (low(grad),)
low.defvjp(low_keep, low_pass)
low_back.defvjp(back_keep, back_low)

def layer_norm(values):
    center = values - lax.optimization_barrier(jnp.mean(values, axis=-1, keepdims=True))
    inverse = lax.rsqrt(lax.optimization_barrier(jnp.mean(center * center, axis=-1, keepdims=True)) + 1e-05)
    return center * inverse

def to_windows(values):
    images = values.shape[0]
    width = values.shape[-1]
    grid = values.reshape(images, SIDE, SIDE, width)
    grid = jnp.roll(grid, (-SHIFT, -SHIFT), (1, 2))
    grid = grid.reshape(images, SIDE // WIN, WIN, SIDE // WIN, WIN, width).transpose(0, 1, 3, 2, 4, 5)
    return grid.reshape(images * (SIDE // WIN) ** 2, WIN * WIN, width)

def from_windows(values, images):
    width = values.shape[-1]
    grid = values.reshape(images, SIDE // WIN, SIDE // WIN, WIN, WIN, width).transpose(0, 1, 3, 2, 4, 5)
    grid = jnp.roll(grid.reshape(images, SIDE, SIDE, width), (SHIFT, SHIFT), (1, 2))
    return grid.reshape(images, SIDE * SIDE, width)

def band_of(values):
    return (values >= SIDE - WIN).astype(jnp.int32) + (values >= SIDE - SHIFT).astype(jnp.int32)

def region_labels():
    cells = jnp.arange(SIDE * SIDE, dtype=jnp.int32)
    labels = 3 * band_of(cells // SIDE) + band_of(cells % SIDE)
    grid = jnp.roll(labels.reshape(SIDE, SIDE), (SHIFT, SHIFT), (0, 1))
    return grid.reshape(SIDE * SIDE).astype(jnp.int32)

def relative_index():
    cells = jnp.arange(WIN * WIN, dtype=jnp.int32)
    rows = cells // WIN
    cols = cells % WIN
    return ((rows[:, None] - rows[None, :] + WIN - 1) * (2 * WIN - 1) + (cols[:, None] - cols[None, :] + WIN - 1)).astype(jnp.int32)

def shard_forward(params, shard, region_mask, relative):
    norm1_gain, norm1_bias, input_proj, query_value_bias, position_bias, output_proj, output_bias, norm2_gain, norm2_bias, router_weight, up_weight, up_bias, down_weight, down_bias = params
    block, count, route_rows, slot_rows = shard
    highest = lax.Precision.HIGHEST
    tokens = IMG * LEN
    inputs = block.reshape(tokens, D)
    keep_rows = jnp.repeat((jnp.arange(IMG, dtype=jnp.int32) < count).astype(jnp.float32), LEN)[:, None]
    low1 = low(layer_norm(inputs) * norm1_gain + norm1_bias)
    windows = to_windows(low1.reshape(IMG, LEN, D))
    count_windows = windows.shape[0]
    packed = jnp.einsum('bnd,dce->bnce', windows, input_proj, precision=highest)
    query = low_back(low(packed[:, :, 0] + query_value_bias[0])).reshape(count_windows, WIN * WIN, HEADS, HD)
    key_low = low_back(low(packed[:, :, 1])).reshape(count_windows, WIN * WIN, HEADS, HD)
    value_low = low_back(low(packed[:, :, 2] + query_value_bias[1])).reshape(count_windows, WIN * WIN, HEADS, HD)
    table_bias = position_bias[relative].transpose(2, 0, 1)
    scores = HD ** (-0.5) * jnp.einsum('bihe,bjhe->bhij', query, key_low, precision=highest)
    scores = low_back(scores + table_bias[None] + region_mask[:, None])
    attn_low = low(jax.nn.softmax(scores, axis=-1))
    mixed = jnp.einsum('bhij,bjhe->bihe', attn_low, value_low, precision=highest).reshape(count_windows, WIN * WIN, D)
    mixed = low_back(low(mixed))
    mixed_tokens = from_windows(mixed, IMG).reshape(tokens, D)
    attn_out = low_back(jnp.dot(mixed_tokens, output_proj, precision=highest) + output_bias)
    hidden1 = inputs + attn_out
    low2 = low(layer_norm(hidden1) * norm2_gain + norm2_bias)
    logits = low_back(jnp.dot(low2, router_weight, precision=highest))
    probs = jax.nn.softmax(logits, axis=-1)
    gate = jnp.take_along_axis(probs, route_rows[:, None], axis=1)[:, 0]
    kept = slot_rows >= 0
    target = jnp.where(kept, route_rows * CAP + slot_rows, E * CAP).astype(jnp.int32)
    buffer = jnp.zeros((E * CAP, D), jnp.float32).at[target].set(low2, mode='drop').reshape(E, CAP, D)
    hidden_pre = low_back(jnp.einsum('ecd,edf->ecf', buffer, up_weight, precision=highest) + up_bias[:, None])
    activated = low(jax.nn.gelu(hidden_pre))
    raw = jnp.einsum('ecf,efd->ecd', activated, down_weight, precision=highest).reshape(E * CAP, D)
    gathered = jnp.take(raw, target, axis=0, mode='fill', fill_value=0.0)
    token_out = low_back(gathered + down_bias[route_rows])
    moe = jnp.where(kept[:, None], gate[:, None] * token_out, 0.0)
    return ((hidden1 + moe) * keep_rows).reshape(IMG, LEN, D)

def forward(inputs, params, image_count, routes, slot_index):
    labels = to_windows(region_labels().reshape(1, LEN, 1))[:, :, 0]
    mask_one = jnp.where(labels[:, :, None] == labels[:, None, :], 0.0, -100.0).astype(jnp.float32)
    region_mask = jnp.tile(mask_one, (IMG, 1, 1))
    relative = relative_index()

    def one_shard(shard):
        return shard_forward(params, shard, region_mask, relative)
    shards = (inputs.reshape(N_DP, IMG, LEN, D), image_count, routes.reshape(N_DP, IMG * LEN), slot_index.reshape(N_DP, IMG * LEN))
    result = lax.map(jax.checkpoint(one_shard), shards)
    return result.reshape(IMAGES, LEN, D)

def reference(patches, image_count, routes, slot_index, norm1_gain, norm1_bias, input_proj, query_value_bias, position_bias, output_proj, output_bias, norm2_gain, norm2_bias, router_weight, up_weight, up_bias, down_weight, down_bias, cotangent):
    params = tuple((item.astype(jnp.float32) for item in (norm1_gain, norm1_bias, input_proj, query_value_bias, position_bias, output_proj, output_bias, norm2_gain, norm2_bias, router_weight, up_weight, up_bias, down_weight, down_bias)))
    inputs = patches.astype(jnp.float32)

    def whole(inputs, *weights):
        return forward(inputs, weights, image_count, routes, slot_index)
    result, backward = jax.vjp(whole, inputs, *params)
    grads = backward(cotangent.astype(jnp.float32))
    return (result.astype(jnp.bfloat16), grads[0], grads[1], grads[2], grads[3], grads[4], grads[5], grads[6], grads[7], grads[8], grads[9], grads[10], grads[11], grads[12], grads[13], grads[14])
```

```python
import functools

import jax
import jax.numpy as jnp
import numpy as np
from jax import lax
from jax.experimental import pallas as pl
from jax.experimental.pallas import tpu as pltpu
from jax.sharding import PartitionSpec as P

HD = 32
WIN = 7
SIDE = 14
SHIFT = 3
CAP = 512
CELLS = WIN * WIN
LEN = SIDE * SIDE
ROWS = 208
WROWS = 64
STEP = 64
EPS = 1e-05
SCALE = HD**-0.5
GROUP = 4
MIB = 1024 * 1024
F32 = jnp.float32
BF16 = jnp.bfloat16


def dot(a, b, dims=((1,), (0,))):
    return lax.dot_general(a, b, (dims, ((), ())), preferred_element_type=F32)


NT = ((1,), (1,))
TN = ((0,), (0,))


def layer_norm(values):
    center = values - jnp.mean(values, axis=-1, keepdims=True)
    inverse = lax.rsqrt(jnp.mean(center * center, axis=-1, keepdims=True) + EPS)
    return center * inverse, inverse


def norm_back(grad_hat, normed, inverse):
    return inverse * (
        grad_hat
        - jnp.mean(grad_hat, axis=-1, keepdims=True)
        - normed * jnp.mean(grad_hat * normed, axis=-1, keepdims=True)
    )


def window_tables():
    perm = np.zeros((4 * WROWS, ROWS), np.float32)
    label = np.zeros((4, CELLS), np.int32)
    for w in range(4):
        for a in range(WIN):
            for b in range(WIN):
                r, c = (w // 2) * WIN + a, (w % 2) * WIN + b
                perm[w * WROWS + a * WIN + b, ((r + SHIFT) % SIDE) * SIDE + (c + SHIFT) % SIDE] = 1
                band = lambda v: int(v >= SIDE - WIN) + int(v >= SIDE - SHIFT)
                label[w, a * WIN + b] = 3 * band(r) + band(c)
    mask = np.full((4, WROWS, WROWS), -1e30, np.float32)
    mask[:, :, :CELLS] = 0
    same = label[:, :, None] == label[:, None, :]
    mask[:, :CELLS, :CELLS] = np.where(same, 0.0, -100.0)
    mask = np.tile(mask, (1, 1, GROUP))
    cells = np.arange(CELLS)
    rows, cols = cells // WIN, cells % WIN
    rel = (rows[:, None] - rows[None, :] + WIN - 1) * (2 * WIN - 1) + (
        cols[:, None] - cols[None, :] + WIN - 1
    )
    relative = np.full((WROWS, WROWS), -1, np.int32)
    relative[:CELLS, :CELLS] = rel
    return perm, mask, relative


def lane_iota(rows, cols):
    return lax.broadcasted_iota(jnp.int32, (rows, cols), 1)


def row_iota(rows, cols):
    return lax.broadcasted_iota(jnp.int32, (rows, cols), 0)


def segment_reduce(values, op, fill):
    low = lane_iota(values.shape[0], 128) < 64
    parts = []
    for half in range(2):
        v = values[:, half * 128 : half * 128 + 128]
        a = op(jnp.where(low, v, fill), axis=-1, keepdims=True)
        b = op(jnp.where(low, fill, v), axis=-1, keepdims=True)
        parts.append(jnp.where(low, a, b))
    return jnp.concatenate(parts, axis=1)


def head_masks():
    lane = lane_iota(1, 128) // HD
    return [(lane == h).astype(F32) for h in range(GROUP)]


def spread(block, masks):
    return jnp.concatenate([block * m for m in masks], axis=0)


def unspread(wide, masks):
    total = wide[0:WROWS] * masks[0]
    for h in range(1, GROUP):
        total = total + wide[h * WROWS : (h + 1) * WROWS] * masks[h]
    return total


def pad_rows(scratch, block):
    scratch[LEN - 4 :, :] = jnp.zeros((ROWS - LEN + 4, scratch.shape[1]), scratch.dtype)
    scratch[0:LEN, :] = block
    return scratch[...]


def attention_kernel(
    place, patches, col, wa, wb, wc, wd, table, mask, perm, perm_t, vecs, router,
    win_o, qkv_o, att_o, mix_o, h1_o, aug_o, w_o, wot_o,
    shards, pad, mixw,
):
    tensor = place[1]

    @pl.when(pl.program_id(0) == 0)
    def _():
        for m, ref in enumerate((wa, wb, wc, wd)):
            shards[m ^ tensor] = ref[...]
        for c in range(4):
            joined = jnp.concatenate(
                [shards[k][:, c * 96 : (c + 1) * 96] for k in range(4)], axis=1
            ).astype(BF16)
            if c < 3:
                w_o[:, c * 384 : (c + 1) * 384] = joined
            else:
                wot_o[...] = joined

    x = pad_rows(pad, patches[0].astype(F32))
    xhat, _ = layer_norm(x)
    low1 = (xhat * vecs[0:1] + vecs[1:2]).astype(BF16)
    win = dot(perm[...], low1).astype(BF16)
    win_o[0] = win
    packed = dot(win, w_o[...])
    qkv_o[0, :, 0:384] = (packed[:, 0:384] + vecs[5:6]).astype(BF16)
    qkv_o[0, :, 384:768] = packed[:, 384:768].astype(BF16)
    qkv_o[0, :, 768:1152] = (packed[:, 768:1152] + vecs[6:7]).astype(BF16)
    masks = [m.astype(BF16) for m in head_masks()]
    for w in range(4):
        rows = slice(w * WROWS, (w + 1) * WROWS)
        for g in range(3):
            lanes = lambda c: slice(c * 384 + g * 128, c * 384 + g * 128 + 128)
            q4 = qkv_o[0, rows, lanes(0)]
            kbd = spread(qkv_o[0, rows, lanes(1)], masks)
            vbd = spread(qkv_o[0, rows, lanes(2)], masks)
            s = dot(q4, kbd, NT) * SCALE + table[g] + mask[w]
            e = jnp.exp(s - segment_reduce(s, jnp.max, -3e38))
            attn = e / segment_reduce(e, jnp.sum, 0.0)
            low = attn.astype(BF16)
            att_o[0, rows, g * 256 : (g + 1) * 256] = low
            mixw[rows, g * 128 : (g + 1) * 128] = dot(low, vbd).astype(BF16)
    mixt = dot(perm_t[...], mixw[...]).astype(BF16)
    mix_o[0] = mixt
    h1 = x + (dot(mixt, wot_o[...], NT) + vecs[2:3])
    h1_o[0] = h1
    xhat2, _ = layer_norm(h1)
    low2 = (xhat2 * vecs[3:4] + vecs[4:5]).astype(BF16)
    aug_o[0, :, 0:384] = low2.astype(F32)
    logits = dot(low2, router[...])
    lane = lane_iota(ROWS, 128)
    real = (lane >= 8) & (lane < 16)
    logits = jnp.where(real, logits, -1e30)
    top = jnp.max(logits, axis=-1, keepdims=True)
    ex = jnp.where(real, jnp.exp(logits - top), 0.0)
    probs = ex / jnp.sum(ex, axis=-1, keepdims=True)
    route = col[0][:, 0:1]
    gate = jnp.sum(jnp.where(lane - 8 == route, probs, 0.0), axis=-1, keepdims=True)
    hi = gate.astype(BF16).astype(F32)
    mid = (gate - hi).astype(BF16).astype(F32)
    lo = (gate - hi - mid).astype(BF16).astype(F32)
    tail = jnp.where(lane == 0, hi, jnp.where(lane == 1, mid, jnp.where(lane == 2, lo, probs)))
    aug_o[0, :, 384:512] = tail


def attention_forward(place, patches, col, ws, table, mask, perm, perm_t, vecs, router, images):
    whole = lambda *shape: pl.BlockSpec(shape, lambda i, p: (0,) * len(shape))
    own = lambda *shape: pl.BlockSpec((1,) + shape, lambda i, p: (images * p[0] + i,) + (0,) * len(shape))
    out = lambda *shape: pl.BlockSpec((1,) + shape, lambda i, p: (i,) + (0,) * len(shape))
    sds = lambda *shape, dtype=BF16: jax.ShapeDtypeStruct(shape, dtype)
    return pl.pallas_call(
        attention_kernel,
        out_shape=(
            sds(images, 256, 384),
            sds(images, 256, 1152),
            sds(images, 256, 768),
            sds(images, ROWS, 384),
            sds(images, ROWS, 384, dtype=F32),
            sds(images, ROWS, 512, dtype=F32),
            sds(384, 1152),
            sds(384, 384),
        ),
        grid_spec=pltpu.PrefetchScalarGridSpec(
            num_scalar_prefetch=1,
            grid=(images,),
            in_specs=[own(LEN, 384), own(ROWS, 8)]
            + [whole(384, 384)] * 4
            + [whole(3, 64, 256), whole(4, 64, 256), whole(256, ROWS), whole(ROWS, 256), whole(8, 384), whole(384, 128)],
            out_specs=(
                out(256, 384), out(256, 1152), out(256, 768), out(ROWS, 384),
                out(ROWS, 384), out(ROWS, 512), whole(384, 1152), whole(384, 384),
            ),
            scratch_shapes=[
                pltpu.VMEM((4, 384, 384), F32),
                pltpu.VMEM((ROWS, 384), F32),
                pltpu.VMEM((256, 384), BF16),
            ],
        ),
        compiler_params=pltpu.CompilerParams(vmem_limit_bytes=40 * MIB),
        cost_estimate=pl.CostEstimate(flops=8 * 10**9, bytes_accessed=30 * 10**6, transcendentals=0),
        name="attention_forward",
    )(place, patches, col, *ws, table, mask, perm, perm_t, vecs, router)


def slot_passes(starts, rounds, image, experts, body):
    def one(r, _):
        first = [starts[image, e] + r * STEP for e in range(experts)]
        base = [jnp.minimum(f, CAP - STEP) for f in first]
        body(base, first)
        return 0

    lax.fori_loop(0, rounds[image], one, 0)


def dispatch_kernel(split, experts, place, starts, rounds, key, first_ref, second_ref, out, acc):
    i = pl.program_id(0)
    width = out.shape[2]

    @pl.when(i == 0)
    def _():
        acc[...] = jnp.zeros_like(acc)

    if split:
        tile = jnp.where(i < pl.num_programs(0) // 2, first_ref[0], second_ref[0]).astype(BF16)
    else:
        tile = first_ref[0]
    tokens = tile.shape[0]
    keys = key[0][0:1, 0:tokens]

    def body(base, first):
        blocks = []
        for e in range(experts):
            code = row_iota(STEP, tokens) + (e * CAP + base[e])
            hit = (code == keys) & (code >= e * CAP + first[e])
            blocks.append(jnp.where(hit, 1.0, 0.0).astype(BF16))
        moved = dot(jnp.concatenate(blocks, axis=0), tile)
        for e in range(experts):
            at = pl.ds(pl.multiple_of(base[e], 16), STEP)
            acc[e, at, :] = acc[e, at, :] + moved[e * STEP : (e + 1) * STEP]

    slot_passes(starts, rounds, i, experts, body)

    @pl.when(i == pl.num_programs(0) - 1)
    def _():
        for e in range(experts):
            out[e] = acc[e].astype(BF16)


def dispatch(place, starts, rounds, key, first, second, experts):
    split = second is not None
    images = starts.shape[0]
    half = images // 2
    tokens, width = first.shape[1], first.shape[2]
    if split:
        data = [
            pl.BlockSpec((1, tokens, width), lambda i, p, s, r: (jnp.minimum(i, half - 1), 0, 0)),
            pl.BlockSpec((1, tokens, width), lambda i, p, s, r: (jnp.maximum(i - half, 0), 0, 0)),
        ]
    else:
        second = first
        data = [
            pl.BlockSpec((1, tokens, width), lambda i, p, s, r: ((i + half * p[0]) % images, 0, 0)),
            pl.BlockSpec((1, 16, 128), lambda i, p, s, r: (0, 0, 0)),
        ]
    return pl.pallas_call(
        functools.partial(dispatch_kernel, split, experts),
        out_shape=jax.ShapeDtypeStruct((experts, CAP, width), BF16),
        grid_spec=pltpu.PrefetchScalarGridSpec(
            num_scalar_prefetch=3,
            grid=(images,),
            in_specs=[pl.BlockSpec((1, 8, ROWS), lambda i, p, s, r: (i, 0, 0))] + data,
            out_specs=pl.BlockSpec((experts, CAP, width), lambda i, p, s, r: (0, 0, 0)),
            scratch_shapes=[pltpu.VMEM((experts, CAP, width), F32)],
        ),
        compiler_params=pltpu.CompilerParams(vmem_limit_bytes=48 * MIB),
        cost_estimate=pl.CostEstimate(flops=8 * 10**9, bytes_accessed=15 * 10**6, transcendentals=0),
        name="dispatch_low2" if split else "dispatch_cotangent",
    )(place, starts, rounds, key, first, second)


def expert_kernel(place, buf, gbuf, up, down, up_b, down_b, gu_o, gd_o, rg_o, gdb_o):
    block = buf[0]
    x = block[:, 0:384]
    tail = block[:, 384:512].astype(F32)
    gate = tail[:, 0:1] + tail[:, 1:2] + tail[:, 2:3]
    g = (gate * gbuf[0].astype(F32)).astype(BF16)
    gdb_o[...] = jnp.broadcast_to(jnp.sum(g.astype(F32), axis=0, keepdims=True), (8, 384))
    w_up, w_down = up[0], down[0]
    hp = dot(x, w_up) + up_b[0][0:1]
    c0 = np.float32(np.sqrt(2 / np.pi))
    th = jnp.tanh(c0 * (hp + 0.044715 * (hp * hp * hp)))
    act = (hp * (0.5 * (1.0 + th))).astype(BF16)
    slope = 0.5 * (1.0 + th) + (0.5 * hp) * (1.0 - th * th) * (c0 * (1.0 + (3 * 0.044715) * (hp * hp)))
    lead = jnp.where(place[1] == 0, 1.0, 0.0)
    rg_o[:, 0:384] = (dot(act, w_down) + lead * down_b[0][0:1]).astype(BF16)
    gd_o[...] = dot(act, g, TN)
    gp = (dot(g, w_down, NT) * slope).astype(BF16)
    gu_o[0:384] = dot(x, gp, TN)
    gu_o[384:392] = jnp.broadcast_to(jnp.sum(gp.astype(F32), axis=0, keepdims=True), (8, 384))
    rg_o[:, 384:768] = dot(gp, w_up, NT).astype(BF16)


def expert_pass(place, buf, gbuf, up, down, up_b, down_b):
    at = lambda *shape: pl.BlockSpec((1,) + shape, lambda i, p: (p[2],) + (0,) * len(shape))
    whole = lambda *shape: pl.BlockSpec(shape, lambda i, p: (0,) * len(shape))
    sds = jax.ShapeDtypeStruct
    return pl.pallas_call(
        expert_kernel,
        out_shape=(sds((392, 384), F32), sds((384, 384), F32), sds((CAP, 768), BF16), sds((8, 384), F32)),
        grid_spec=pltpu.PrefetchScalarGridSpec(
            num_scalar_prefetch=1,
            grid=(1,),
            in_specs=[at(CAP, 512), at(CAP, 384), at(384, 384), at(384, 384), at(1, 384), at(1, 384)],
            out_specs=(whole(392, 384), whole(384, 384), whole(CAP, 768), whole(8, 384)),
        ),
        compiler_params=pltpu.CompilerParams(vmem_limit_bytes=32 * MIB),
        cost_estimate=pl.CostEstimate(flops=9 * 10**8, bytes_accessed=4 * 10**6, transcendentals=0),
        name="expert_pass",
    )(place, buf, gbuf, up, down, up_b, down_b)


def combine_kernel(
    experts, offset, place, order, starts, rounds, col, cot,
    r0, r1, r2, r3, r4, r5, r6, r7, gl_o, tok_o, windows,
):
    i = pl.program_id(0) + offset
    refs = (r0, r1, r2, r3, r4, r5, r6, r7)
    keys = col[0][:, 1:2]
    gl_o[0] = jnp.zeros((ROWS, 384), F32)
    tok_o[0] = jnp.zeros((ROWS, 384), F32)

    def one(r, _):
        lane = lane_iota(1, experts * STEP)
        code = jnp.zeros((1, experts * STEP), jnp.int32)
        for s in range(experts):
            e = order[s]
            first = starts[i, e] + r * STEP
            base = jnp.minimum(first, CAP - STEP)
            windows[s * STEP : (s + 1) * STEP, :] = refs[s][pl.ds(pl.multiple_of(base, 16), STEP), :]
            slot = lane - s * STEP + base
            here = (lane >= s * STEP) & (lane < (s + 1) * STEP)
            code = jnp.where(here, jnp.where(slot >= first, e * CAP + slot, -2), code)
        hit = jnp.where(code == keys, 1.0, 0.0).astype(BF16)
        back = dot(hit, windows[...])
        tok_o[0] = tok_o[0] + back[:, 0:384]
        gl_o[0] = gl_o[0] + back[:, 384:768]
        return 0

    lax.fori_loop(0, rounds[i], one, 0)
    dots = jnp.sum(tok_o[0, 0:LEN, :] * cot[0].astype(F32), axis=-1, keepdims=True)
    eye = row_iota(LEN, ROWS) == lane_iota(LEN, ROWS)
    gl_o[0, 200:201, 0:ROWS] = jnp.sum(jnp.where(eye, dots, 0.0), axis=0, keepdims=True)


def combine(place, order, starts, rounds, col, cot, results, offset, count):
    experts = len(results)
    images = starts.shape[0]
    half = images // 2
    at = lambda *shape: pl.BlockSpec(
        (1,) + shape, lambda i, p, o, s, r: ((i + offset + half * p[0]) % images,) + (0,) * len(shape)
    )
    out = pl.BlockSpec((1, ROWS, 384), lambda i, p, o, s, r: (i, 0, 0))
    return pl.pallas_call(
        functools.partial(combine_kernel, experts, offset),
        out_shape=(jax.ShapeDtypeStruct((count, ROWS, 384), F32),) * 2,
        grid_spec=pltpu.PrefetchScalarGridSpec(
            num_scalar_prefetch=4,
            grid=(count,),
            in_specs=[at(ROWS, 8), at(LEN, 384)]
            + [pl.BlockSpec((CAP, 768), lambda i, p, o, s, r: (0, 0))] * experts,
            out_specs=(out, out),
            scratch_shapes=[pltpu.VMEM((experts * STEP, 768), BF16)],
        ),
        compiler_params=pltpu.CompilerParams(vmem_limit_bytes=40 * MIB),
        cost_estimate=pl.CostEstimate(flops=2 * 10**9, bytes_accessed=20 * 10**6, transcendentals=0),
        name="combine",
    )(place, order, starts, rounds, col, cot, *results)


def backward_kernel(
    first, offset, place, keep, own, other, cot, col, h1, aug, mix, win, qkv, att, patches,
    w, wot, perm, perm_t, vecs, router,
    dw_i, dwo_i, dtb_i, dv_i, dr_i,
    gp_o, dw_o, dwo_o, dtb_o, dv_o, dr_o,
    pad, dqkv,
):
    i = pl.program_id(0)

    @pl.when(i == 0)
    def _():
        for src, dst in ((dw_i, dw_o), (dwo_i, dwo_o), (dtb_i, dtb_o), (dv_i, dv_o), (dr_i, dr_o)):
            dst[...] = jnp.zeros(dst.shape, F32) if first else src[...]

    total = own[0] + other[0]
    rows = row_iota(ROWS, 384)
    gl = jnp.where(rows < LEN, total, 0.0)
    eye = row_iota(ROWS, ROWS) == lane_iota(ROWS, ROWS)
    gg = jnp.sum(jnp.where(eye, total[200:201, 0:ROWS], 0.0), axis=-1, keepdims=True)
    grad = pad_rows(pad, cot[0].astype(F32)) * keep[offset + i]
    tail = aug[0, :, 384:512]
    lane = lane_iota(ROWS, 128)
    probs = jnp.where((lane >= 8) & (lane < 16), tail, 0.0)
    hot = jnp.where(lane - 8 == col[0][:, 0:1], 1.0, 0.0)
    gate = jnp.sum(probs * hot, axis=-1, keepdims=True)
    glog = (probs * (hot - gate) * gg).astype(BF16)
    low2 = aug[0, :, 0:384].astype(BF16)
    dr_o[...] += dot(low2, glog, TN)
    g2 = gl + dot(glog, router[...], NT)
    xhat2, inv2 = layer_norm(h1[0])
    add = lambda r, v: dv_o.__setitem__((slice(r, r + 1), slice(None)), dv_o[r : r + 1, :] + jnp.sum(v, axis=0, keepdims=True))
    add(3, g2 * xhat2)
    add(4, g2)
    gh1 = grad + norm_back(g2 * vecs[3:4], xhat2, inv2)
    gattn = gh1.astype(BF16)
    add(2, gattn.astype(F32))
    dwo_o[...] += dot(gattn, mix[0], TN)
    gmix = dot(gattn, wot[...]).astype(BF16)
    gmw = dot(perm[...], gmix).astype(BF16)
    masks = head_masks()
    low_masks = [m.astype(BF16) for m in masks]
    for wi in range(4):
        rs = slice(wi * WROWS, (wi + 1) * WROWS)
        for g in range(3):
            lanes = lambda c: slice(c * 384 + g * 128, c * 384 + g * 128 + 128)
            q4 = qkv[0, rs, lanes(0)]
            kbd = spread(qkv[0, rs, lanes(1)], low_masks)
            vbd = spread(qkv[0, rs, lanes(2)], low_masks)
            dm = gmw[rs, g * 128 : (g + 1) * 128]
            a_low = att[0, rs, g * 256 : (g + 1) * 256]
            a = a_low.astype(F32)
            da = dot(dm, vbd, NT)
            ds = (a * (da - segment_reduce(da * a, jnp.sum, 0.0))).astype(BF16)
            dtb_o[g] += ds.astype(F32)
            dqkv[rs, lanes(0)] = (SCALE * dot(ds, kbd)).astype(BF16)
            dqkv[rs, lanes(1)] = (SCALE * unspread(dot(ds, q4, TN), masks)).astype(BF16)
            dqkv[rs, lanes(2)] = unspread(dot(a_low, dm, TN), masks).astype(BF16)
    packed = dqkv[...]
    dw_o[...] += dot(win[0], packed, TN)
    add(5, packed[:, 0:384].astype(F32))
    add(6, packed[:, 768:1152].astype(F32))
    gl1w = dot(packed, w[...], NT)
    hi = gl1w.astype(BF16)
    lo = (gl1w - hi.astype(F32)).astype(BF16)
    gl1 = dot(perm_t[...], hi) + dot(perm_t[...], lo)
    xhat1, inv1 = layer_norm(pad_rows(pad, patches[0].astype(F32)))
    add(0, gl1 * xhat1)
    add(1, gl1)
    gp_o[0] = gh1 + norm_back(gl1 * vecs[0:1], xhat1, inv1)


def attention_backward(
    first, place, keep, own, other, cot, col, h1, aug, mix, win, qkv, att, patches,
    w, wot, perm, perm_t, vecs, router, acc, offset, count, images,
):
    whole = lambda *shape: pl.BlockSpec(shape, lambda i, p, k: (0,) * len(shape))
    here = lambda *shape: pl.BlockSpec((1,) + shape, lambda i, p, k: (i,) + (0,) * len(shape))
    mine = lambda *shape: pl.BlockSpec((1,) + shape, lambda i, p, k: (i + offset,) + (0,) * len(shape))
    glob = lambda *shape: pl.BlockSpec(
        (1,) + shape, lambda i, p, k: (images * p[0] + offset + i,) + (0,) * len(shape)
    )
    sds = jax.ShapeDtypeStruct
    accs = [whole(384, 1152), whole(384, 384), whole(3, 64, 256), whole(8, 384), whole(384, 128)]
    return pl.pallas_call(
        functools.partial(backward_kernel, first, offset),
        out_shape=(sds((count, ROWS, 384), F32),) + tuple(sds(a.shape, F32) for a in acc),
        grid_spec=pltpu.PrefetchScalarGridSpec(
            num_scalar_prefetch=2,
            grid=(count,),
            in_specs=[
                here(ROWS, 384), here(ROWS, 384), glob(LEN, 384), glob(ROWS, 8), mine(ROWS, 384), mine(ROWS, 512),
                mine(ROWS, 384), mine(256, 384), mine(256, 1152), mine(256, 768), glob(LEN, 384),
                whole(384, 1152), whole(384, 384), whole(256, ROWS), whole(ROWS, 256), whole(8, 384), whole(384, 128),
            ]
            + accs,
            out_specs=(here(ROWS, 384),) + tuple(accs),
            scratch_shapes=[pltpu.VMEM((ROWS, 384), F32), pltpu.VMEM((256, 1152), BF16)],
        ),
        input_output_aliases={19 + j: 1 + j for j in range(5)},
        compiler_params=pltpu.CompilerParams(vmem_limit_bytes=48 * MIB),
        cost_estimate=pl.CostEstimate(flops=4 * 10**9, bytes_accessed=15 * 10**6, transcendentals=0),
        name="attention_backward",
    )(
        place, keep, own, other, cot, col, h1, aug, mix, win, qkv, att, patches,
        w, wot, perm, perm_t, vecs, router, *acc,
    )


def add_kernel(a, b, o):
    o[...] = a[...] + b[...]


def add_arrays(a, b, blocks=4):
    rows = a.shape[0] // blocks
    spec = pl.BlockSpec((rows,) + a.shape[1:], lambda i: (i,) + (0,) * (a.ndim - 1))
    return pl.pallas_call(
        add_kernel,
        out_shape=jax.ShapeDtypeStruct(a.shape, a.dtype),
        grid=(blocks,),
        in_specs=[spec, spec],
        out_specs=spec,
        cost_estimate=pl.CostEstimate(flops=a.size, bytes_accessed=12 * a.size, transcendentals=0),
        name="ring_add",
    )(a, b)


def block_out_kernel(keep, h1, aug, own, other, col, o):
    tail = aug[0, :, 384:512]
    gate = tail[:, 0:1] + tail[:, 1:2] + tail[:, 2:3]
    kept = jnp.where(col[0][:, 1:2] >= 0, 1.0, 0.0)
    token_out = own[0] + other[0]
    value = keep[pl.program_id(0)] * (h1[0] + (kept * gate) * token_out)
    o[0] = value.astype(BF16).astype(F32)


def block_out_pass(place, keep, h1, aug, own, other, col, images):
    here = lambda *shape: pl.BlockSpec((1,) + shape, lambda i, p, k: (i,) + (0,) * len(shape))

    def body(p, k, *refs):
        block_out_kernel(k, *refs)

    return pl.pallas_call(
        body,
        out_shape=jax.ShapeDtypeStruct((images, ROWS, 384), F32),
        grid_spec=pltpu.PrefetchScalarGridSpec(
            num_scalar_prefetch=2,
            grid=(images,),
            in_specs=[
                here(ROWS, 384), here(ROWS, 512), here(ROWS, 384), here(ROWS, 384),
                pl.BlockSpec((1, ROWS, 8), lambda i, p, k: (images * p[0] + i, 0, 0)),
            ],
            out_specs=here(ROWS, 384),
        ),
        cost_estimate=pl.CostEstimate(flops=10**7, bytes_accessed=16 * 10**6, transcendentals=0),
        name="block_out",
    )(place, keep, h1, aug, own, other, col)


def join_pass(place, own, other, dtype):
    images = own.shape[0]

    def body(p, a, b, o):
        mine = pl.program_id(0) // images == p[0]

        @pl.when(mine)
        def _():
            o[0] = a[0, 0:LEN, :].astype(dtype)

        @pl.when(jnp.logical_not(mine))
        def _():
            o[0] = b[0, 0:LEN, :].astype(dtype)

    def index(flip):
        def at(i, p):
            me = p[0] if flip == 0 else 1 - p[0]
            return (jnp.clip(i - images * me, 0, images - 1), 0, 0)

        return at

    return pl.pallas_call(
        body,
        out_shape=jax.ShapeDtypeStruct((2 * images, LEN, 384), dtype),
        grid_spec=pltpu.PrefetchScalarGridSpec(
            num_scalar_prefetch=1,
            grid=(2 * images,),
            in_specs=[pl.BlockSpec((1, ROWS, 384), index(0)), pl.BlockSpec((1, ROWS, 384), index(1))],
            out_specs=pl.BlockSpec((1, LEN, 384), lambda i, p: (i, 0, 0)),
        ),
        cost_estimate=pl.CostEstimate(flops=10**6, bytes_accessed=10**7, transcendentals=0),
        name="join",
    )(place, own, other)


def swap_core(x):
    return lax.ppermute(x, "tensor", [(0, 1), (1, 0), (2, 3), (3, 2)])


def swap_chip(x):
    return lax.ppermute(x, "tensor", [(0, 2), (2, 0), (1, 3), (3, 1)])


def on_device(
    n_dp, patches, image_count, routes, slot_index, norm1_gain, norm1_bias, input_proj, query_value_bias,
    position_bias, output_proj, output_bias, norm2_gain, norm2_bias, router_weight, up_weight, up_bias,
    down_weight, down_bias, cotangent,
):
    images, length, width = patches.shape
    half = images // 2
    experts = up_weight.shape[0]
    tensor = lax.axis_index("tensor")
    core = tensor % 2
    perm_np, mask_np, relative_np = window_tables()
    perm = jnp.asarray(perm_np, BF16)
    perm_t = jnp.asarray(perm_np.T, BF16)
    mask = jnp.asarray(mask_np)

    small = jnp.zeros((8, 384), F32)
    small = small.at[0:3, 0:169].set(position_bias.T)
    small = small.at[3, 0:96].set(query_value_bias[0]).at[3, 96:192].set(query_value_bias[1])
    proj = jnp.concatenate(
        [input_proj.reshape(width, 288).astype(F32), output_proj.T.astype(F32)], axis=1
    )
    small_x = swap_chip(small)
    proj_x = swap_chip(proj)
    small_c = swap_core(small)
    proj_c = swap_core(proj)
    small_d = swap_core(small_x)
    proj_d = swap_core(proj_x)
    smalls = jnp.stack([small, small_c, small_x, small_d])
    swap1 = jnp.where(core == 1, smalls[jnp.array([1, 0, 3, 2])], smalls)
    smalls = jnp.where(tensor >= 2, swap1[jnp.array([2, 3, 0, 1])], swap1)
    heads_table = smalls[:, 0:3, 0:169].reshape(12, 169)
    hot = (jnp.arange(169)[:, None] == jnp.asarray(relative_np.reshape(1, -1))).astype(F32)
    table = jnp.dot(heads_table, hot, precision=lax.Precision.HIGHEST)
    table = table.reshape(3, 4, 64, 64).transpose(0, 2, 1, 3).reshape(3, 64, 256)
    vecs = jnp.concatenate(
        [
            norm1_gain[None], norm1_bias[None], output_bias[None], norm2_gain[None], norm2_bias[None],
            smalls[:, 3, 0:96].reshape(1, 384), smalls[:, 3, 96:192].reshape(1, 384), jnp.zeros((1, 384), F32),
        ]
    )
    router = jnp.zeros((384, 128), BF16).at[:, 8:16].set(router_weight)

    key = jnp.where(slot_index >= 0, routes * CAP + slot_index, -1)
    key = jnp.pad(key, ((0, 0), (0, ROWS - length)), constant_values=-1)
    route_pad = jnp.pad(routes, ((0, 0), (0, ROWS - length)))
    col = jnp.pad(jnp.stack([route_pad, key], axis=-1), ((0, 0), (0, 0), (0, 6)))
    rolled = jnp.where(core == 1, jnp.roll(key, half, axis=0), key)
    row = jnp.broadcast_to(rolled[:, None, :], (images, 8, ROWS))
    mine = (rolled[:, None, :] >= 0) & (rolled[:, None, :] // CAP == jnp.arange(experts)[None, :, None])
    slot = rolled[:, None, :] % CAP
    lowest = jnp.min(jnp.where(mine, slot, CAP), axis=2)
    highest = jnp.max(jnp.where(mine, slot + 1, 0), axis=2)
    starts = jnp.minimum(lowest // 16 * 16, CAP - STEP).astype(jnp.int32)
    rounds = jnp.max((highest - starts + STEP - 1) // STEP, axis=1).astype(jnp.int32)
    keep = (jnp.arange(images) < image_count[0]).astype(F32)
    keep_own = jnp.where(core == 1, keep[half:], keep[:half])

    ring = n_dp == experts
    if ring:
        cycle = [0, 2, 4, 6, 7, 5, 3, 1]
        where = {d: i for i, d in enumerate(cycle)}
        pairs = []
        for d in range(n_dp):
            for t in range(4):
                to = cycle[(where[d] + (1 if t % 2 == 0 else -1)) % n_dp]
                pairs.append((d * 4 + t, to * 4 + t))
        position = jnp.array([where[d] for d in range(n_dp)], jnp.int32)[lax.axis_index("dp")]
        rank = jnp.where(core == 0, position, (n_dp - position) % n_dp)
        onward = lambda v: lax.ppermute(v, ("dp", "tensor"), pairs)
    else:
        rank = jnp.int32(0)
    order = ((rank - jnp.arange(experts)) % experts).astype(jnp.int32)
    place = jnp.stack([core, tensor]).astype(jnp.int32)

    gbuf = dispatch(place, starts, rounds, row, cotangent, None, experts)
    win, qkv, att, mix, h1, aug, w, wot = attention_forward(
        place, patches, col, (proj, proj_c, proj_x, proj_d), table, mask, perm, perm_t, vecs, router, half
    )
    aug_c = swap_core(aug)
    buf = dispatch(place, starts, rounds, row, aug, aug_c, experts)

    results, ups, downs, down_sums = [], [], [], []
    up_b = up_bias.reshape(experts, 1, 384)
    down_b = down_bias.reshape(experts, 1, 384)
    acc_up = acc_down = None
    for s in range(experts):
        spot = jnp.stack([core, tensor, order[s]]).astype(jnp.int32)
        gu, gd, rg, gdb = expert_pass(spot, buf, gbuf, up_weight, down_weight, up_b, down_b)
        results.append(rg)
        down_sums.append(gdb[0:1])
        ups.append(gu)
        downs.append(gd)
    grad_up = jnp.zeros((experts, 384, 384), F32)
    grad_down = jnp.zeros((experts, 384, 384), F32)
    grad_up_bias = jnp.zeros((experts, 384), F32)
    if ring:
        acc_up, acc_down = ups[0], downs[0]
        for s in range(experts - 1):
            acc_up = add_arrays(onward(acc_up), ups[s + 1], 7)
            acc_down = add_arrays(onward(acc_down), downs[s + 1], 6)
        for s in range(experts):
            at = (rank + 1 - s) % experts
            grad_up = lax.dynamic_update_slice(grad_up, acc_up[None, 0:384], (at, 0, 0))
            grad_up_bias = lax.dynamic_update_slice(grad_up_bias, acc_up[384:385], (at, 0))
            grad_down = lax.dynamic_update_slice(grad_down, acc_down[None], (at, 0, 0))
            if s < experts - 1:
                acc_up, acc_down = onward(acc_up), onward(acc_down)
    else:
        all_up = lax.psum(jnp.stack(ups), "dp")
        all_down = lax.psum(jnp.stack(downs), "dp")
        grad_up, grad_up_bias, grad_down = all_up[:, 0:384], all_up[:, 384], all_down
        grad_up = jnp.take(grad_up, order, axis=0)
        grad_up_bias = jnp.take(grad_up_bias, order, axis=0)
        grad_down = jnp.take(grad_down, order, axis=0)
    grad_down_bias = jnp.take(jnp.concatenate(down_sums), order, axis=0)

    gl_far, tok_far = combine(place, order, starts, rounds, col, cotangent, results, half, half)
    gl_got = swap_core(gl_far)
    tok_got = swap_core(tok_far)
    gl_own, tok_own = combine(place, order, starts, rounds, col, cotangent, results, 0, half)
    chunk = 2
    acc = (
        jnp.zeros((384, 1152), F32), jnp.zeros((384, 384), F32), jnp.zeros((3, 64, 256), F32),
        jnp.zeros((8, 384), F32), jnp.zeros((384, 128), F32),
    )
    grads = []
    for c in range(0, half, chunk):
        mine_sum = add_arrays(gl_own[c : c + chunk], gl_got[c : c + chunk], 2)
        their_sum = swap_chip(mine_sum)
        gp, *acc = attention_backward(
            c == 0, place, keep_own, mine_sum, their_sum, cotangent, col, h1, aug, mix, win, qkv, att, patches,
            w, wot, perm, perm_t, vecs, router, acc, c, chunk, half,
        )
        grads.append(gp)
    tok_mine = add_arrays(tok_own, tok_got, half)
    tok_their = swap_chip(tok_mine)
    out_own = block_out_pass(place, keep_own, h1, aug, tok_mine, tok_their, col, half)
    block_out = join_pass(place, out_own, swap_core(out_own), BF16)
    gp_own = jnp.concatenate(grads, axis=0)
    grad_patches = join_pass(place, gp_own, swap_core(gp_own), F32)

    dw, dwo, dtb, dvec, drouter = acc
    joined = jnp.concatenate([dw, dwo], axis=1).reshape(384, 4, 4, 96)
    hot_t = jnp.dot(
        dtb.reshape(3, 64, 4, 64).transpose(0, 2, 1, 3).reshape(12, 4096), hot.T, precision=lax.Precision.HIGHEST
    )

    def share(t):
        main = lax.dynamic_slice(joined, (0, 0, t, 0), (384, 4, 1, 96)).reshape(384, 384)
        table_part = jnp.pad(lax.dynamic_slice(hot_t, (3 * t, 0), (3, 169)), ((0, 0), (0, 384 - 169)))
        biases = lax.dynamic_slice(dvec[5:7], (0, 96 * t), (2, 96)).reshape(1, 192)
        return jnp.concatenate([main, table_part, jnp.pad(biases, ((0, 0), (0, 192))), dvec[0:5], drouter[:, 8:16].T])

    mine_share = share(tensor) + swap_core(share(tensor ^ 1))
    total = lax.psum(jnp.concatenate([mine_share, grad_down_bias]), "dp")
    main = total[0:384].reshape(384, 4, 96)
    return (
        block_out,
        grad_patches,
        total[388],
        total[389],
        main[:, 0:3],
        total[387, 0:192].reshape(2, 96),
        total[384:387, 0:169].T,
        main[:, 3].T,
        total[390],
        total[391],
        total[392],
        total[393:401].T,
        grad_up,
        grad_up_bias,
        grad_down,
        total[401:409],
    )


def solution(mesh):
    in_specs = (
        P("dp", None, None), P("dp"), P("dp", None), P("dp", None), P(), P(), P(None, None, "tensor"),
        P(None, "tensor"), P(None, "tensor"), P("tensor", None), P(), P(), P(), P(), P(None, None, "tensor"),
        P(None, "tensor"), P(None, "tensor", None), P(), P("dp", None, None),
    )
    out_specs = (
        P("dp", None, None), P("dp", None, None), P(), P(), P(None, None, "tensor"), P(None, "tensor"),
        P(None, "tensor"), P("tensor", None), P(), P(), P(), P(), P(None, None, "tensor"), P(None, "tensor"),
        P(None, "tensor", None), P(),
    )
    return jax.shard_map(
        functools.partial(on_device, mesh.shape["dp"]),
        mesh=mesh, in_specs=in_specs, out_specs=out_specs, check_vma=False,
    )
```

```python
import functools

import jax
import jax.numpy as jnp
import numpy as np
from jax import lax
from jax.experimental import pallas as pl
from jax.experimental.pallas import tpu as pltpu
from jax.sharding import PartitionSpec as P

HD = 32
WIN = 7
SIDE = 14
SHIFT = 3
CAP = 512
CELLS = WIN * WIN
LEN = SIDE * SIDE
ROWS = 208
WROWS = 64
OUT_STEP = 64
BACK_STEP = 64
REL = (2 * WIN - 1) ** 2
EPS = 1e-05
SCALE = HD**-0.5
GROUP = 4
MIB = 1024 * 1024
COSTS = dict(
    plan=1, bias_tables=1.5, offset_sums=2, attention_forward=24, dispatch_cotangent=9, dispatch_low2=8, expert_pass=2.4,
    combine_far=4.4, combine_own=6.4, attention_backward=8.5, add=0.1, hand_on=0.1, block_out=4, join=4.8, share=1,
    halve=0.5, double=0.5, gather=5,
)
F32 = jnp.float32
BF16 = jnp.bfloat16
NN = ((1,), (0,))
NT = ((1,), (1,))
TN = ((0,), (0,))


def dot(a, b, dims=NN):
    return lax.dot_general(a, b, (dims, ((), ())), preferred_element_type=F32)


def layer_norm(values):
    center = values - jnp.mean(values, axis=-1, keepdims=True)
    inverse = lax.rsqrt(jnp.mean(center * center, axis=-1, keepdims=True) + EPS)
    return center * inverse, inverse


def norm_back(grad_hat, normed, inverse):
    return inverse * (
        grad_hat
        - jnp.mean(grad_hat, axis=-1, keepdims=True)
        - normed * jnp.mean(grad_hat * normed, axis=-1, keepdims=True)
    )


def window_tables():
    perm = np.zeros((4 * WROWS, ROWS), np.float32)
    label = np.zeros((4, CELLS), np.int32)
    band = lambda v: int(v >= SIDE - WIN) + int(v >= SIDE - SHIFT)
    for w in range(4):
        for a in range(WIN):
            for b in range(WIN):
                r, c = (w // 2) * WIN + a, (w % 2) * WIN + b
                perm[w * WROWS + a * WIN + b, ((r + SHIFT) % SIDE) * SIDE + (c + SHIFT) % SIDE] = 1
                label[w, a * WIN + b] = 3 * band(r) + band(c)
    mask = np.full((4, WROWS, WROWS), -1e30, np.float32)
    mask[:, :CELLS, :] = 0
    same = label[:, :, None] == label[:, None, :]
    mask[:, :CELLS, :CELLS] = np.where(same, 0.0, -100.0)
    cells = np.arange(CELLS)
    rows, cols = cells // WIN, cells % WIN
    rel = (rows[None, :] - rows[:, None] + WIN - 1) * (2 * WIN - 1) + (cols[None, :] - cols[:, None] + WIN - 1)
    relative = np.full((WROWS, WROWS), -1, np.int32)
    relative[:CELLS, :CELLS] = rel
    return perm, np.tile(mask, (1, 1, GROUP)), relative


def lane_iota(rows, cols):
    return lax.broadcasted_iota(jnp.int32, (rows, cols), 1)


def row_iota(rows, cols):
    return lax.broadcasted_iota(jnp.int32, (rows, cols), 0)


def head_masks():
    lane = lane_iota(1, 128) // HD
    return [(lane == h).astype(F32).astype(BF16) for h in range(GROUP)]


def spread(block, masks):
    return jnp.concatenate([block * m for m in masks], axis=0)


def place_diagonal(target, wides, row, pair):
    lane = lane_iota(HD, 128)
    for h in range(GROUP):
        first, second = (v[h * HD : (h + 1) * HD, (h // 2) * 128 : (h // 2) * 128 + 128] for v in wides)
        if h % 2 == 0:
            second = pltpu.roll(second, 64, 1)
        else:
            first = pltpu.roll(first, 64, 1)
        both = jnp.where(lane < 64, first, second).astype(BF16)
        target[row + h * HD : row + (h + 1) * HD, pair * 128 : pair * 128 + 128] = both


def to_column(values, rows):
    lanes = values.shape[1]
    return jnp.sum(jnp.where(row_iota(rows, lanes) == lane_iota(rows, lanes), values, 0.0), axis=-1, keepdims=True)


def to_row(values, lanes):
    rows = values.shape[0]
    return jnp.sum(jnp.where(row_iota(rows, lanes) == lane_iota(rows, lanes), values, 0.0), axis=0, keepdims=True)


def pad_rows(scratch, block):
    scratch[LEN - 4 :, :] = jnp.zeros((ROWS - LEN + 4, scratch.shape[1]), scratch.dtype)
    scratch[0:LEN, :] = block
    return scratch[...]


def split_lanes(slabs, values):
    for j in range(3):
        slabs[j] = values[:, j * 128 : (j + 1) * 128]


def image_rows(slabs, image, images):
    return jnp.concatenate([slabs[j, pl.ds(image, LEN, stride=images), :] for j in range(3)], axis=1)


def call(
    kernel, name, args, in_specs, out_shape, out_specs, scalars=(), grid=(1,), scratch=(), after=(), carry=(), vmem=16, aliases=None
):
    lead = len(scalars) + len(args)
    single = not isinstance(out_shape, tuple)
    shapes, specs = ((out_shape,), (out_specs,)) if single else (out_shape, tuple(out_specs))
    results = len(shapes)
    anywhere = pl.BlockSpec(memory_space=pl.ANY)
    aliases = dict(aliases or {})
    for j in range(len(carry)):
        aliases[lead + len(after) + j] = results + j

    def body(*refs):
        rest = refs[lead + len(after) + len(carry) :]
        kernel(*refs[:lead], *rest[:results], *rest[results + len(carry) :])

    out = pl.pallas_call(
        body,
        out_shape=shapes + tuple(sds(*c.shape, dtype=c.dtype) for c in carry),
        grid_spec=pltpu.PrefetchScalarGridSpec(
            num_scalar_prefetch=len(scalars),
            grid=grid,
            in_specs=list(in_specs) + [anywhere] * (len(after) + len(carry)),
            out_specs=specs + (anywhere,) * len(carry),
            scratch_shapes=list(scratch),
        ),
        input_output_aliases=aliases,
        compiler_params=pltpu.CompilerParams(vmem_limit_bytes=vmem * MIB),
        cost_estimate=pl.CostEstimate(flops=int(COSTS[name] * 1e9) + 1, bytes_accessed=int(COSTS[name] * 3e6) + 1, transcendentals=0),
        name=name,
    )(*scalars, *args, *after, *carry)
    return out[0] if single and not carry else out


def whole(*shape, buffers=None):
    mode = {} if buffers is None else dict(pipeline_mode=pl.Buffered(buffers))
    return pl.BlockSpec(shape, lambda i, *refs: (0,) * len(shape), **mode)


once = functools.partial(whole, buffers=1)


def each(*shape, per=1, shift=0):
    return pl.BlockSpec((per,) + shape, lambda i, *refs: (i + shift,) + (0,) * len(shape))


def sds(*shape, dtype=F32):
    return jax.ShapeDtypeStruct(shape, dtype)


def plan_kernel(place, routes, slots, rows_o, table_o):
    turned = place[0] == 1

    def mine_first(ref):
        v = ref[...]
        half = v.shape[0] // 2
        return jnp.where(turned, jnp.concatenate([v[half:], v[:half]], axis=0), v)

    route, slot = mine_first(routes), mine_first(slots)
    images = route.shape[0]
    key = jnp.where(slot >= 0, route * CAP + slot, -1)
    rows_o[...] = jnp.full(rows_o.shape, -1, jnp.int32)
    for i in range(images):
        rows_o[i, 0:1, 0:LEN] = key[i : i + 1]
        rows_o[i, 1:2, 0:LEN] = route[i : i + 1]
    lane = lane_iota(images, 128)
    table = jnp.zeros((images, 128), jnp.int32)
    slot_f = slot.astype(F32)
    for e in range(8):
        mine = (slot >= 0) & (route == e)
        low = jnp.min(jnp.where(mine, slot_f, float(CAP)), axis=-1, keepdims=True).astype(jnp.int32)
        high = jnp.max(jnp.where(mine, slot_f + 1.0, 0.0), axis=-1, keepdims=True).astype(jnp.int32)
        for n, (step, mask) in enumerate(((OUT_STEP, -8), (BACK_STEP, -16))):
            start = jnp.minimum(low & mask, CAP - step)
            passes = jnp.zeros_like(start)
            for k in range(-(-CAP // step) + 1):
                passes = passes + jnp.where(high - start > k * step, 1, 0)
            table = jnp.where(lane == 16 * n + e, start, table)
            table = jnp.where(lane == 16 * n + 8 + e, passes, table)
            table = jnp.where((lane == 32 + n) & (passes > 1), 1, table)
    table_o[...] = table


def plan(place, routes, slots):
    images = routes.shape[0]
    return call(
        plan_kernel, "plan", (routes, slots), [whole(*routes.shape)] * 2,
        (sds(images, 8, ROWS, dtype=jnp.int32), sds(images, 128, dtype=jnp.int32)),
        (whole(images, 8, ROWS), whole(images, 128)), scalars=(place,),
    )


def bias_kernel(place, sa, sb, sc, sd, params, hot, table_o, vecs_o, col_o, shards):
    for m, ref in enumerate((sa, sb, sc, sd)):
        shards[m ^ place[1]] = ref[...]
    heads = jnp.concatenate([shards[k][0:3, 0:256] for k in range(4)] + [jnp.zeros((4, 256), F32)], axis=0)
    high = heads.astype(BF16)
    mid = (heads - high.astype(F32)).astype(BF16)
    low = (heads - high.astype(F32) - mid.astype(F32)).astype(BF16)
    table_o[...] = dot(high, hot[...]) + dot(mid, hot[...]) + dot(low, hot[...])
    query = jnp.concatenate([shards[k][3:4, 0:96] for k in range(4)], axis=1)
    value = jnp.concatenate([shards[k][4:5, 0:96] for k in range(4)], axis=1)
    vecs_o[0:5] = params[0:5]
    vecs_o[5:6] = query
    vecs_o[6:7] = value
    vecs_o[7:8] = value
    col_o[...] = jnp.broadcast_to(to_column(value, 384), (384, 128))


def bias_tables(place, shares, params, hot):
    return call(
        bias_kernel, "bias_tables", (*shares, params, hot), [pl.BlockSpec((8, 384), lambda i, p: (48, 0))] * 4 + [once(8, 384), once(256, 4096)],
        (sds(16, 4096), sds(8, 384), sds(384, 128)), (whole(16, 4096), whole(8, 384), whole(384, 128)),
        scalars=(place,), scratch=[pltpu.VMEM((4, 8, 384), F32)],
    )


def offset_kernel(sums, hot, o):
    v = sums[...]
    high = v.astype(BF16)
    mid = (v - high.astype(F32)).astype(BF16)
    low = (v - high.astype(F32) - mid.astype(F32)).astype(BF16)
    o[...] = dot(high, hot[...], NT) + dot(mid, hot[...], NT) + dot(low, hot[...], NT)


def offset_sums(sums, hot):
    heads = sums.shape[0]
    return call(
        offset_kernel, "offset_sums", (sums, hot), [whole(*sums.shape), whole(*hot.shape)],
        sds(heads, 256), whole(heads, 256),
    )


def attention_kernel(
    place, patches, rows, wa, wb, wc, wd, table, mask, perm, perm_t, vecs, vcol, router_t,
    win_o, qkv_o, kt_o, att_o, mixt_o, x_o, h1_o, low2_o, gate_o, w_o, wt_o, wo_o, wot_o,
    block, pad, vt, bias,
):
    per = win_o.shape[0]
    images = 2 * per * pl.num_programs(0)

    @pl.when(pl.program_id(0) == 0)
    def _():
        split_lanes(block, patches[...].astype(F32))
        for m, ref in enumerate((wa, wb, wc, wd)):
            to = (m ^ place[1]) * 96
            for c in range(3):
                wt_o[pl.ds(pl.multiple_of(c * 384 + to, 32), 96), :] = ref[c * 96 : (c + 1) * 96, :].astype(BF16)
            wo_o[pl.ds(pl.multiple_of(to, 32), 96), :] = ref[288:384, :].astype(BF16)
        for c in range(3):
            w_o[:, c * 384 : (c + 1) * 384] = wt_o[c * 384 : (c + 1) * 384, :].T
        wot_o[...] = wo_o[...].T
        for w in range(4):
            for g in range(3):
                bias[w, g] = table[g] + mask[w]

    masks = head_masks()
    none = jnp.zeros((WROWS, 256), BF16)
    for n in range(per):
        at = place[0] * (images // 2) + pl.program_id(0) * per + n
        x = pad_rows(pad.at[n], image_rows(block, at, images))
        x_o[n] = x.astype(BF16)
        xhat, _ = layer_norm(x)
        low1 = (xhat * vecs[0:1] + vecs[1:2]).astype(BF16)
        win = dot(perm[...], low1).astype(BF16)
        win_o[n] = win
        packed = dot(win, w_o[...])
        qkv_o[n, :, 0:384] = (packed[:, 0:384] + vecs[5:6]).astype(BF16)
        qkv_o[n, :, 384:768] = packed[:, 384:768].astype(BF16)
        qkv_o[n, :, 768:1152] = (packed[:, 768:1152] + vecs[6:7]).astype(BF16)
        kt_o[n] = dot(wt_o[384:768, :], win, NT).astype(BF16)
        vt[n] = (dot(wt_o[768:1152, :], win, NT) + vcol[:, 0:1]).astype(BF16)
        for pair in range(2):
            for g in range(3):
                lanes = lambda c: slice(c * 384 + g * 128, c * 384 + g * 128 + 128)
                v4 = vt[n, g * 128 : (g + 1) * 128, pair * 128 : (pair + 1) * 128]
                wides = []
                for w in (2 * pair, 2 * pair + 1):
                    rs = slice(w * WROWS, (w + 1) * WROWS)
                    qs = spread(qkv_o[n, rs, lanes(0)], masks)
                    s = dot(qkv_o[n, rs, lanes(1)], qs, NT) * SCALE + bias[w, g]
                    e = jnp.exp(s - jnp.max(s, axis=0, keepdims=True))
                    low = (e * (1.0 / jnp.sum(e, axis=0, keepdims=True))).astype(BF16)
                    att_o[n, rs, g * 256 : (g + 1) * 256] = low
                    wides.append(dot(v4, jnp.concatenate([low, none] if w % 2 == 0 else [none, low], axis=0)))
                place_diagonal(mixt_o.at[n], wides, g * 128, pair)
        mixed = dot(perm_t[...], mixt_o[n], NT).astype(BF16)
        h1 = x + (dot(mixed, wo_o[...]) + vecs[2:3])
        h1_o[n] = h1
        xhat2, _ = layer_norm(h1)
        low2 = (xhat2 * vecs[3:4] + vecs[4:5]).astype(BF16)
        low2_o[n] = low2.astype(F32)
        logits = dot(router_t[...], low2, NT)[0:8]
        ex = jnp.exp(logits - jnp.max(logits, axis=0, keepdims=True))
        probs = ex / jnp.sum(ex, axis=0, keepdims=True)
        gate = jnp.sum(jnp.where(row_iota(8, ROWS) == rows[n, 1:2, :], probs, 0.0), axis=0, keepdims=True)
        hi = gate.astype(BF16).astype(F32)
        mid = (gate - hi).astype(BF16).astype(F32)
        gate_o[n, 0:1] = hi
        gate_o[n, 1:2] = mid
        gate_o[n, 2:3] = (gate - hi - mid).astype(BF16).astype(F32)
        gate_o[n, 3:8] = jnp.zeros((5, ROWS), F32)
        gate_o[n, 8:16] = probs


def attention_forward(place, patches, rows, ws, table, mask, perm, perm_t, vecs, vcol, router_t, images, after):
    per = 2
    bf = functools.partial(sds, dtype=BF16)
    out = functools.partial(each, per=per)
    return call(
        attention_kernel, "attention_forward",
        (patches, rows, *ws, table, mask, perm, perm_t, vecs, vcol, router_t),
        [once(*patches.shape), out(8, ROWS)] + [once(392, 384)] * 4
        + [once(*a.shape) for a in (table, mask, perm, perm_t, vecs, vcol, router_t)],
        (
            bf(images, 256, 384), bf(images, 256, 1152), bf(images, 384, 256), bf(images, 256, 768),
            bf(images, 384, 256), bf(images, ROWS, 384), sds(images, ROWS, 384), sds(images, ROWS, 384),
            sds(images, 16, ROWS), bf(384, 1152), bf(1152, 384), bf(384, 384), bf(384, 384),
        ),
        (
            out(256, 384), out(256, 1152), out(384, 256), out(256, 768), out(384, 256), out(ROWS, 384),
            out(ROWS, 384), out(ROWS, 384), out(16, ROWS),
            whole(384, 1152), whole(1152, 384), whole(384, 384), whole(384, 384),
        ),
        scalars=(place,), grid=(images // per,),
        scratch=[
            pltpu.VMEM((3, patches.shape[0], 128), F32),
            pltpu.VMEM((per, ROWS, 384), F32),
            pltpu.VMEM((per, 384, 256), BF16),
            pltpu.VMEM((4, 3, WROWS, 256), F32),
        ],
        after=after,
        vmem=40,
    )


def hits(keys, expert, first, base, step):
    code = row_iota(step, keys.shape[1]) + (expert * CAP + base)
    return jnp.where((code == keys) & (code >= expert * CAP + first), 1.0, 0.0).astype(BF16)


def to_slots(i, table, keys, tile, gates, acc, acc_gate):
    experts, step = acc.shape[0], OUT_STEP

    def store(e, base, moved, gated):
        at = pl.ds(pl.multiple_of(base, 8), step)
        acc[e, at, :] = acc[e, at, :] + moved
        if gates is not None:
            acc_gate[e, at, :] = acc_gate[e, at, :] + gated

    firsts = [table[i, e] for e in range(experts)]
    hit = jnp.concatenate([hits(keys, e, firsts[e], firsts[e], step) for e in range(experts)], axis=0)
    moved = dot(hit, tile)
    gated = None if gates is None else dot(hit, gates, NT)
    for e in range(experts):
        part = slice(e * step, (e + 1) * step)
        store(e, firsts[e], moved[part], None if gates is None else gated[part])

    @pl.when(table[i, 32] > 0)
    def _():
        def expert(e, _):
            def more(r, _):
                first = table[i, e] + r * step
                base = jnp.minimum(first, CAP - step)
                extra = hits(keys, e, first, base, step)
                store(e, base, dot(extra, tile), None if gates is None else dot(extra, gates, NT))
                return 0

            return lax.fori_loop(1, table[i, 8 + e], more, 0)

        lax.fori_loop(0, experts, expert, 0)


def cotangent_kernel(place, table, rows, cot, slots_o, tokens_o, block, acc):
    i = pl.program_id(0)
    per = tokens_o.shape[0]
    images = pl.num_programs(0) * per

    @pl.when(i == 0)
    def _():
        split_lanes(block, cot[...].astype(F32))
        acc[...] = jnp.zeros_like(acc)

    for n in range(per):
        at = lax.rem(i * per + n + place[0] * (images // 2), images)
        tokens_o[n] = jnp.zeros((ROWS, 384), BF16)
        tile = image_rows(block, at, images).astype(BF16)
        tokens_o[n, 0:LEN, :] = tile
        to_slots(i * per + n, table, rows[n, 0:1, 0:LEN], tile, None, acc, None)

    @pl.when(i == pl.num_programs(0) - 1)
    def _():
        slots_o[...] = acc[...].astype(BF16)


def dispatch_cotangent(place, table, rows, cot, experts, after):
    images = rows.shape[0]
    return call(
        cotangent_kernel, "dispatch_cotangent", (rows, cot), [each(8, ROWS, per=4), once(*cot.shape)],
        (sds(experts, CAP, 384, dtype=BF16), sds(images, ROWS, 384, dtype=BF16)),
        (whole(experts, CAP, 384), each(ROWS, 384, per=4)), scalars=(place, table), grid=(images // 4,),
        scratch=[pltpu.VMEM((3, cot.shape[0], 128), F32), pltpu.VMEM((experts, CAP, 384), F32)], after=after, vmem=28,
    )


def low2_kernel(table, rows, mine, other, gates, gates_other, slots_o, gate_o, acc):
    i = pl.program_id(0)
    images = pl.num_programs(0)

    @pl.when(i == 0)
    def _():
        acc[...] = jnp.zeros_like(acc)
        gate_o[...] = jnp.zeros_like(gate_o)

    own = i < images // 2
    per = mine.shape[0]
    for n in range(per):
        tile = jnp.where(own, mine[n], other[n]).astype(BF16)
        gate = jnp.where(own, gates[n], gates_other[n]).astype(BF16)
        to_slots(i * per + n, table, rows[n, 0:1, :], tile, gate, acc, gate_o)

    @pl.when(i == images - 1)
    def _():
        slots_o[...] = acc[...].astype(BF16)


def dispatch_low2(table, rows, mine, other, gates, gates_other, experts, after):
    images = rows.shape[0] // 4
    half = images // 2
    first = lambda *shape: pl.BlockSpec((4,) + shape, lambda i, t: (jnp.minimum(i, half - 1), 0, 0))
    second = lambda *shape: pl.BlockSpec((4,) + shape, lambda i, t: (jnp.maximum(i - half, 0), 0, 0))
    return call(
        low2_kernel, "dispatch_low2", (rows, mine, other, gates, gates_other),
        [each(8, ROWS, per=4), first(ROWS, 384), second(ROWS, 384), first(16, ROWS), second(16, ROWS)],
        (sds(experts, CAP, 384, dtype=BF16), sds(experts, CAP, 16)),
        (whole(experts, CAP, 384), whole(experts, CAP, 16)), scalars=(table,), grid=(images,),
        scratch=[pltpu.VMEM((experts, CAP, 384), F32)], after=after, vmem=28,
    )


def expert_kernel(place, buf, gates, gbuf, up, down, up_b, down_b, unused, gu_o, gd_o, rg_o, gdb_o):
    x = buf[0]
    gate = gates[0][:, 0:1] + gates[0][:, 1:2] + gates[0][:, 2:3]
    g = (gate * gbuf[0].astype(F32)).astype(BF16)
    gdb_o[0] = jnp.broadcast_to(jnp.sum(g.astype(F32), axis=0, keepdims=True), (8, 384))
    w_up, w_down = up[0], down[0]
    hp = dot(x, w_up) + up_b[0]
    c0 = np.float32(np.sqrt(2 / np.pi))
    th = jnp.tanh(c0 * (hp + 0.044715 * (hp * hp * hp)))
    act = (hp * (0.5 * (1.0 + th))).astype(BF16)
    slope = 0.5 * (1.0 + th) + (0.5 * hp) * (1.0 - th * th) * (c0 * (1.0 + (3 * 0.044715) * (hp * hp)))
    lead = jnp.where(place[1] == 0, 1.0, 0.0)
    rg_o[:, 0:384] = (dot(act, w_down) + lead * down_b[0]).astype(BF16)
    gd_o[...] = dot(act, g, TN)
    gp = (dot(g, w_down, NT) * slope).astype(BF16)
    gu_o[0:384] = dot(x, gp, TN)
    gu_o[384:392] = jnp.broadcast_to(jnp.sum(gp.astype(F32), axis=0, keepdims=True), (8, 384))
    rg_o[:, 384:768] = dot(gp, w_up, NT).astype(BF16)


def expert_pass(step, place, buf, gates, gbuf, up, down, up_b, down_b, sums, after):
    at = lambda *shape: pl.BlockSpec((1,) + shape, lambda i, p: (p[2 + step],) + (0,) * len(shape))
    return call(
        expert_kernel, "expert_pass", (buf, gates, gbuf, up, down, up_b, down_b, sums),
        [at(CAP, 384), at(CAP, 16), at(CAP, 384), at(384, 384), at(384, 384), at(1, 384), at(1, 384)]
        + [pl.BlockSpec(memory_space=pl.ANY)],
        (sds(392, 384), sds(384, 384), sds(CAP, 768, dtype=BF16), sds(*sums.shape)),
        (whole(392, 384), whole(384, 384), whole(CAP, 768), pl.BlockSpec((1, 8, 384), lambda i, p: (step, 0, 0))),
        scalars=(place,), after=after, aliases={8: 3},
    )


def back_to_tokens(i, place, table, key_row, cot, refs, windows, back):
    experts, step = len(refs), BACK_STEP
    keys = to_column(key_row.astype(F32), ROWS).astype(jnp.int32)
    lane = lane_iota(1, experts * step)
    code = jnp.zeros((1, experts * step), jnp.int32)
    for s in range(experts):
        e = place[2 + s]
        first = table[i, 16 + e]
        windows[s * step : (s + 1) * step, :] = refs[s][pl.ds(pl.multiple_of(first, 16), step), :]
        code = jnp.where(lane >= s * step, e * CAP + first + lane - s * step, code)
    back[...] = dot(jnp.where(code == keys, 1.0, 0.0).astype(BF16), windows[...])

    @pl.when(table[i, 33] > 0)
    def _():
        narrow = lane_iota(1, step)
        for s in range(experts):
            e = place[2 + s]

            def more(r, _):
                first = table[i, 16 + e] + r * step
                base = jnp.minimum(first, CAP - step)
                slot = narrow + base
                hit = (e * CAP + slot == keys) & (slot >= first)
                block = refs[s][pl.ds(pl.multiple_of(base, 16), step), :]
                back[...] = back[...] + dot(jnp.where(hit, 1.0, 0.0).astype(BF16), block)
                return 0

            lax.fori_loop(1, table[i, 24 + e], more, 0)

    tok, gl = back[:, 0:384], back[:, 384:768]
    dots = jnp.sum(tok * cot.astype(F32), axis=-1, keepdims=True)
    mark = jnp.concatenate([to_row(dots, ROWS), jnp.zeros((1, 384 - ROWS), F32)], axis=1)
    return jnp.where(row_iota(ROWS, 384) == LEN + 4, mark, gl), tok


def combine_far_kernel(offset, place, table, rows, cot, r0, r1, r2, r3, r4, r5, r6, r7, gl_o, tok_o, windows, back):
    refs = (r0, r1, r2, r3, r4, r5, r6, r7)
    per = gl_o.shape[0]
    for n in range(per):
        at = pl.program_id(0) * per + n + offset
        gl_o[n], tok_o[n] = back_to_tokens(at, place, table, rows[n, 0:1, :], cot[n], refs, windows.at[n], back.at[n])


def combine_scratch(experts):
    return [pltpu.VMEM((2, experts * BACK_STEP, 768), BF16), pltpu.VMEM((2, ROWS, 768), F32)]


def combine_far(place, table, rows, cot, results, after):
    images = rows.shape[0]
    half = images // 2
    return call(
        functools.partial(combine_far_kernel, half), "combine_far", (rows, cot, *results),
        [each(8, ROWS, per=2, shift=half // 2), each(ROWS, 384, per=2, shift=half // 2)] + [once(CAP, 768)] * len(results),
        (sds(half, ROWS, 384),) * 2, (each(ROWS, 384, per=2),) * 2, scalars=(place, table), grid=(half // 2,),
        scratch=combine_scratch(len(results)), after=after, vmem=20,
    )


def combine_own_kernel(
    place, table, rows, cot, r0, r1, r2, r3, r4, r5, r6, r7, gl_got, tok_got, g0, g1, g2, g3, tok_o, windows, back
):
    i = pl.program_id(0)
    refs = (r0, r1, r2, r3, r4, r5, r6, r7)
    parts = []
    for n in range(2):
        gl, tok = back_to_tokens(2 * i + n, place, table, rows[n, 0:1, :], cot[n], refs, windows.at[n], back.at[n])
        tok_o[n] = tok + tok_got[n]
        parts.append(gl + gl_got[n])
    for c, ref in enumerate((g0, g1, g2, g3)):

        @pl.when(i == c)
        def _():
            ref[0], ref[1] = parts


def combine_own(place, table, rows, cot, results, gl_got, tok_got, after):
    half = gl_got.shape[0]
    return call(
        combine_own_kernel, "combine_own", (rows, cot, *results, gl_got, tok_got),
        [each(8, ROWS, per=2), each(ROWS, 384, per=2)] + [once(CAP, 768)] * len(results) + [each(ROWS, 384, per=2)] * 2,
        (sds(2, ROWS, 384),) * 4 + (sds(half, ROWS, 384),), (whole(2, ROWS, 384),) * 4 + (each(ROWS, 384, per=2),),
        scalars=(place, table), grid=(half // 2,), scratch=combine_scratch(len(results)), after=after, vmem=24,
    )


def backward_kernel(
    first, offset, images, place, count, own, other, cot, rows, h1, low2_r, gate_r, mixt, win_r, qkv, kt, att, x_r,
    w, wt, wot, perm, perm_t, vecs, router_t,
    dw_i, dwo_i, dtb_i, dv_i, dr_i,
    gp_o, dw_o, dwo_o, dtb_o, dv_o, dr_o,
    dqt, dkv,
):
    for src, dst in ((dw_i, dw_o), (dwo_i, dwo_o), (dtb_i, dtb_o), (dv_i, dv_o), (dr_i, dr_o)):
        dst[...] = jnp.zeros(dst.shape, F32) if first else src[...]
    masks = head_masks()
    none = jnp.zeros((WROWS, 256), BF16)
    ones = jnp.ones((16, 256), BF16)

    def add(r, v):
        dv_o[r : r + 1, :] = dv_o[r : r + 1, :] + v

    for n in range(own.shape[0]):
        total = own[n] + other[n]
        gl = jnp.where(row_iota(ROWS, 384) < LEN, total, 0.0)
        gg = total[LEN + 4 : LEN + 5, 0:ROWS]
        at = place[0] * images + offset + n
        grad = cot[n].astype(F32) * jnp.where(at < count[0], 1.0, 0.0)
        probs = gate_r[n, 8:16]
        hot = jnp.where(row_iota(8, ROWS) == rows[n, 1:2, :], 1.0, 0.0)
        gate = jnp.sum(probs * hot, axis=0, keepdims=True)
        glog = jnp.concatenate([probs * (hot - gate) * gg, jnp.zeros((8, ROWS), F32)], axis=0).astype(BF16)
        low2 = low2_r[n].astype(BF16)
        dr_o[...] += dot(glog, low2)
        g2 = gl + dot(glog, router_t[...], TN)
        xhat2, inv2 = layer_norm(h1[n])
        add(3, jnp.sum(g2 * xhat2, axis=0, keepdims=True))
        add(4, jnp.sum(g2, axis=0, keepdims=True))
        gh1 = grad + norm_back(g2 * vecs[3:4], xhat2, inv2)
        gattn = gh1.astype(BF16)
        gwin = dot(perm[...], gattn).astype(BF16)
        add(2, dot(ones, gwin)[0:1])
        dwo_o[...] += dot(mixt[n], gwin)
        gmw = dot(gwin, wot[...]).astype(BF16)
        for g in range(3):
            lanes = lambda c: slice(c * 384 + g * 128, c * 384 + g * 128 + 128)
            table_sum = dtb_o[g]
            for pair in range(2):
                k4 = kt[n, g * 128 : (g + 1) * 128, pair * 128 : (pair + 1) * 128]
                wides = []
                for wi in (2 * pair, 2 * pair + 1):
                    rs = slice(wi * WROWS, (wi + 1) * WROWS)
                    qs = spread(qkv[n, rs, lanes(0)], masks)
                    dms = spread(gmw[rs, g * 128 : (g + 1) * 128], masks)
                    a_low = att[n, rs, g * 256 : (g + 1) * 256]
                    a = a_low.astype(F32)
                    da = dot(qkv[n, rs, lanes(2)], dms, NT)
                    ds = (a * (da - jnp.sum(da * a, axis=0, keepdims=True))).astype(BF16)
                    table_sum = table_sum + ds.astype(F32)
                    dkv[n, rs, g * 128 : (g + 1) * 128] = (SCALE * dot(ds, qs)).astype(BF16)
                    dkv[n, rs, 384 + g * 128 : 512 + g * 128] = dot(a_low, dms).astype(BF16)
                    wides.append(SCALE * dot(k4, jnp.concatenate([ds, none] if wi % 2 == 0 else [none, ds], axis=0)))
                place_diagonal(dqt.at[n], wides, g * 128, pair)
            dtb_o[g] = table_sum
        win = win_r[n]
        dw_o[0:384] += dot(dqt[n], win)
        dw_o[384:1152] += dot(dkv[n], win, TN)
        add(5, dot(ones, dqt[n], NT)[0:1])
        add(6, dot(ones, dkv[n, :, 384:768])[0:1])
        part = dot(dkv[n], wt[384:1152, :])
        hi = part.astype(BF16)
        lo = (part - hi.astype(F32)).astype(BF16)
        part_t = dot(w[:, 0:384], dqt[n])
        hi_t = part_t.astype(BF16)
        lo_t = (part_t - hi_t.astype(F32)).astype(BF16)
        pt = perm_t[...]
        gl1 = dot(pt, hi) + dot(pt, lo) + dot(pt, hi_t, NT) + dot(pt, lo_t, NT)
        xhat1, inv1 = layer_norm(x_r[n].astype(F32))
        add(0, jnp.sum(gl1 * xhat1, axis=0, keepdims=True))
        add(1, jnp.sum(gl1, axis=0, keepdims=True))
        gp_o[n] = gh1 + norm_back(gl1 * vecs[0:1], xhat1, inv1)


def attention_backward(first, c, place, count, own, other, cot, rows, saved, w, wt, wot, consts, acc, after, carry=()):
    per = own.shape[0]
    h1, low2, gates, mixt, win, qkv, kt, att, x = saved
    mine = functools.partial(each, per=per, shift=c)
    accs = [once(*a.shape) for a in acc]
    args = (own, other, cot, rows, h1, low2, gates, mixt, win, qkv, kt, att, x, w, wt, wot, *consts, *acc)
    specs = (
        [each(ROWS, 384, per=per)] * 2
        + [mine(*a.shape[1:]) for a in (cot, rows, h1, low2, gates, mixt, win, qkv, kt, att, x)]
        + [once(*a.shape) for a in (w, wt, wot, *consts)]
        + accs
    )
    lead = 2 + len(args) - len(acc)
    return call(
        functools.partial(backward_kernel, first, c * per, h1.shape[0]), "attention_backward", args, specs,
        (sds(per, ROWS, 384),) + tuple(sds(*a.shape) for a in acc), (each(ROWS, 384, per=per),) + tuple(whole(*a.shape) for a in acc),
        scalars=(place, count), scratch=[pltpu.VMEM((per, 384, 256), BF16), pltpu.VMEM((per, 256, 768), BF16)],
        after=after, carry=carry, vmem=32, aliases={lead + j: 1 + j for j in range(len(acc))},
    )


def add_arrays(a, b, blocks, after=(), carry=()):
    def kernel(x, y, o):
        o[...] = x[...] + y[...]

    rows = a.shape[0] // blocks
    spec = pl.BlockSpec((rows,) + a.shape[1:], lambda i: (i,) + (0,) * (a.ndim - 1))
    return call(kernel, "add", (a, b), [spec, spec], sds(*a.shape), spec, grid=(blocks,), after=after, carry=carry)


def hand_on(after, carry):
    def kernel(o):
        o[...] = jnp.zeros(o.shape, F32)

    return call(kernel, "hand_on", (), (), (sds(8, 128),), (whole(8, 128),), after=after, carry=carry)[1:]


def block_out_kernel(place, count, h1, gates, own, other, rows, o):
    per = o.shape[0]
    for n in range(per):
        i = pl.program_id(0) * per + n
        gate = gates[n, 0:1] + gates[n, 1:2] + gates[n, 2:3]
        weight = to_column(jnp.where(rows[n, 0:1] >= 0, gate, 0.0), ROWS)
        keep = jnp.where(place[0] * pl.num_programs(0) * per + i < count[0], 1.0, 0.0)
        value = keep * (h1[n] + weight * (own[n] + other[n]))
        o[n] = value.astype(BF16).astype(F32)


def block_out_pass(place, count, h1, gates, own, other, rows, after):
    images = h1.shape[0]
    return call(
        block_out_kernel, "block_out", (h1, gates, own, other, rows),
        [each(ROWS, 384, per=2), each(16, ROWS, per=2), each(ROWS, 384, per=2), each(ROWS, 384, per=2), each(8, ROWS, per=2)],
        sds(images, ROWS, 384), each(ROWS, 384, per=2), scalars=(place, count), grid=(images // 2,), after=after,
    )


def join_pass(place, own, other, dtype, after=()):
    images = 2 * sum(a.shape[0] for a in own)
    slab = lambda *lead: pl.BlockSpec(lead + (128,), lambda j, p: (0,) * len(lead) + (j,))

    def kernel(p, *refs):
        out = refs[len(own) + len(other)]
        wide = out if dtype == F32 else refs[-1]
        for side, group in ((0, refs[: len(own)]), (1, refs[len(own) : len(own) + len(other)])):
            at = (p[0] ^ side) * (images // 2)
            for ref in group:
                for n in range(ref.shape[0]):
                    wide[pl.ds(at, LEN, stride=images), :] = ref[n, 0:LEN, :]
                    at = at + 1
        if dtype != F32:
            out[...] = wide[...].astype(dtype)

    return call(
        kernel, "join", (*own, *other), [slab(a.shape[0], ROWS) for a in (*own, *other)],
        sds(LEN * images, 384, dtype=dtype), slab(LEN * images), scalars=(place,), grid=(3,),
        scratch=[] if dtype == F32 else [pltpu.VMEM((LEN * images, 128), F32)], after=after,
    )


def share_kernel(place, dw, dwo, by_offset, vec, router, downs, mine, far):
    for flip, out in ((0, mine), (1, far)):
        t = place[1] ^ flip
        at = pl.multiple_of(t * 96, 32)
        for c in range(3):
            out[c * 96 : (c + 1) * 96, :] = dw[pl.ds(pl.multiple_of(c * 384 + at, 32), 96), :]
        out[288:384, :] = dwo[pl.ds(at, 96), :]
        out[384:448, :] = jnp.zeros((64, 384), F32)
        for k in range(4):

            @pl.when(t == k)
            def _():
                out[384:387, 0:256] = by_offset[3 * k : 3 * k + 3, :]
                out[387:388, 0:96] = vec[5:6, 96 * k : 96 * k + 96]
                out[388:389, 0:96] = vec[6:7, 96 * k : 96 * k + 96]

        out[392:397, :] = vec[0:5, :]
        out[400:408, :] = router[0:8, :]
    for s in range(downs.shape[0]):
        mine[pl.ds(408 + place[2 + s], 1), :] = downs[s, 0:1, :]


def share_pass(place, dw, dwo, by_offset, vec, router, downs):
    args = (dw, dwo, by_offset, vec, router, downs)
    return call(
        share_kernel, "share", args, [once(*a.shape) for a in args],
        (sds(448, 384), sds(448, 384)), (whole(448, 384), whole(448, 384)), scalars=(place,),
    )


def halve_pass(own, got, bit, place, after=()):
    half = own.shape[0] // 2

    def kernel(p, a, b, send, keep):
        up = p[bit] != 0
        low = a[:half] + b[:half]
        high = a[half:] + b[half:]
        send[...] = jnp.where(up, low, high)
        keep[...] = jnp.where(up, high, low)

    return call(
        kernel, "halve", (own, got), [whole(*own.shape)] * 2, (sds(half, 384),) * 2, (whole(half, 384),) * 2,
        scalars=(place,), after=after,
    )


def double_pass(own, got, bit, place, after=()):
    rows = own.shape[0]

    def kernel(p, a, b, o):
        up = p[bit] != 0
        o[:rows] = jnp.where(up, b[...], a[...])
        o[rows:] = jnp.where(up, a[...], b[...])

    return call(
        kernel, "double", (own, got), [whole(*own.shape)] * 2, sds(2 * rows, 384), whole(2 * rows, 384),
        scalars=(place,), after=after,
    )


def gather_pass(place, ups, downs, shift, targets, after=()):
    count, experts = len(ups), 8

    def kernel(p, *refs):
        up_o, down_o, bias_o = refs[-3:]
        for k in range(count):

            @pl.when(pl.program_id(0) == k)
            def _():
                up_o[0] = refs[k][0:384, :]
                down_o[0] = refs[count + k][...]
                bias_o[0] = refs[k][384:392, :]

    at = lambda *shape: pl.BlockSpec((1,) + shape, lambda i, p: (p[2 + lax.rem(i + shift + experts - 1, experts)], 0, 0))
    anywhere = pl.BlockSpec(memory_space=pl.ANY)
    return call(
        kernel, "gather", (*ups, *downs, *targets),
        [once(392, 384)] * count + [once(384, 384)] * count + [anywhere] * len(targets),
        (sds(experts, 384, 384), sds(experts, 384, 384), sds(experts, 8, 384)), (at(384, 384), at(384, 384), at(8, 384)),
        scalars=(place,), grid=(count,), after=after, aliases={1 + 2 * count + j: j for j in range(len(targets))}, vmem=20,
    )


def swap_core(x):
    return lax.ppermute(x, "tensor", [(0, 1), (1, 0), (2, 3), (3, 2)])


def swap_chip(x):
    return lax.ppermute(x, "tensor", [(0, 2), (2, 0), (1, 3), (3, 1)])


def shape_back(values, length, images):
    return values.reshape(length, images, values.shape[-1]).transpose(1, 0, 2)


def on_device(
    n_dp, patches, image_count, routes, slot_index, norm1_gain, norm1_bias, input_proj, query_value_bias,
    position_bias, output_proj, output_bias, norm2_gain, norm2_bias, router_weight, up_weight, up_bias,
    down_weight, down_bias, cotangent,
):
    images, length, width = patches.shape
    half = images // 2
    experts = up_weight.shape[0]
    tensor = lax.axis_index("tensor")
    core = tensor % 2
    ring = n_dp == experts
    cycle = [0, 2, 4, 6, 7, 5, 3, 1]
    where = {d: i for i, d in enumerate(cycle)}
    dp = lax.axis_index("dp")
    spots = np.zeros((4 * n_dp, 16), np.int32)
    for d in range(n_dp):
        for t in range(4):
            rank = 0
            if ring:
                rank = where[d] if t % 2 == 0 else (n_dp - where[d]) % n_dp
            spots[4 * d + t, :13] = [t % 2, t] + [(rank - s) % experts for s in range(experts)] + [d >> b & 1 for b in range(3)]
    place = lax.dynamic_slice(jnp.asarray(spots), (4 * dp + tensor, 0), (1, 16)).reshape(16)
    if ring:
        pairs = []
        for d in range(n_dp):
            for t in range(4):
                to = cycle[(where[d] + (1 if t % 2 == 0 else -1)) % n_dp]
                pairs.append((d * 4 + t, to * 4 + t))
    onward = lambda v: lax.ppermute(v, ("dp", "tensor"), pairs)
    swap_dp = lambda v, bit: lax.ppermute(v, "dp", [(d, d ^ bit) for d in range(n_dp)])
    perm_np, mask_np, relative_np = window_tables()
    perm = jnp.asarray(perm_np, BF16)
    perm_t = jnp.asarray(perm_np.T, BF16)
    mask = jnp.asarray(mask_np)
    hot_np = np.arange(256)[:, None] == relative_np.reshape(1, -1)
    hot = jnp.asarray(hot_np, BF16)

    local = query_value_bias.shape[1]
    proj = jnp.concatenate(
        [
            input_proj.transpose(1, 2, 0).reshape(3 * local, width).astype(F32),
            output_proj.astype(F32),
            jnp.pad(position_bias.T, ((0, 0), (0, width - REL))),
            jnp.pad(query_value_bias, ((0, 3), (0, width - local))),
        ]
    )
    proj_x = swap_chip(proj)
    proj_c = swap_core(proj)
    params = jnp.stack([norm1_gain, norm1_bias, output_bias, norm2_gain, norm2_bias] + [norm1_gain] * 3)
    router_t = jnp.pad(router_weight.T, ((0, 8), (0, 0)))

    rows, table = plan(place, routes, slot_index)
    flat = lambda v: v.transpose(1, 0, 2).reshape(length * images, width)
    gbuf, cot = dispatch_cotangent(place, table, rows, flat(cotangent), experts, ())
    (proj_x,) = hand_on((gbuf,), (proj_x,))
    proj_d = swap_core(proj_x)
    shares = (proj, proj_c, proj_x, proj_d)
    flat_table, vecs, vcol = bias_tables(place, shares, params, hot)
    bias = flat_table[0:12].reshape(3, 4, 64, 64).transpose(0, 2, 1, 3).reshape(3, 64, 256)
    win, qkv, kt, att, mixt, x, h1, low2, gates, w, wt, wo, wot = attention_forward(
        place, flat(patches), rows, shares, bias, mask, perm, perm_t, vecs, vcol, router_t, half, (gbuf,)
    )
    buf, slot_gates = dispatch_low2(table, rows, low2, swap_core(low2), gates, swap_core(gates), experts, (gbuf,))

    results, ups, downs, down_sums = [], [], [], [jnp.zeros((experts, 8, 384), F32)]
    up_b = up_bias.reshape(experts, 1, 384)
    down_b = down_bias.reshape(experts, 1, 384)

    def expert(s, last=None):
        after = () if last is None else (last,)
        gu, gd, rg, gdb = expert_pass(
            s, place, buf, slot_gates, gbuf, up_weight, down_weight, up_b, down_b, down_sums[0], after
        )
        results.append(rg)
        ups.append(gu)
        downs.append(gd)
        down_sums[0] = gdb
        return gdb

    flying, sums = {}, ([], [])
    steps = [0, 0]

    def serve(which, last, carry=(), also=()):
        if not ring:
            return (last, *carry) if carry else last
        steps[which] += 1
        step = steps[which]
        value = flying[which]
        if step < experts:
            value = add_arrays(value, (ups, downs)[which][step], 1 if which == 0 else 2, (last, *also), carry)
            if carry:
                value, *carry = value
        if step >= experts - 1:
            sums[which].append(value)
        if step < 2 * experts - 2:
            flying[which] = onward(value)
        return (value, *carry) if carry else value

    UP, DOWN = 0, 1
    last = expert(0)
    if ring:
        flying = {UP: onward(ups[0]), DOWN: onward(downs[0])}
    last = expert(2, expert(1, last))
    last = serve(UP, last)
    last = expert(3, last)
    last = serve(DOWN, last)
    last = expert(5, expert(4, last))
    last = serve(UP, last)
    last = expert(6, last)
    last = serve(DOWN, last)
    last = expert(7, last)
    gl_far, tok_far = combine_far(place, table, rows, cot, results, (last,))
    last, gl_far, tok_far = serve(UP, gl_far, (gl_far, tok_far))
    gl_got, tok_got = swap_core(gl_far), swap_core(tok_far)
    last = serve(DOWN, last)
    *gl, tok_mine = combine_own(place, table, rows, cot, results, gl_got, tok_got, (last,))
    their = [swap_chip(gl[0])]
    last, gl[1] = serve(UP, tok_mine, (gl[1],))
    their.append(swap_chip(gl[1]))
    last = serve(DOWN, last)
    last, gl[2] = serve(UP, last, (gl[2],), (their[0],))
    their.append(swap_chip(gl[2]))
    last = serve(DOWN, last)
    consts = (perm, perm_t, vecs, router_t)
    saved = (h1, low2, gates, mixt, win, qkv, kt, att, x)
    acc = [
        jnp.zeros((1152, 384), F32), jnp.zeros((384, 384), F32), jnp.zeros((3, 64, 256), F32),
        jnp.zeros((8, 384), F32), jnp.zeros((16, 384), F32),
    ]
    grads = []

    def backward(c, carry):
        gp, *more = attention_backward(
            c == 0, c, place, image_count, gl[c], their[c], cot, rows, saved, w, wt, wot, consts, acc, (last,), carry
        )
        acc[:] = more[:5]
        grads.append(gp)
        return more[5:]

    (gl[3],) = backward(0, (gl[3],))
    their.append(swap_chip(gl[3]))
    last = serve(DOWN, serve(UP, grads[-1]))
    backward(1, ())
    last = serve(DOWN, serve(UP, grads[-1]))
    backward(2, ())
    last = serve(DOWN, serve(UP, grads[-1]))
    (tok_mine,) = backward(3, (tok_mine,))
    tok_their = swap_chip(tok_mine)
    last = serve(DOWN, serve(UP, grads[-1]))
    gp_got = [swap_core(v) for v in grads]

    dw, dwo, dtb, dvec, drouter = acc
    by_offset = offset_sums(dtb.reshape(3, 64, 4, 64).transpose(0, 2, 1, 3).reshape(12, 4096), hot)
    mine, far = share_pass(place, dw, dwo, by_offset, dvec, drouter, down_sums[0])
    got = swap_core(far)
    if ring:
        for b in range(3):
            send, mine = halve_pass(mine, got, 10 + b, place, (last,))
            got = swap_dp(send, 1 << b)
            last = serve(b % 2, mine)
        total = add_arrays(mine, got, 1, (last,))
        for b in (2, 1, 0):
            got = swap_dp(total, 1 << b)
            last = serve((b + 1) % 2, last)
            total = double_pass(total, got, 10 + b, place, (last,))
    else:
        total = lax.psum(mine + got, "dp")
    grad_patches = shape_back(join_pass(place, grads, gp_got, F32, (last,)), length, images)
    if ring:
        while steps[DOWN] < 2 * experts - 2:
            last = serve(UP, last) if steps[UP] <= steps[DOWN] else serve(DOWN, last)
    out_own = block_out_pass(place, image_count, h1, gates, tok_mine, tok_their, rows, (last, total))
    block_out = shape_back(join_pass(place, (out_own,), (swap_core(out_own),), BF16), length, images)
    if ring:
        early = 6
        targets = gather_pass(place, sums[UP][:early], sums[DOWN][:early], 0, ())
        grad_up, grad_down, bias8 = gather_pass(place, sums[UP][early:], sums[DOWN][early:], early, targets)
        grad_up_bias = bias8[:, 0]
    else:
        everything = lax.psum(jnp.concatenate([jnp.stack(ups), jnp.stack(downs)], axis=1), "dp")
        everything = jnp.take(everything, jnp.asarray([(0 - s) % experts for s in range(experts)]), axis=0)
        grad_up, grad_up_bias, grad_down = everything[:, 0:384], everything[:, 384], everything[:, 392:776]
    return (
        block_out,
        grad_patches,
        total[392],
        total[393],
        total[0:288].reshape(3, 96, 384).transpose(2, 0, 1),
        total[387:389, 0:96],
        total[384:387, 0:REL].T,
        total[288:384],
        total[394],
        total[395],
        total[396],
        total[400:408].T,
        grad_up,
        grad_up_bias,
        grad_down,
        total[408:416],
    )


def solution(mesh):
    in_specs = (
        P("dp", None, None), P("dp"), P("dp", None), P("dp", None), P(), P(), P(None, None, "tensor"),
        P(None, "tensor"), P(None, "tensor"), P("tensor", None), P(), P(), P(), P(), P(None, None, "tensor"),
        P(None, "tensor"), P(None, "tensor", None), P(), P("dp", None, None),
    )
    out_specs = (
        P("dp", None, None), P("dp", None, None), P(), P(), P(None, None, "tensor"), P(None, "tensor"),
        P(None, "tensor"), P("tensor", None), P(), P(), P(), P(), P(None, None, "tensor"), P(None, "tensor"),
        P(None, "tensor", None), P(),
    )
    return jax.shard_map(
        functools.partial(on_device, mesh.shape["dp"]),
        mesh=mesh, in_specs=in_specs, out_specs=out_specs, check_vma=False,
    )
```

```python
import functools

import jax
import jax.numpy as jnp
import numpy as np
from jax import lax
from jax.experimental import pallas as pl
from jax.experimental.pallas import tpu as pltpu
from jax.sharding import PartitionSpec as P

HD = 32
WIN = 7
SIDE = 14
SHIFT = 3
CAP = 512
CELLS = WIN * WIN
LEN = SIDE * SIDE
ROWS = 208
WROWS = 64
OUT_STEP = 64
BACK_STEP = 64
REL = (2 * WIN - 1) ** 2
EPS = 1e-05
SCALE = HD**-0.5
GROUP = 4
MIB = 1024 * 1024
COSTS = dict(
    pack=1, plan=1, bias_tables=1.5, offset_sums=2, attention_forward=24, dispatch_cotangent=9, dispatch_low2=4.5, expert_pass=2.4,
    combine_far=4.4, combine_own=6.4, attention_backward=8.5, add=0.1, hand_on=0.1, block_out=4, join=4.8, share=1,
    halve=0.5, double=0.5, gather=5,
)
F32 = jnp.float32
BF16 = jnp.bfloat16
NN = ((1,), (0,))
NT = ((1,), (1,))
TN = ((0,), (0,))


def dot(a, b, dims=NN):
    return lax.dot_general(a, b, (dims, ((), ())), preferred_element_type=F32)


def layer_norm(values):
    center = values - jnp.mean(values, axis=-1, keepdims=True)
    inverse = lax.rsqrt(jnp.mean(center * center, axis=-1, keepdims=True) + EPS)
    return center * inverse, inverse


def norm_back(grad_hat, normed, inverse):
    return inverse * (
        grad_hat
        - jnp.mean(grad_hat, axis=-1, keepdims=True)
        - normed * jnp.mean(grad_hat * normed, axis=-1, keepdims=True)
    )


def window_tables():
    perm = np.zeros((4 * WROWS, ROWS), np.float32)
    label = np.zeros((4, CELLS), np.int32)
    band = lambda v: int(v >= SIDE - WIN) + int(v >= SIDE - SHIFT)
    for w in range(4):
        for a in range(WIN):
            for b in range(WIN):
                r, c = (w // 2) * WIN + a, (w % 2) * WIN + b
                perm[w * WROWS + a * WIN + b, ((r + SHIFT) % SIDE) * SIDE + (c + SHIFT) % SIDE] = 1
                label[w, a * WIN + b] = 3 * band(r) + band(c)
    mask = np.full((4, WROWS, WROWS), -1e30, np.float32)
    mask[:, :CELLS, :] = 0
    same = label[:, :, None] == label[:, None, :]
    mask[:, :CELLS, :CELLS] = np.where(same, 0.0, -100.0)
    cells = np.arange(CELLS)
    rows, cols = cells // WIN, cells % WIN
    rel = (rows[None, :] - rows[:, None] + WIN - 1) * (2 * WIN - 1) + (cols[None, :] - cols[:, None] + WIN - 1)
    relative = np.full((WROWS, WROWS), -1, np.int32)
    relative[:CELLS, :CELLS] = rel
    return perm, np.tile(mask, (1, 1, GROUP)), relative


def lane_iota(rows, cols):
    return lax.broadcasted_iota(jnp.int32, (rows, cols), 1)


def row_iota(rows, cols):
    return lax.broadcasted_iota(jnp.int32, (rows, cols), 0)


def head_masks():
    lane = lane_iota(1, 128) // HD
    return [(lane == h).astype(F32).astype(BF16) for h in range(GROUP)]


def spread(block, masks):
    return jnp.concatenate([block * m for m in masks], axis=0)


def place_diagonal(target, wides, row, pair):
    lane = lane_iota(HD, 128)
    for h in range(GROUP):
        first, second = (v[h * HD : (h + 1) * HD, (h // 2) * 128 : (h // 2) * 128 + 128] for v in wides)
        if h % 2 == 0:
            second = pltpu.roll(second, 64, 1)
        else:
            first = pltpu.roll(first, 64, 1)
        both = jnp.where(lane < 64, first, second).astype(BF16)
        target[row + h * HD : row + (h + 1) * HD, pair * 128 : pair * 128 + 128] = both


def to_column(values, rows):
    lanes = values.shape[1]
    return jnp.sum(jnp.where(row_iota(rows, lanes) == lane_iota(rows, lanes), values, 0.0), axis=-1, keepdims=True)


def to_row(values, lanes):
    rows = values.shape[0]
    return jnp.sum(jnp.where(row_iota(rows, lanes) == lane_iota(rows, lanes), values, 0.0), axis=0, keepdims=True)


def pad_rows(scratch, block):
    scratch[LEN - 4 :, :] = jnp.zeros((ROWS - LEN + 4, scratch.shape[1]), scratch.dtype)
    scratch[0:LEN, :] = block
    return scratch[...]


def split_lanes(slabs, values):
    for j in range(3):
        slabs[j] = values[:, j * 128 : (j + 1) * 128]


def image_rows(slabs, image, images):
    return jnp.concatenate([slabs[j, pl.ds(image, LEN, stride=images), :] for j in range(3)], axis=1)


def call(
    kernel, name, args, in_specs, out_shape, out_specs, scalars=(), grid=(1,), scratch=(), after=(), carry=(), vmem=16, aliases=None
):
    lead = len(scalars) + len(args)
    single = not isinstance(out_shape, tuple)
    shapes, specs = ((out_shape,), (out_specs,)) if single else (out_shape, tuple(out_specs))
    results = len(shapes)
    anywhere = pl.BlockSpec(memory_space=pl.ANY)
    aliases = dict(aliases or {})
    for j in range(len(carry)):
        aliases[lead + len(after) + j] = results + j

    def body(*refs):
        rest = refs[lead + len(after) + len(carry) :]
        kernel(*refs[:lead], *rest[:results], *rest[results + len(carry) :])

    out = pl.pallas_call(
        body,
        out_shape=shapes + tuple(sds(*c.shape, dtype=c.dtype) for c in carry),
        grid_spec=pltpu.PrefetchScalarGridSpec(
            num_scalar_prefetch=len(scalars),
            grid=grid,
            in_specs=list(in_specs) + [anywhere] * (len(after) + len(carry)),
            out_specs=specs + (anywhere,) * len(carry),
            scratch_shapes=list(scratch),
        ),
        input_output_aliases=aliases,
        compiler_params=pltpu.CompilerParams(vmem_limit_bytes=vmem * MIB),
        cost_estimate=pl.CostEstimate(flops=int(COSTS[name] * 1e9) + 1, bytes_accessed=int(COSTS[name] * 3e6) + 1, transcendentals=0),
        name=name,
    )(*scalars, *args, *after, *carry)
    return out[0] if single and not carry else out


def whole(*shape, buffers=None):
    mode = {} if buffers is None else dict(pipeline_mode=pl.Buffered(buffers))
    return pl.BlockSpec(shape, lambda i, *refs: (0,) * len(shape), **mode)


once = functools.partial(whole, buffers=1)


def each(*shape, per=1, shift=0):
    return pl.BlockSpec((per,) + shape, lambda i, *refs: (i + shift,) + (0,) * len(shape))


def sds(*shape, dtype=F32):
    return jax.ShapeDtypeStruct(shape, dtype)


def plan_kernel(place, routes, slots, rows_o, table_o):
    turned = place[0] == 1

    def mine_first(ref):
        v = ref[...]
        half = v.shape[0] // 2
        return jnp.where(turned, jnp.concatenate([v[half:], v[:half]], axis=0), v)

    route, slot = mine_first(routes), mine_first(slots)
    images = route.shape[0]
    key = jnp.where(slot >= 0, route * CAP + slot, -1)
    rows_o[...] = jnp.full(rows_o.shape, -1, jnp.int32)
    for i in range(images):
        rows_o[i, 0:1, 0:LEN] = key[i : i + 1]
        rows_o[i, 1:2, 0:LEN] = route[i : i + 1]
    lane = lane_iota(images, 128)
    table = jnp.zeros((images, 128), jnp.int32)
    slot_f = slot.astype(F32)
    for e in range(8):
        mine = (slot >= 0) & (route == e)
        low = jnp.min(jnp.where(mine, slot_f, float(CAP)), axis=-1, keepdims=True).astype(jnp.int32)
        high = jnp.max(jnp.where(mine, slot_f + 1.0, 0.0), axis=-1, keepdims=True).astype(jnp.int32)
        for n, (step, mask) in enumerate(((OUT_STEP, -8), (BACK_STEP, -16))):
            start = jnp.minimum(low & mask, CAP - step)
            passes = jnp.zeros_like(start)
            for k in range(-(-CAP // step) + 1):
                passes = passes + jnp.where(high - start > k * step, 1, 0)
            table = jnp.where(lane == 16 * n + e, start, table)
            table = jnp.where(lane == 16 * n + 8 + e, passes, table)
            table = jnp.where((lane == 32 + n) & (passes > 1), 1, table)
    table_o[...] = table


def plan(place, routes, slots):
    images = routes.shape[0]
    return call(
        plan_kernel, "plan", (routes, slots), [whole(*routes.shape)] * 2,
        (sds(images, 8, ROWS, dtype=jnp.int32), sds(images, 128, dtype=jnp.int32)),
        (whole(images, 8, ROWS), whole(images, 128)), scalars=(place,),
    )


def pack_kernel(proj, out, table, biases, o):
    rows = proj.shape[0]
    o[0:rows] = proj[...].astype(F32)
    o[rows:384] = out[...].astype(F32)
    o[384:392] = jnp.zeros((8, 384), F32)
    o[384:387, 0:REL] = table[...]
    o[387:389, 0 : biases.shape[1]] = biases[...]


def pack(proj, out, table, biases):
    args = (proj, out, table, biases)
    return call(pack_kernel, "pack", args, [once(*a.shape) for a in args], sds(392, 384), whole(392, 384))


def bias_kernel(place, sa, sb, sc, sd, params, hot, table_o, vecs_o, col_o, shards):
    for m, ref in enumerate((sa, sb, sc, sd)):
        shards[m ^ place[1]] = ref[...]
    heads = jnp.concatenate([shards[k][0:3, 0:256] for k in range(4)] + [jnp.zeros((4, 256), F32)], axis=0)
    high = heads.astype(BF16)
    mid = (heads - high.astype(F32)).astype(BF16)
    low = (heads - high.astype(F32) - mid.astype(F32)).astype(BF16)
    table_o[...] = dot(high, hot[...]) + dot(mid, hot[...]) + dot(low, hot[...])
    query = jnp.concatenate([shards[k][3:4, 0:96] for k in range(4)], axis=1)
    value = jnp.concatenate([shards[k][4:5, 0:96] for k in range(4)], axis=1)
    vecs_o[0:5] = params[0:5]
    vecs_o[5:6] = query
    vecs_o[6:7] = value
    vecs_o[7:8] = value
    col_o[...] = jnp.broadcast_to(to_column(value, 384), (384, 128))


def bias_tables(place, shares, params, hot):
    return call(
        bias_kernel, "bias_tables", (*shares, params, hot), [pl.BlockSpec((8, 384), lambda i, p: (48, 0))] * 4 + [once(8, 384), once(256, 4096)],
        (sds(16, 4096), sds(8, 384), sds(384, 128)), (whole(16, 4096), whole(8, 384), whole(384, 128)),
        scalars=(place,), scratch=[pltpu.VMEM((4, 8, 384), F32)],
    )


def offset_kernel(sums, hot, o):
    v = sums[...]
    high = v.astype(BF16)
    mid = (v - high.astype(F32)).astype(BF16)
    low = (v - high.astype(F32) - mid.astype(F32)).astype(BF16)
    o[...] = dot(high, hot[...], NT) + dot(mid, hot[...], NT) + dot(low, hot[...], NT)


def offset_sums(sums, hot):
    heads = sums.shape[0]
    return call(
        offset_kernel, "offset_sums", (sums, hot), [whole(*sums.shape), whole(*hot.shape)],
        sds(heads, 256), whole(heads, 256),
    )


def attention_kernel(
    place, patches, rows, wa, wb, wc, wd, table, mask, perm, perm_t, vecs, vcol, router_t,
    win_o, qkv_o, kt_o, att_o, mixt_o, x_o, h1_o, low2_o, gate_o, w_o, wt_o, wo_o, wot_o,
    block, pad, vt, bias,
):
    per = win_o.shape[0]
    images = 2 * per * pl.num_programs(0)

    @pl.when(pl.program_id(0) == 0)
    def _():
        split_lanes(block, patches[...].astype(F32))
        for m, ref in enumerate((wa, wb, wc, wd)):
            to = (m ^ place[1]) * 96
            for c in range(3):
                wt_o[pl.ds(pl.multiple_of(c * 384 + to, 32), 96), :] = ref[c * 96 : (c + 1) * 96, :].astype(BF16)
            wo_o[pl.ds(pl.multiple_of(to, 32), 96), :] = ref[288:384, :].astype(BF16)
        for c in range(3):
            w_o[:, c * 384 : (c + 1) * 384] = wt_o[c * 384 : (c + 1) * 384, :].T
        wot_o[...] = wo_o[...].T
        for w in range(4):
            for g in range(3):
                bias[w, g] = table[g] + mask[w]

    masks = head_masks()
    none = jnp.zeros((WROWS, 256), BF16)
    for n in range(per):
        at = place[0] * (images // 2) + pl.program_id(0) * per + n
        x = pad_rows(pad.at[n], image_rows(block, at, images))
        x_o[n] = x.astype(BF16)
        xhat, _ = layer_norm(x)
        low1 = (xhat * vecs[0:1] + vecs[1:2]).astype(BF16)
        win = dot(perm[...], low1).astype(BF16)
        win_o[n] = win
        packed = dot(win, w_o[...])
        qkv_o[n, :, 0:384] = (packed[:, 0:384] + vecs[5:6]).astype(BF16)
        qkv_o[n, :, 384:768] = packed[:, 384:768].astype(BF16)
        qkv_o[n, :, 768:1152] = (packed[:, 768:1152] + vecs[6:7]).astype(BF16)
        kt_o[n] = dot(wt_o[384:768, :], win, NT).astype(BF16)
        vt[n] = (dot(wt_o[768:1152, :], win, NT) + vcol[:, 0:1]).astype(BF16)
        for pair in range(2):
            for g in range(3):
                lanes = lambda c: slice(c * 384 + g * 128, c * 384 + g * 128 + 128)
                v4 = vt[n, g * 128 : (g + 1) * 128, pair * 128 : (pair + 1) * 128]
                wides = []
                for w in (2 * pair, 2 * pair + 1):
                    rs = slice(w * WROWS, (w + 1) * WROWS)
                    qs = spread(qkv_o[n, rs, lanes(0)], masks)
                    s = dot(qkv_o[n, rs, lanes(1)], qs, NT) * SCALE + bias[w, g]
                    e = jnp.exp(s - jnp.max(s, axis=0, keepdims=True))
                    low = (e * (1.0 / jnp.sum(e, axis=0, keepdims=True))).astype(BF16)
                    att_o[n, rs, g * 256 : (g + 1) * 256] = low
                    wides.append(dot(v4, jnp.concatenate([low, none] if w % 2 == 0 else [none, low], axis=0)))
                place_diagonal(mixt_o.at[n], wides, g * 128, pair)
        mixed = dot(perm_t[...], mixt_o[n], NT).astype(BF16)
        h1 = x + (dot(mixed, wo_o[...]) + vecs[2:3])
        h1_o[n] = h1
        xhat2, _ = layer_norm(h1)
        low2 = (xhat2 * vecs[3:4] + vecs[4:5]).astype(BF16)
        low2_o[n] = low2.astype(F32)
        logits = dot(router_t[...], low2, NT)[0:8]
        ex = jnp.exp(logits - jnp.max(logits, axis=0, keepdims=True))
        probs = ex / jnp.sum(ex, axis=0, keepdims=True)
        gate = jnp.sum(jnp.where(row_iota(8, ROWS) == rows[n, 1:2, :], probs, 0.0), axis=0, keepdims=True)
        hi = gate.astype(BF16).astype(F32)
        mid = (gate - hi).astype(BF16).astype(F32)
        gate_o[n, 0:1] = hi
        gate_o[n, 1:2] = mid
        gate_o[n, 2:3] = (gate - hi - mid).astype(BF16).astype(F32)
        gate_o[n, 3:8] = jnp.zeros((5, ROWS), F32)
        gate_o[n, 8:16] = probs


def attention_forward(place, patches, rows, ws, table, mask, perm, perm_t, vecs, vcol, router_t, images, after):
    per = 2
    bf = functools.partial(sds, dtype=BF16)
    out = functools.partial(each, per=per)
    return call(
        attention_kernel, "attention_forward",
        (patches, rows, *ws, table, mask, perm, perm_t, vecs, vcol, router_t),
        [once(*patches.shape), out(8, ROWS)] + [once(392, 384)] * 4
        + [once(*a.shape) for a in (table, mask, perm, perm_t, vecs, vcol, router_t)],
        (
            bf(images, 256, 384), bf(images, 256, 1152), bf(images, 384, 256), bf(images, 256, 768),
            bf(images, 384, 256), bf(images, ROWS, 384), sds(images, ROWS, 384), sds(images, ROWS, 384),
            sds(images, 16, ROWS), bf(384, 1152), bf(1152, 384), bf(384, 384), bf(384, 384),
        ),
        (
            out(256, 384), out(256, 1152), out(384, 256), out(256, 768), out(384, 256), out(ROWS, 384),
            out(ROWS, 384), out(ROWS, 384), out(16, ROWS),
            whole(384, 1152), whole(1152, 384), whole(384, 384), whole(384, 384),
        ),
        scalars=(place,), grid=(images // per,),
        scratch=[
            pltpu.VMEM((3, patches.shape[0], 128), F32),
            pltpu.VMEM((per, ROWS, 384), F32),
            pltpu.VMEM((per, 384, 256), BF16),
            pltpu.VMEM((4, 3, WROWS, 256), F32),
        ],
        after=after,
        vmem=60,
    )


def hits(keys, expert, first, base, step):
    code = row_iota(step, keys.shape[1]) + (expert * CAP + base)
    return jnp.where((code == keys) & (code >= expert * CAP + first), 1.0, 0.0).astype(BF16)


def to_slots(i, table, keys, tile, gates, acc, acc_gate):
    experts, step = acc.shape[0], OUT_STEP

    def store(e, base, moved, gated):
        at = pl.ds(pl.multiple_of(base, 8), step)
        acc[e, at, :] = acc[e, at, :] + moved
        if gates is not None:
            acc_gate[e, at, :] = acc_gate[e, at, :] + gated

    firsts = [table[i, e] for e in range(experts)]
    hit = jnp.concatenate([hits(keys, e, firsts[e], firsts[e], step) for e in range(experts)], axis=0)
    moved = dot(hit, tile)
    gated = None if gates is None else dot(hit, gates, NT)
    for e in range(experts):
        part = slice(e * step, (e + 1) * step)
        store(e, firsts[e], moved[part], None if gates is None else gated[part])

    @pl.when(table[i, 32] > 0)
    def _():
        def expert(e, _):
            def more(r, _):
                first = table[i, e] + r * step
                base = jnp.minimum(first, CAP - step)
                extra = hits(keys, e, first, base, step)
                store(e, base, dot(extra, tile), None if gates is None else dot(extra, gates, NT))
                return 0

            return lax.fori_loop(1, table[i, 8 + e], more, 0)

        lax.fori_loop(0, experts, expert, 0)


def cotangent_kernel(place, table, rows, cot, slots_o, tokens_o, block, acc):
    i = pl.program_id(0)
    per = tokens_o.shape[0]
    images = pl.num_programs(0) * per

    @pl.when(i == 0)
    def _():
        split_lanes(block, cot[...].astype(F32))
        acc[...] = jnp.zeros_like(acc)

    for n in range(per):
        at = lax.rem(i * per + n + place[0] * (images // 2), images)
        tokens_o[n] = jnp.zeros((ROWS, 384), BF16)
        tile = image_rows(block, at, images).astype(BF16)
        tokens_o[n, 0:LEN, :] = tile
        to_slots(i * per + n, table, rows[n, 0:1, 0:LEN], tile, None, acc, None)

    @pl.when(i == pl.num_programs(0) - 1)
    def _():
        slots_o[...] = acc[...].astype(BF16)


def dispatch_cotangent(place, table, rows, cot, experts, after):
    images = rows.shape[0]
    return call(
        cotangent_kernel, "dispatch_cotangent", (rows, cot), [each(8, ROWS, per=4), once(*cot.shape)],
        (sds(experts, CAP, 384, dtype=BF16), sds(images, ROWS, 384, dtype=BF16)),
        (whole(experts, CAP, 384), each(ROWS, 384, per=4)), scalars=(place, table), grid=(images // 4,),
        scratch=[pltpu.VMEM((3, cot.shape[0], 128), F32), pltpu.VMEM((experts, CAP, 384), F32)], after=after, vmem=28,
    )


def low2_kernel(first, offset, table, rows, data, gates, *refs):
    *before, slots_o, gate_o, acc = refs
    i = pl.program_id(0)
    per = data.shape[0]

    @pl.when(i == 0)
    def _():
        if first:
            acc[...] = jnp.zeros_like(acc)
            gate_o[...] = jnp.zeros_like(gate_o)
        else:
            acc[...] = before[0][...].astype(F32)
            gate_o[...] = before[1][...]

    for n in range(per):
        to_slots(
            offset + i * per + n, table, rows[n, 0:1, :], data[n].astype(BF16), gates[n].astype(BF16), acc, gate_o
        )

    @pl.when(i == pl.num_programs(0) - 1)
    def _():
        slots_o[...] = acc[...].astype(BF16)


def dispatch_low2(table, rows, data, gates, experts, before=(), after=()):
    images = data.shape[0]
    offset = images if before else 0
    return call(
        functools.partial(low2_kernel, not before, offset), "dispatch_low2", (rows, data, gates, *before),
        [each(8, ROWS, per=4, shift=offset // 4), each(ROWS, 384, per=4), each(16, ROWS, per=4)]
        + [once(*a.shape) for a in before],
        (sds(experts, CAP, 384, dtype=BF16), sds(experts, CAP, 16)),
        (whole(experts, CAP, 384), whole(experts, CAP, 16)), scalars=(table,), grid=(images // 4,),
        scratch=[pltpu.VMEM((experts, CAP, 384), F32)], after=after, vmem=32,
    )


def expert_kernel(place, buf, gates, gbuf, up, down, up_b, down_b, unused, gu_o, gd_o, rg_o, gdb_o):
    x = buf[0]
    gate = gates[0][:, 0:1] + gates[0][:, 1:2] + gates[0][:, 2:3]
    g = (gate * gbuf[0].astype(F32)).astype(BF16)
    gdb_o[0] = jnp.broadcast_to(jnp.sum(g.astype(F32), axis=0, keepdims=True), (8, 384))
    w_up, w_down = up[0], down[0]
    hp = dot(x, w_up) + up_b[0]
    c0 = np.float32(np.sqrt(2 / np.pi))
    th = jnp.tanh(c0 * (hp + 0.044715 * (hp * hp * hp)))
    act = (hp * (0.5 * (1.0 + th))).astype(BF16)
    slope = 0.5 * (1.0 + th) + (0.5 * hp) * (1.0 - th * th) * (c0 * (1.0 + (3 * 0.044715) * (hp * hp)))
    lead = jnp.where(place[1] == 0, 1.0, 0.0)
    rg_o[:, 0:384] = (dot(act, w_down) + lead * down_b[0]).astype(BF16)
    gd_o[...] = dot(act, g, TN)
    gp = (dot(g, w_down, NT) * slope).astype(BF16)
    gu_o[0:384] = dot(x, gp, TN)
    gu_o[384:392] = jnp.broadcast_to(jnp.sum(gp.astype(F32), axis=0, keepdims=True), (8, 384))
    rg_o[:, 384:768] = dot(gp, w_up, NT).astype(BF16)


def expert_pass(step, place, buf, gates, gbuf, up, down, up_b, down_b, sums, after):
    at = lambda *shape: pl.BlockSpec((1,) + shape, lambda i, p: (p[2 + step],) + (0,) * len(shape))
    return call(
        expert_kernel, "expert_pass", (buf, gates, gbuf, up, down, up_b, down_b, sums),
        [at(CAP, 384), at(CAP, 16), at(CAP, 384), at(384, 384), at(384, 384), at(1, 384), at(1, 384)]
        + [pl.BlockSpec(memory_space=pl.ANY)],
        (sds(392, 384), sds(384, 384), sds(CAP, 768, dtype=BF16), sds(*sums.shape)),
        (whole(392, 384), whole(384, 384), whole(CAP, 768), pl.BlockSpec((1, 8, 384), lambda i, p: (step, 0, 0))),
        scalars=(place,), after=after, aliases={8: 3},
    )


def back_to_tokens(i, place, table, key_row, cot, refs, windows, back):
    experts, step = len(refs), BACK_STEP
    keys = to_column(key_row.astype(F32), ROWS).astype(jnp.int32)
    lane = lane_iota(1, experts * step)
    code = jnp.zeros((1, experts * step), jnp.int32)
    for s in range(experts):
        e = place[2 + s]
        first = table[i, 16 + e]
        windows[s * step : (s + 1) * step, :] = refs[s][pl.ds(pl.multiple_of(first, 16), step), :]
        code = jnp.where(lane >= s * step, e * CAP + first + lane - s * step, code)
    back[...] = dot(jnp.where(code == keys, 1.0, 0.0).astype(BF16), windows[...])

    @pl.when(table[i, 33] > 0)
    def _():
        narrow = lane_iota(1, step)
        for s in range(experts):
            e = place[2 + s]

            def more(r, _):
                first = table[i, 16 + e] + r * step
                base = jnp.minimum(first, CAP - step)
                slot = narrow + base
                hit = (e * CAP + slot == keys) & (slot >= first)
                block = refs[s][pl.ds(pl.multiple_of(base, 16), step), :]
                back[...] = back[...] + dot(jnp.where(hit, 1.0, 0.0).astype(BF16), block)
                return 0

            lax.fori_loop(1, table[i, 24 + e], more, 0)

    tok, gl = back[:, 0:384], back[:, 384:768]
    dots = jnp.sum(tok * cot.astype(F32), axis=-1, keepdims=True)
    mark = jnp.concatenate([to_row(dots, ROWS), jnp.zeros((1, 384 - ROWS), F32)], axis=1)
    return jnp.where(row_iota(ROWS, 384) == LEN + 4, mark, gl), tok


def combine_far_kernel(offset, place, table, rows, cot, r0, r1, r2, r3, r4, r5, r6, r7, gl_o, tok_o, windows, back):
    refs = (r0, r1, r2, r3, r4, r5, r6, r7)
    per = gl_o.shape[0]
    for n in range(per):
        at = pl.program_id(0) * per + n + offset
        gl_o[n], tok_o[n] = back_to_tokens(at, place, table, rows[n, 0:1, :], cot[n], refs, windows.at[n], back.at[n])


def combine_scratch(experts):
    return [pltpu.VMEM((2, experts * BACK_STEP, 768), BF16), pltpu.VMEM((2, ROWS, 768), F32)]


def combine_far(place, table, rows, cot, results, after):
    images = rows.shape[0]
    half = images // 2
    return call(
        functools.partial(combine_far_kernel, half), "combine_far", (rows, cot, *results),
        [each(8, ROWS, per=2, shift=half // 2), each(ROWS, 384, per=2, shift=half // 2)] + [once(CAP, 768)] * len(results),
        (sds(half, ROWS, 384),) * 2, (each(ROWS, 384, per=2),) * 2, scalars=(place, table), grid=(half // 2,),
        scratch=combine_scratch(len(results)), after=after, vmem=20,
    )


def combine_own_kernel(
    place, table, rows, cot, r0, r1, r2, r3, r4, r5, r6, r7, gl_got, tok_got, g0, g1, g2, g3, tok_o, windows, back
):
    i = pl.program_id(0)
    refs = (r0, r1, r2, r3, r4, r5, r6, r7)
    parts = []
    for n in range(2):
        gl, tok = back_to_tokens(2 * i + n, place, table, rows[n, 0:1, :], cot[n], refs, windows.at[n], back.at[n])
        tok_o[n] = tok + tok_got[n]
        parts.append(gl + gl_got[n])
    for c, ref in enumerate((g0, g1, g2, g3)):

        @pl.when(i == c)
        def _():
            ref[0], ref[1] = parts


def combine_own(place, table, rows, cot, results, gl_got, tok_got, after):
    half = gl_got.shape[0]
    return call(
        combine_own_kernel, "combine_own", (rows, cot, *results, gl_got, tok_got),
        [each(8, ROWS, per=2), each(ROWS, 384, per=2)] + [once(CAP, 768)] * len(results) + [each(ROWS, 384, per=2)] * 2,
        (sds(2, ROWS, 384),) * 4 + (sds(half, ROWS, 384),), (whole(2, ROWS, 384),) * 4 + (each(ROWS, 384, per=2),),
        scalars=(place, table), grid=(half // 2,), scratch=combine_scratch(len(results)), after=after, vmem=24,
    )


def backward_kernel(
    first, offset, images, place, count, own, other, cot, rows, h1, low2_r, gate_r, mixt, win_r, qkv, kt, att, x_r,
    w, wt, wot, perm, perm_t, vecs, router_t,
    dw_i, dwo_i, dtb_i, dv_i, dr_i,
    gp_o, dw_o, dwo_o, dtb_o, dv_o, dr_o,
    dqt, dkv,
):
    for src, dst in ((dw_i, dw_o), (dwo_i, dwo_o), (dtb_i, dtb_o), (dv_i, dv_o), (dr_i, dr_o)):
        dst[...] = jnp.zeros(dst.shape, F32) if first else src[...]
    masks = head_masks()
    none = jnp.zeros((WROWS, 256), BF16)
    ones = jnp.ones((16, 256), BF16)

    def add(r, v):
        dv_o[r : r + 1, :] = dv_o[r : r + 1, :] + v

    for n in range(own.shape[0]):
        total = own[n] + other[n]
        gl = jnp.where(row_iota(ROWS, 384) < LEN, total, 0.0)
        gg = total[LEN + 4 : LEN + 5, 0:ROWS]
        at = place[0] * images + offset + n
        grad = cot[n].astype(F32) * jnp.where(at < count[0], 1.0, 0.0)
        probs = gate_r[n, 8:16]
        hot = jnp.where(row_iota(8, ROWS) == rows[n, 1:2, :], 1.0, 0.0)
        gate = jnp.sum(probs * hot, axis=0, keepdims=True)
        glog = jnp.concatenate([probs * (hot - gate) * gg, jnp.zeros((8, ROWS), F32)], axis=0).astype(BF16)
        low2 = low2_r[n].astype(BF16)
        dr_o[...] += dot(glog, low2)
        g2 = gl + dot(glog, router_t[...], TN)
        xhat2, inv2 = layer_norm(h1[n])
        add(3, jnp.sum(g2 * xhat2, axis=0, keepdims=True))
        add(4, jnp.sum(g2, axis=0, keepdims=True))
        gh1 = grad + norm_back(g2 * vecs[3:4], xhat2, inv2)
        gattn = gh1.astype(BF16)
        gwin = dot(perm[...], gattn).astype(BF16)
        add(2, dot(ones, gwin)[0:1])
        dwo_o[...] += dot(mixt[n], gwin)
        gmw = dot(gwin, wot[...]).astype(BF16)
        for g in range(3):
            lanes = lambda c: slice(c * 384 + g * 128, c * 384 + g * 128 + 128)
            table_sum = dtb_o[g]
            for pair in range(2):
                k4 = kt[n, g * 128 : (g + 1) * 128, pair * 128 : (pair + 1) * 128]
                wides = []
                for wi in (2 * pair, 2 * pair + 1):
                    rs = slice(wi * WROWS, (wi + 1) * WROWS)
                    qs = spread(qkv[n, rs, lanes(0)], masks)
                    dms = spread(gmw[rs, g * 128 : (g + 1) * 128], masks)
                    a_low = att[n, rs, g * 256 : (g + 1) * 256]
                    a = a_low.astype(F32)
                    da = dot(qkv[n, rs, lanes(2)], dms, NT)
                    ds = (a * (da - jnp.sum(da * a, axis=0, keepdims=True))).astype(BF16)
                    table_sum = table_sum + ds.astype(F32)
                    dkv[n, rs, g * 128 : (g + 1) * 128] = (SCALE * dot(ds, qs)).astype(BF16)
                    dkv[n, rs, 384 + g * 128 : 512 + g * 128] = dot(a_low, dms).astype(BF16)
                    wides.append(SCALE * dot(k4, jnp.concatenate([ds, none] if wi % 2 == 0 else [none, ds], axis=0)))
                place_diagonal(dqt.at[n], wides, g * 128, pair)
            dtb_o[g] = table_sum
        win = win_r[n]
        dw_o[0:384] += dot(dqt[n], win)
        dw_o[384:1152] += dot(dkv[n], win, TN)
        add(5, dot(ones, dqt[n], NT)[0:1])
        add(6, dot(ones, dkv[n, :, 384:768])[0:1])
        part = dot(dkv[n], wt[384:1152, :])
        hi = part.astype(BF16)
        lo = (part - hi.astype(F32)).astype(BF16)
        part_t = dot(w[:, 0:384], dqt[n])
        hi_t = part_t.astype(BF16)
        lo_t = (part_t - hi_t.astype(F32)).astype(BF16)
        pt = perm_t[...]
        gl1 = dot(pt, hi) + dot(pt, lo) + dot(pt, hi_t, NT) + dot(pt, lo_t, NT)
        xhat1, inv1 = layer_norm(x_r[n].astype(F32))
        add(0, jnp.sum(gl1 * xhat1, axis=0, keepdims=True))
        add(1, jnp.sum(gl1, axis=0, keepdims=True))
        gp_o[n] = gh1 + norm_back(gl1 * vecs[0:1], xhat1, inv1)


def attention_backward(first, c, place, count, own, other, cot, rows, saved, w, wt, wot, consts, acc, after, carry=()):
    per = own.shape[0]
    h1, low2, gates, mixt, win, qkv, kt, att, x = saved
    mine = functools.partial(each, per=per, shift=c)
    accs = [once(*a.shape) for a in acc]
    args = (own, other, cot, rows, h1, low2, gates, mixt, win, qkv, kt, att, x, w, wt, wot, *consts, *acc)
    specs = (
        [each(ROWS, 384, per=per)] * 2
        + [mine(*a.shape[1:]) for a in (cot, rows, h1, low2, gates, mixt, win, qkv, kt, att, x)]
        + [once(*a.shape) for a in (w, wt, wot, *consts)]
        + accs
    )
    lead = 2 + len(args) - len(acc)
    return call(
        functools.partial(backward_kernel, first, c * per, h1.shape[0]), "attention_backward", args, specs,
        (sds(per, ROWS, 384),) + tuple(sds(*a.shape) for a in acc), (each(ROWS, 384, per=per),) + tuple(whole(*a.shape) for a in acc),
        scalars=(place, count), scratch=[pltpu.VMEM((per, 384, 256), BF16), pltpu.VMEM((per, 256, 768), BF16)],
        after=after, carry=carry, vmem=32, aliases={lead + j: 1 + j for j in range(len(acc))},
    )


def add_arrays(a, b, blocks, after=(), carry=()):
    def kernel(x, y, o):
        o[...] = x[...] + y[...]

    rows = a.shape[0] // blocks
    spec = pl.BlockSpec((rows,) + a.shape[1:], lambda i: (i,) + (0,) * (a.ndim - 1))
    return call(kernel, "add", (a, b), [spec, spec], sds(*a.shape), spec, grid=(blocks,), after=after, carry=carry)


def hand_on(after, carry):
    def kernel(o):
        o[...] = jnp.zeros(o.shape, F32)

    return call(kernel, "hand_on", (), (), (sds(8, 128),), (whole(8, 128),), after=after, carry=carry)[1:]


def block_out_kernel(place, count, h1, gates, own, other, rows, o):
    per = o.shape[0]
    for n in range(per):
        i = pl.program_id(0) * per + n
        gate = gates[n, 0:1] + gates[n, 1:2] + gates[n, 2:3]
        weight = to_column(jnp.where(rows[n, 0:1] >= 0, gate, 0.0), ROWS)
        keep = jnp.where(place[0] * pl.num_programs(0) * per + i < count[0], 1.0, 0.0)
        value = keep * (h1[n] + weight * (own[n] + other[n]))
        o[n] = value.astype(BF16).astype(F32)


def block_out_pass(place, count, h1, gates, own, other, rows, after):
    images = h1.shape[0]
    return call(
        block_out_kernel, "block_out", (h1, gates, own, other, rows),
        [each(ROWS, 384, per=2), each(16, ROWS, per=2), each(ROWS, 384, per=2), each(ROWS, 384, per=2), each(8, ROWS, per=2)],
        sds(images, ROWS, 384), each(ROWS, 384, per=2), scalars=(place, count), grid=(images // 2,), after=after,
    )


def join_pass(place, own, other, dtype, after=()):
    images = 2 * sum(a.shape[0] for a in own)
    slab = lambda *lead: pl.BlockSpec(lead + (128,), lambda j, p: (0,) * len(lead) + (j,))

    def kernel(p, *refs):
        out = refs[len(own) + len(other)]
        wide = out if dtype == F32 else refs[-1]
        for side, group in ((0, refs[: len(own)]), (1, refs[len(own) : len(own) + len(other)])):
            at = (p[0] ^ side) * (images // 2)
            for ref in group:
                for n in range(ref.shape[0]):
                    wide[pl.ds(at, LEN, stride=images), :] = ref[n, 0:LEN, :]
                    at = at + 1
        if dtype != F32:
            out[...] = wide[...].astype(dtype)

    return call(
        kernel, "join", (*own, *other), [slab(a.shape[0], ROWS) for a in (*own, *other)],
        sds(LEN * images, 384, dtype=dtype), slab(LEN * images), scalars=(place,), grid=(3,),
        scratch=[] if dtype == F32 else [pltpu.VMEM((LEN * images, 128), F32)], after=after,
    )


def share_kernel(place, dw, dwo, by_offset, vec, router, downs, mine, far):
    for flip, out in ((0, mine), (1, far)):
        t = place[1] ^ flip
        at = pl.multiple_of(t * 96, 32)
        for c in range(3):
            out[c * 96 : (c + 1) * 96, :] = dw[pl.ds(pl.multiple_of(c * 384 + at, 32), 96), :]
        out[288:384, :] = dwo[pl.ds(at, 96), :]
        out[384:448, :] = jnp.zeros((64, 384), F32)
        for k in range(4):

            @pl.when(t == k)
            def _():
                out[384:387, 0:256] = by_offset[3 * k : 3 * k + 3, :]
                out[387:388, 0:96] = vec[5:6, 96 * k : 96 * k + 96]
                out[388:389, 0:96] = vec[6:7, 96 * k : 96 * k + 96]

        out[392:397, :] = vec[0:5, :]
        out[400:408, :] = router[0:8, :]
    for s in range(downs.shape[0]):
        mine[pl.ds(408 + place[2 + s], 1), :] = downs[s, 0:1, :]


def share_pass(place, dw, dwo, by_offset, vec, router, downs):
    args = (dw, dwo, by_offset, vec, router, downs)
    return call(
        share_kernel, "share", args, [once(*a.shape) for a in args],
        (sds(448, 384), sds(448, 384)), (whole(448, 384), whole(448, 384)), scalars=(place,),
    )


def halve_pass(own, got, bit, place, after=()):
    half = own.shape[0] // 2

    def kernel(p, a, b, send, keep):
        up = p[bit] != 0
        low = a[:half] + b[:half]
        high = a[half:] + b[half:]
        send[...] = jnp.where(up, low, high)
        keep[...] = jnp.where(up, high, low)

    return call(
        kernel, "halve", (own, got), [whole(*own.shape)] * 2, (sds(half, 384),) * 2, (whole(half, 384),) * 2,
        scalars=(place,), after=after,
    )


def double_pass(own, got, bit, place, after=()):
    rows = own.shape[0]

    def kernel(p, a, b, o):
        up = p[bit] != 0
        o[:rows] = jnp.where(up, b[...], a[...])
        o[rows:] = jnp.where(up, a[...], b[...])

    return call(
        kernel, "double", (own, got), [whole(*own.shape)] * 2, sds(2 * rows, 384), whole(2 * rows, 384),
        scalars=(place,), after=after,
    )


def gather_pass(place, ups, downs, shift, targets, after=()):
    count, experts = len(ups), 8

    def kernel(p, *refs):
        up_o, down_o, bias_o = refs[-3:]
        for k in range(count):

            @pl.when(pl.program_id(0) == k)
            def _():
                up_o[0] = refs[k][0:384, :]
                down_o[0] = refs[count + k][...]
                bias_o[0] = refs[k][384:392, :]

    at = lambda *shape: pl.BlockSpec((1,) + shape, lambda i, p: (p[2 + lax.rem(i + shift + experts - 1, experts)], 0, 0))
    anywhere = pl.BlockSpec(memory_space=pl.ANY)
    return call(
        kernel, "gather", (*ups, *downs, *targets),
        [once(392, 384)] * count + [once(384, 384)] * count + [anywhere] * len(targets),
        (sds(experts, 384, 384), sds(experts, 384, 384), sds(experts, 8, 384)), (at(384, 384), at(384, 384), at(8, 384)),
        scalars=(place,), grid=(count,), after=after, aliases={1 + 2 * count + j: j for j in range(len(targets))}, vmem=20,
    )


def swap_core(x):
    return lax.ppermute(x, "tensor", [(0, 1), (1, 0), (2, 3), (3, 2)])


def swap_chip(x):
    return lax.ppermute(x, "tensor", [(0, 2), (2, 0), (1, 3), (3, 1)])


def shape_back(values, length, images):
    return values.reshape(length, images, values.shape[-1]).transpose(1, 0, 2)


def on_device(
    n_dp, patches, image_count, routes, slot_index, norm1_gain, norm1_bias, input_proj, query_value_bias,
    position_bias, output_proj, output_bias, norm2_gain, norm2_bias, router_weight, up_weight, up_bias,
    down_weight, down_bias, cotangent,
):
    images, length, width = patches.shape
    half = images // 2
    experts = up_weight.shape[0]
    tensor = lax.axis_index("tensor")
    core = tensor % 2
    ring = n_dp == experts
    cycle = [0, 2, 4, 6, 7, 5, 3, 1]
    where = {d: i for i, d in enumerate(cycle)}
    dp = lax.axis_index("dp")
    spots = np.zeros((4 * n_dp, 16), np.int32)
    for d in range(n_dp):
        for t in range(4):
            rank = 0
            if ring:
                rank = where[d] if t % 2 == 0 else (n_dp - where[d]) % n_dp
            spots[4 * d + t, :13] = [t % 2, t] + [(rank - s) % experts for s in range(experts)] + [d >> b & 1 for b in range(3)]
    place = lax.dynamic_slice(jnp.asarray(spots), (4 * dp + tensor, 0), (1, 16)).reshape(16)
    if ring:
        pairs = []
        for d in range(n_dp):
            for t in range(4):
                to = cycle[(where[d] + (1 if t % 2 == 0 else -1)) % n_dp]
                pairs.append((d * 4 + t, to * 4 + t))
    onward = lambda v: lax.ppermute(v, ("dp", "tensor"), pairs)
    swap_dp = lambda v, bit: lax.ppermute(v, "dp", [(d, d ^ bit) for d in range(n_dp)])
    perm_np, mask_np, relative_np = window_tables()
    perm = jnp.asarray(perm_np, BF16)
    perm_t = jnp.asarray(perm_np.T, BF16)
    mask = jnp.asarray(mask_np)
    hot_np = np.arange(256)[:, None] == relative_np.reshape(1, -1)
    hot = jnp.asarray(hot_np, BF16)

    proj = pack(input_proj.transpose(1, 2, 0).reshape(-1, width), output_proj, position_bias.T, query_value_bias)
    proj_x = swap_chip(proj)
    proj_c = swap_core(proj)
    params = jnp.stack([norm1_gain, norm1_bias, output_bias, norm2_gain, norm2_bias] + [norm1_gain] * 3)
    router_t = jnp.pad(router_weight.T, ((0, 8), (0, 0)))

    rows, table = plan(place, routes, slot_index)
    flat = lambda v: v.transpose(1, 0, 2).reshape(length * images, width)
    gbuf, cot = dispatch_cotangent(place, table, rows, flat(cotangent), experts, ())
    (proj_x,) = hand_on((gbuf,), (proj_x,))
    proj_d = swap_core(proj_x)
    shares = (proj, proj_c, proj_x, proj_d)
    flat_table, vecs, vcol = bias_tables(place, shares, params, hot)
    bias = flat_table[0:12].reshape(3, 4, 64, 64).transpose(0, 2, 1, 3).reshape(3, 64, 256)
    win, qkv, kt, att, mixt, x, h1, low2, gates, w, wt, wo, wot = attention_forward(
        place, flat(patches), rows, shares, bias, mask, perm, perm_t, vecs, vcol, router_t, half, (gbuf,)
    )
    buf, slot_gates = dispatch_low2(table, rows, low2, gates, experts)
    buf, slot_gates = dispatch_low2(table, rows, swap_core(low2), swap_core(gates), experts, (buf, slot_gates))

    results, ups, downs, down_sums = [], [], [], [jnp.zeros((experts, 8, 384), F32)]
    up_b = up_bias.reshape(experts, 1, 384)
    down_b = down_bias.reshape(experts, 1, 384)

    def expert(s, last=None):
        after = () if last is None else (last,)
        gu, gd, rg, gdb = expert_pass(
            s, place, buf, slot_gates, gbuf, up_weight, down_weight, up_b, down_b, down_sums[0], after
        )
        results.append(rg)
        ups.append(gu)
        downs.append(gd)
        down_sums[0] = gdb
        return gdb

    flying, sums = {}, ([], [])
    steps = [0, 0]

    def serve(which, last, carry=(), also=()):
        if not ring:
            return (last, *carry) if carry else last
        steps[which] += 1
        step = steps[which]
        value = flying[which]
        if step < experts:
            value = add_arrays(value, (ups, downs)[which][step], 1 if which == 0 else 2, (last, *also), carry)
            if carry:
                value, *carry = value
        if step >= experts - 1:
            sums[which].append(value)
        if step < 2 * experts - 2:
            flying[which] = onward(value)
        return (value, *carry) if carry else value

    UP, DOWN = 0, 1
    last = expert(0)
    if ring:
        flying = {UP: onward(ups[0]), DOWN: onward(downs[0])}
    last = expert(2, expert(1, last))
    last = serve(UP, last)
    last = expert(3, last)
    last = serve(DOWN, last)
    last = expert(5, expert(4, last))
    last = serve(UP, last)
    last = expert(6, last)
    last = serve(DOWN, last)
    last = expert(7, last)
    gl_far, tok_far = combine_far(place, table, rows, cot, results, (last,))
    last, gl_far, tok_far = serve(UP, gl_far, (gl_far, tok_far))
    gl_got, tok_got = swap_core(gl_far), swap_core(tok_far)
    last = serve(DOWN, last)
    *gl, tok_mine = combine_own(place, table, rows, cot, results, gl_got, tok_got, (last,))
    their = [swap_chip(gl[0])]
    last, gl[1] = serve(UP, tok_mine, (gl[1],))
    their.append(swap_chip(gl[1]))
    last = serve(DOWN, last)
    last, gl[2] = serve(UP, last, (gl[2],), (their[0],))
    their.append(swap_chip(gl[2]))
    last = serve(DOWN, last)
    consts = (perm, perm_t, vecs, router_t)
    saved = (h1, low2, gates, mixt, win, qkv, kt, att, x)
    acc = [
        jnp.zeros((1152, 384), F32), jnp.zeros((384, 384), F32), jnp.zeros((3, 64, 256), F32),
        jnp.zeros((8, 384), F32), jnp.zeros((16, 384), F32),
    ]
    grads = []

    def backward(c, carry):
        gp, *more = attention_backward(
            c == 0, c, place, image_count, gl[c], their[c], cot, rows, saved, w, wt, wot, consts, acc, (last,), carry
        )
        acc[:] = more[:5]
        grads.append(gp)
        return more[5:]

    (gl[3],) = backward(0, (gl[3],))
    their.append(swap_chip(gl[3]))
    last = serve(DOWN, serve(UP, grads[-1]))
    backward(1, ())
    last = serve(DOWN, serve(UP, grads[-1]))
    backward(2, ())
    last = serve(DOWN, serve(UP, grads[-1]))
    (tok_mine,) = backward(3, (tok_mine,))
    tok_their = swap_chip(tok_mine)
    last = serve(DOWN, serve(UP, grads[-1]))
    gp_got = [swap_core(v) for v in grads]

    dw, dwo, dtb, dvec, drouter = acc
    by_offset = offset_sums(dtb.reshape(3, 64, 4, 64).transpose(0, 2, 1, 3).reshape(12, 4096), hot)
    mine, far = share_pass(place, dw, dwo, by_offset, dvec, drouter, down_sums[0])
    got = swap_core(far)
    if ring:
        for b in range(3):
            send, mine = halve_pass(mine, got, 10 + b, place, (last,))
            got = swap_dp(send, 1 << b)
            last = serve(b % 2, mine)
        total = add_arrays(mine, got, 1, (last,))
        for b in (2, 1, 0):
            got = swap_dp(total, 1 << b)
            last = serve((b + 1) % 2, last)
            total = double_pass(total, got, 10 + b, place, (last,))
    else:
        total = lax.psum(mine + got, "dp")
    out_own = block_out_pass(place, image_count, h1, gates, tok_mine, tok_their, rows, (total,))
    grad_patches = join_pass(place, grads, gp_got, F32, (out_own,))
    block_out = join_pass(place, (out_own,), (swap_core(out_own),), BF16, (grad_patches,))
    if ring:
        while steps[DOWN] < 2 * experts - 2:
            last = serve(UP, last) if steps[UP] <= steps[DOWN] else serve(DOWN, last)
    if ring:
        early = 6
        targets = gather_pass(place, sums[UP][:early], sums[DOWN][:early], 0, (), (grad_patches,))
        grad_up, grad_down, bias8 = gather_pass(
            place, sums[UP][early:], sums[DOWN][early:], early, targets, (block_out,)
        )
        grad_up_bias = bias8[:, 0]
    if not ring:
        everything = lax.psum(jnp.concatenate([jnp.stack(ups), jnp.stack(downs)], axis=1), "dp")
        everything = jnp.take(everything, jnp.asarray([(0 - s) % experts for s in range(experts)]), axis=0)
        grad_up, grad_up_bias, grad_down = everything[:, 0:384], everything[:, 384], everything[:, 392:776]
    block_out, grad_patches = (shape_back(v, length, images) for v in (block_out, grad_patches))
    return (
        block_out,
        grad_patches,
        total[392],
        total[393],
        total[0:288].reshape(3, 96, 384).transpose(2, 0, 1),
        total[387:389, 0:96],
        total[384:387, 0:REL].T,
        total[288:384],
        total[394],
        total[395],
        total[396],
        total[400:408].T,
        grad_up,
        grad_up_bias,
        grad_down,
        total[408:416],
    )


def solution(mesh):
    in_specs = (
        P("dp", None, None), P("dp"), P("dp", None), P("dp", None), P(), P(), P(None, None, "tensor"),
        P(None, "tensor"), P(None, "tensor"), P("tensor", None), P(), P(), P(), P(), P(None, None, "tensor"),
        P(None, "tensor"), P(None, "tensor", None), P(), P("dp", None, None),
    )
    out_specs = (
        P("dp", None, None), P("dp", None, None), P(), P(), P(None, None, "tensor"), P(None, "tensor"),
        P(None, "tensor"), P("tensor", None), P(), P(), P(), P(), P(None, None, "tensor"), P(None, "tensor"),
        P(None, "tensor", None), P(),
    )
    return jax.shard_map(
        functools.partial(on_device, mesh.shape["dp"]),
        mesh=mesh, in_specs=in_specs, out_specs=out_specs, check_vma=False,
    )
```

```python
import functools

import jax
import jax.numpy as jnp
import numpy as np
from jax import lax
from jax.experimental import pallas as pl
from jax.experimental.pallas import tpu as pltpu
from jax.sharding import PartitionSpec as P

HD = 32
WIN = 7
SIDE = 14
SHIFT = 3
CAP = 512
CELLS = WIN * WIN
LEN = SIDE * SIDE
ROWS = 208
WROWS = 64
OUT_STEP = 64
BACK_STEP = 64
REL = (2 * WIN - 1) ** 2
EPS = 1e-05
SCALE = HD**-0.5
GROUP = 4
MIB = 1024 * 1024
COSTS = dict(
    pack=1, plan=1, bias_tables=1.5, offset_sums=2, attention_forward=24, dispatch_cotangent=9, dispatch_low2=4.5, expert_pass=2.4,
    combine_far=4.4, combine_own=6.4, attention_backward=8.5, add=0.1, hand_on=0.1, block_out=4, join=4.8, share=1,
    halve=0.5, double=0.5, gather=5,
)
F32 = jnp.float32
BF16 = jnp.bfloat16
NN = ((1,), (0,))
NT = ((1,), (1,))
TN = ((0,), (0,))


def dot(a, b, dims=NN):
    return lax.dot_general(a, b, (dims, ((), ())), preferred_element_type=F32)


def layer_norm(values):
    center = values - jnp.mean(values, axis=-1, keepdims=True)
    inverse = lax.rsqrt(jnp.mean(center * center, axis=-1, keepdims=True) + EPS)
    return center * inverse, inverse


def norm_back(grad_hat, normed, inverse):
    return inverse * (
        grad_hat
        - jnp.mean(grad_hat, axis=-1, keepdims=True)
        - normed * jnp.mean(grad_hat * normed, axis=-1, keepdims=True)
    )


def window_tables():
    perm = np.zeros((4 * WROWS, ROWS), np.float32)
    label = np.zeros((4, CELLS), np.int32)
    band = lambda v: int(v >= SIDE - WIN) + int(v >= SIDE - SHIFT)
    for w in range(4):
        for a in range(WIN):
            for b in range(WIN):
                r, c = (w // 2) * WIN + a, (w % 2) * WIN + b
                perm[w * WROWS + a * WIN + b, ((r + SHIFT) % SIDE) * SIDE + (c + SHIFT) % SIDE] = 1
                label[w, a * WIN + b] = 3 * band(r) + band(c)
    mask = np.full((4, WROWS, WROWS), -1e30, np.float32)
    mask[:, :CELLS, :] = 0
    same = label[:, :, None] == label[:, None, :]
    mask[:, :CELLS, :CELLS] = np.where(same, 0.0, -100.0)
    cells = np.arange(CELLS)
    rows, cols = cells // WIN, cells % WIN
    rel = (rows[None, :] - rows[:, None] + WIN - 1) * (2 * WIN - 1) + (cols[None, :] - cols[:, None] + WIN - 1)
    relative = np.full((WROWS, WROWS), -1, np.int32)
    relative[:CELLS, :CELLS] = rel
    return perm, np.tile(mask, (1, 1, GROUP)), relative


def lane_iota(rows, cols):
    return lax.broadcasted_iota(jnp.int32, (rows, cols), 1)


def row_iota(rows, cols):
    return lax.broadcasted_iota(jnp.int32, (rows, cols), 0)


def head_masks():
    lane = lane_iota(1, 128) // HD
    return [(lane == h).astype(F32).astype(BF16) for h in range(GROUP)]


def spread(block, masks):
    return jnp.concatenate([block * m for m in masks], axis=0)


def place_diagonal(target, wides, row, pair):
    lane = lane_iota(HD, 128)
    for h in range(GROUP):
        first, second = (v[h * HD : (h + 1) * HD, (h // 2) * 128 : (h // 2) * 128 + 128] for v in wides)
        if h % 2 == 0:
            second = pltpu.roll(second, 64, 1)
        else:
            first = pltpu.roll(first, 64, 1)
        both = jnp.where(lane < 64, first, second).astype(BF16)
        target[row + h * HD : row + (h + 1) * HD, pair * 128 : pair * 128 + 128] = both


def to_column(values, rows):
    lanes = values.shape[1]
    return jnp.sum(jnp.where(row_iota(rows, lanes) == lane_iota(rows, lanes), values, 0.0), axis=-1, keepdims=True)


def to_row(values, lanes):
    rows = values.shape[0]
    return jnp.sum(jnp.where(row_iota(rows, lanes) == lane_iota(rows, lanes), values, 0.0), axis=0, keepdims=True)


def pad_rows(scratch, block):
    scratch[LEN - 4 :, :] = jnp.zeros((ROWS - LEN + 4, scratch.shape[1]), scratch.dtype)
    scratch[0:LEN, :] = block
    return scratch[...]


def split_lanes(slabs, values):
    for j in range(3):
        slabs[j] = values[:, j * 128 : (j + 1) * 128]


def image_rows(slabs, image, images):
    return jnp.concatenate([slabs[j, pl.ds(image, LEN, stride=images), :] for j in range(3)], axis=1)


def call(
    kernel, name, args, in_specs, out_shape, out_specs, scalars=(), grid=(1,), scratch=(), after=(), carry=(), vmem=16, aliases=None
):
    lead = len(scalars) + len(args)
    single = not isinstance(out_shape, tuple)
    shapes, specs = ((out_shape,), (out_specs,)) if single else (out_shape, tuple(out_specs))
    results = len(shapes)
    anywhere = pl.BlockSpec(memory_space=pl.ANY)
    aliases = dict(aliases or {})
    for j in range(len(carry)):
        aliases[lead + len(after) + j] = results + j

    def body(*refs):
        rest = refs[lead + len(after) + len(carry) :]
        kernel(*refs[:lead], *rest[:results], *rest[results + len(carry) :])

    out = pl.pallas_call(
        body,
        out_shape=shapes + tuple(sds(*c.shape, dtype=c.dtype) for c in carry),
        grid_spec=pltpu.PrefetchScalarGridSpec(
            num_scalar_prefetch=len(scalars),
            grid=grid,
            in_specs=list(in_specs) + [anywhere] * (len(after) + len(carry)),
            out_specs=specs + (anywhere,) * len(carry),
            scratch_shapes=list(scratch),
        ),
        input_output_aliases=aliases,
        compiler_params=pltpu.CompilerParams(vmem_limit_bytes=vmem * MIB),
        cost_estimate=pl.CostEstimate(flops=int(COSTS[name] * 1e9) + 1, bytes_accessed=int(COSTS[name] * 3e6) + 1, transcendentals=0),
        name=name,
    )(*scalars, *args, *after, *carry)
    return out[0] if single and not carry else out


def whole(*shape, buffers=None):
    mode = {} if buffers is None else dict(pipeline_mode=pl.Buffered(buffers))
    return pl.BlockSpec(shape, lambda i, *refs: (0,) * len(shape), **mode)


once = functools.partial(whole, buffers=1)


def each(*shape, per=1, shift=0):
    return pl.BlockSpec((per,) + shape, lambda i, *refs: (i + shift,) + (0,) * len(shape))


def sds(*shape, dtype=F32):
    return jax.ShapeDtypeStruct(shape, dtype)


def plan_kernel(place, routes, slots, rows_o, table_o):
    turned = place[0] == 1

    def mine_first(ref):
        v = ref[...]
        half = v.shape[0] // 2
        return jnp.where(turned, jnp.concatenate([v[half:], v[:half]], axis=0), v)

    route, slot = mine_first(routes), mine_first(slots)
    images = route.shape[0]
    key = jnp.where(slot >= 0, route * CAP + slot, -1)
    rows_o[...] = jnp.full(rows_o.shape, -1, jnp.int32)
    for i in range(images):
        rows_o[i, 0:1, 0:LEN] = key[i : i + 1]
        rows_o[i, 1:2, 0:LEN] = route[i : i + 1]
    lane = lane_iota(images, 128)
    table = jnp.zeros((images, 128), jnp.int32)
    slot_f = slot.astype(F32)
    for e in range(8):
        mine = (slot >= 0) & (route == e)
        low = jnp.min(jnp.where(mine, slot_f, float(CAP)), axis=-1, keepdims=True).astype(jnp.int32)
        high = jnp.max(jnp.where(mine, slot_f + 1.0, 0.0), axis=-1, keepdims=True).astype(jnp.int32)
        for n, (step, mask) in enumerate(((OUT_STEP, -8), (BACK_STEP, -16))):
            start = jnp.minimum(low & mask, CAP - step)
            passes = jnp.zeros_like(start)
            for k in range(-(-CAP // step) + 1):
                passes = passes + jnp.where(high - start > k * step, 1, 0)
            table = jnp.where(lane == 16 * n + e, start, table)
            table = jnp.where(lane == 16 * n + 8 + e, passes, table)
            table = jnp.where((lane == 32 + n) & (passes > 1), 1, table)
    table_o[...] = table


def plan(place, routes, slots):
    images = routes.shape[0]
    return call(
        plan_kernel, "plan", (routes, slots), [whole(*routes.shape)] * 2,
        (sds(images, 8, ROWS, dtype=jnp.int32), sds(images, 128, dtype=jnp.int32)),
        (whole(images, 8, ROWS), whole(images, 128)), scalars=(place,),
    )


def pack_kernel(proj, out, table, biases, o):
    rows = proj.shape[0]
    o[0:rows] = proj[...].astype(F32)
    o[rows:384] = out[...].astype(F32)
    o[384:392] = jnp.zeros((8, 384), F32)
    o[384:387, 0:REL] = table[...]
    o[387:389, 0 : biases.shape[1]] = biases[...]


def pack(proj, out, table, biases):
    args = (proj, out, table, biases)
    return call(pack_kernel, "pack", args, [once(*a.shape) for a in args], sds(392, 384), whole(392, 384))


def bias_kernel(place, sa, sb, sc, sd, params, hot, table_o, vecs_o, col_o, shards):
    for m, ref in enumerate((sa, sb, sc, sd)):
        shards[m ^ place[1]] = ref[...]
    heads = jnp.concatenate([shards[k][0:3, 0:256] for k in range(4)] + [jnp.zeros((4, 256), F32)], axis=0)
    high = heads.astype(BF16)
    mid = (heads - high.astype(F32)).astype(BF16)
    low = (heads - high.astype(F32) - mid.astype(F32)).astype(BF16)
    table_o[...] = dot(high, hot[...]) + dot(mid, hot[...]) + dot(low, hot[...])
    query = jnp.concatenate([shards[k][3:4, 0:96] for k in range(4)], axis=1)
    value = jnp.concatenate([shards[k][4:5, 0:96] for k in range(4)], axis=1)
    vecs_o[0:5] = params[0:5]
    vecs_o[5:6] = query
    vecs_o[6:7] = value
    vecs_o[7:8] = value
    col_o[...] = jnp.broadcast_to(to_column(value, 384), (384, 128))


def bias_tables(place, shares, params, hot):
    return call(
        bias_kernel, "bias_tables", (*shares, params, hot), [pl.BlockSpec((8, 384), lambda i, p: (48, 0))] * 4 + [once(8, 384), once(256, 4096)],
        (sds(16, 4096), sds(8, 384), sds(384, 128)), (whole(16, 4096), whole(8, 384), whole(384, 128)),
        scalars=(place,), scratch=[pltpu.VMEM((4, 8, 384), F32)],
    )


def offset_kernel(sums, hot, o):
    v = sums[...]
    high = v.astype(BF16)
    mid = (v - high.astype(F32)).astype(BF16)
    low = (v - high.astype(F32) - mid.astype(F32)).astype(BF16)
    o[...] = dot(high, hot[...], NT) + dot(mid, hot[...], NT) + dot(low, hot[...], NT)


def offset_sums(sums, hot):
    heads = sums.shape[0]
    return call(
        offset_kernel, "offset_sums", (sums, hot), [whole(*sums.shape), whole(*hot.shape)],
        sds(heads, 256), whole(heads, 256),
    )


def attention_kernel(
    place, patches, rows, wa, wb, wc, wd, table, mask, perm, perm_t, vecs, vcol, router_t,
    win_o, qkv_o, kt_o, att_o, mixt_o, x_o, h1_o, low2_o, gate_o, w_o, wt_o, wo_o, wot_o,
    block, pad, vt, bias,
):
    per = win_o.shape[0]
    images = 2 * per * pl.num_programs(0)

    @pl.when(pl.program_id(0) == 0)
    def _():
        split_lanes(block, patches[...].astype(F32))
        for m, ref in enumerate((wa, wb, wc, wd)):
            to = (m ^ place[1]) * 96
            for c in range(3):
                wt_o[pl.ds(pl.multiple_of(c * 384 + to, 32), 96), :] = ref[c * 96 : (c + 1) * 96, :].astype(BF16)
            wo_o[pl.ds(pl.multiple_of(to, 32), 96), :] = ref[288:384, :].astype(BF16)
        for c in range(3):
            w_o[:, c * 384 : (c + 1) * 384] = wt_o[c * 384 : (c + 1) * 384, :].T
        wot_o[...] = wo_o[...].T
        for w in range(4):
            for g in range(3):
                bias[w, g] = table[g] + mask[w]

    masks = head_masks()
    none = jnp.zeros((WROWS, 256), BF16)
    for n in range(per):
        at = place[0] * (images // 2) + pl.program_id(0) * per + n
        x = pad_rows(pad.at[n], image_rows(block, at, images))
        x_o[n] = x.astype(BF16)
        xhat, _ = layer_norm(x)
        low1 = (xhat * vecs[0:1] + vecs[1:2]).astype(BF16)
        win = dot(perm[...], low1).astype(BF16)
        win_o[n] = win
        packed = dot(win, w_o[...])
        qkv_o[n, :, 0:384] = (packed[:, 0:384] + vecs[5:6]).astype(BF16)
        qkv_o[n, :, 384:768] = packed[:, 384:768].astype(BF16)
        qkv_o[n, :, 768:1152] = (packed[:, 768:1152] + vecs[6:7]).astype(BF16)
        kt_o[n] = dot(wt_o[384:768, :], win, NT).astype(BF16)
        vt[n] = (dot(wt_o[768:1152, :], win, NT) + vcol[:, 0:1]).astype(BF16)
        for pair in range(2):
            for g in range(3):
                lanes = lambda c: slice(c * 384 + g * 128, c * 384 + g * 128 + 128)
                v4 = vt[n, g * 128 : (g + 1) * 128, pair * 128 : (pair + 1) * 128]
                wides = []
                for w in (2 * pair, 2 * pair + 1):
                    rs = slice(w * WROWS, (w + 1) * WROWS)
                    qs = spread(qkv_o[n, rs, lanes(0)], masks)
                    s = dot(qkv_o[n, rs, lanes(1)], qs, NT) * SCALE + bias[w, g]
                    e = jnp.exp(s - jnp.max(s, axis=0, keepdims=True))
                    low = (e * (1.0 / jnp.sum(e, axis=0, keepdims=True))).astype(BF16)
                    att_o[n, rs, g * 256 : (g + 1) * 256] = low
                    wides.append(dot(v4, jnp.concatenate([low, none] if w % 2 == 0 else [none, low], axis=0)))
                place_diagonal(mixt_o.at[n], wides, g * 128, pair)
        mixed = dot(perm_t[...], mixt_o[n], NT).astype(BF16)
        h1 = x + (dot(mixed, wo_o[...]) + vecs[2:3])
        h1_o[n] = h1
        xhat2, _ = layer_norm(h1)
        low2 = (xhat2 * vecs[3:4] + vecs[4:5]).astype(BF16)
        low2_o[n] = low2.astype(F32)
        logits = dot(router_t[...], low2, NT)[0:8]
        ex = jnp.exp(logits - jnp.max(logits, axis=0, keepdims=True))
        probs = ex / jnp.sum(ex, axis=0, keepdims=True)
        gate = jnp.sum(jnp.where(row_iota(8, ROWS) == rows[n, 1:2, :], probs, 0.0), axis=0, keepdims=True)
        hi = gate.astype(BF16).astype(F32)
        mid = (gate - hi).astype(BF16).astype(F32)
        gate_o[n, 0:1] = hi
        gate_o[n, 1:2] = mid
        gate_o[n, 2:3] = (gate - hi - mid).astype(BF16).astype(F32)
        gate_o[n, 3:8] = jnp.zeros((5, ROWS), F32)
        gate_o[n, 8:16] = probs


def attention_forward(place, patches, rows, ws, table, mask, perm, perm_t, vecs, vcol, router_t, images, after):
    per = 2
    bf = functools.partial(sds, dtype=BF16)
    out = functools.partial(each, per=per)
    return call(
        attention_kernel, "attention_forward",
        (patches, rows, *ws, table, mask, perm, perm_t, vecs, vcol, router_t),
        [once(*patches.shape), out(8, ROWS)] + [once(392, 384)] * 4
        + [once(*a.shape) for a in (table, mask, perm, perm_t, vecs, vcol, router_t)],
        (
            bf(images, 256, 384), bf(images, 256, 1152), bf(images, 384, 256), bf(images, 256, 768),
            bf(images, 384, 256), bf(images, ROWS, 384), sds(images, ROWS, 384), sds(images, ROWS, 384),
            sds(images, 16, ROWS), bf(384, 1152), bf(1152, 384), bf(384, 384), bf(384, 384),
        ),
        (
            out(256, 384), out(256, 1152), out(384, 256), out(256, 768), out(384, 256), out(ROWS, 384),
            out(ROWS, 384), out(ROWS, 384), out(16, ROWS),
            whole(384, 1152), whole(1152, 384), whole(384, 384), whole(384, 384),
        ),
        scalars=(place,), grid=(images // per,),
        scratch=[
            pltpu.VMEM((3, patches.shape[0], 128), F32),
            pltpu.VMEM((per, ROWS, 384), F32),
            pltpu.VMEM((per, 384, 256), BF16),
            pltpu.VMEM((4, 3, WROWS, 256), F32),
        ],
        after=after,
        vmem=60,
    )


def hits(keys, expert, first, base, step):
    code = row_iota(step, keys.shape[1]) + (expert * CAP + base)
    return jnp.where((code == keys) & (code >= expert * CAP + first), 1.0, 0.0).astype(BF16)


def to_slots(i, table, keys, tile, gates, acc, acc_gate):
    experts, step = acc.shape[0], OUT_STEP

    def store(e, base, moved, gated):
        at = pl.ds(pl.multiple_of(base, 8), step)
        acc[e, at, :] = acc[e, at, :] + moved
        if gates is not None:
            acc_gate[e, at, :] = acc_gate[e, at, :] + gated

    firsts = [table[i, e] for e in range(experts)]
    hit = jnp.concatenate([hits(keys, e, firsts[e], firsts[e], step) for e in range(experts)], axis=0)
    moved = dot(hit, tile)
    gated = None if gates is None else dot(hit, gates, NT)
    for e in range(experts):
        part = slice(e * step, (e + 1) * step)
        store(e, firsts[e], moved[part], None if gates is None else gated[part])

    @pl.when(table[i, 32] > 0)
    def _():
        def expert(e, _):
            def more(r, _):
                first = table[i, e] + r * step
                base = jnp.minimum(first, CAP - step)
                extra = hits(keys, e, first, base, step)
                store(e, base, dot(extra, tile), None if gates is None else dot(extra, gates, NT))
                return 0

            return lax.fori_loop(1, table[i, 8 + e], more, 0)

        lax.fori_loop(0, experts, expert, 0)


def cotangent_kernel(place, table, rows, cot, slots_o, tokens_o, block, acc):
    i = pl.program_id(0)
    per = tokens_o.shape[0]
    images = pl.num_programs(0) * per

    @pl.when(i == 0)
    def _():
        split_lanes(block, cot[...].astype(F32))
        acc[...] = jnp.zeros_like(acc)

    for n in range(per):
        at = lax.rem(i * per + n + place[0] * (images // 2), images)
        tokens_o[n] = jnp.zeros((ROWS, 384), BF16)
        tile = image_rows(block, at, images).astype(BF16)
        tokens_o[n, 0:LEN, :] = tile
        to_slots(i * per + n, table, rows[n, 0:1, 0:LEN], tile, None, acc, None)

    @pl.when(i == pl.num_programs(0) - 1)
    def _():
        slots_o[...] = acc[...].astype(BF16)


def dispatch_cotangent(place, table, rows, cot, experts, after):
    images = rows.shape[0]
    return call(
        cotangent_kernel, "dispatch_cotangent", (rows, cot), [each(8, ROWS, per=4), once(*cot.shape)],
        (sds(experts, CAP, 384, dtype=BF16), sds(images, ROWS, 384, dtype=BF16)),
        (whole(experts, CAP, 384), each(ROWS, 384, per=4)), scalars=(place, table), grid=(images // 4,),
        scratch=[pltpu.VMEM((3, cot.shape[0], 128), F32), pltpu.VMEM((experts, CAP, 384), F32)], after=after, vmem=28,
    )


def low2_kernel(first, offset, table, rows, data, gates, *refs):
    *before, slots_o, gate_o, acc = refs
    i = pl.program_id(0)
    per = data.shape[0]

    @pl.when(i == 0)
    def _():
        if first:
            acc[...] = jnp.zeros_like(acc)
            gate_o[...] = jnp.zeros_like(gate_o)
        else:
            acc[...] = before[0][...].astype(F32)
            gate_o[...] = before[1][...]

    for n in range(per):
        to_slots(
            offset + i * per + n, table, rows[n, 0:1, :], data[n].astype(BF16), gates[n].astype(BF16), acc, gate_o
        )

    @pl.when(i == pl.num_programs(0) - 1)
    def _():
        slots_o[...] = acc[...].astype(BF16)


def dispatch_low2(table, rows, data, gates, experts, before=(), after=()):
    images = data.shape[0]
    offset = images if before else 0
    return call(
        functools.partial(low2_kernel, not before, offset), "dispatch_low2", (rows, data, gates, *before),
        [each(8, ROWS, per=4, shift=offset // 4), each(ROWS, 384, per=4), each(16, ROWS, per=4)]
        + [once(*a.shape) for a in before],
        (sds(experts, CAP, 384, dtype=BF16), sds(experts, CAP, 16)),
        (whole(experts, CAP, 384), whole(experts, CAP, 16)), scalars=(table,), grid=(images // 4,),
        scratch=[pltpu.VMEM((experts, CAP, 384), F32)], after=after, vmem=32,
    )


def expert_kernel(place, buf, gates, gbuf, up, down, up_b, down_b, unused, gu_o, gd_o, rg_o, gdb_o):
    x = buf[0]
    gate = gates[0][:, 0:1] + gates[0][:, 1:2] + gates[0][:, 2:3]
    g = (gate * gbuf[0].astype(F32)).astype(BF16)
    gdb_o[0] = jnp.broadcast_to(jnp.sum(g.astype(F32), axis=0, keepdims=True), (8, 384))
    w_up, w_down = up[0], down[0]
    hp = dot(x, w_up) + up_b[0]
    c0 = np.float32(np.sqrt(2 / np.pi))
    th = jnp.tanh(c0 * (hp + 0.044715 * (hp * hp * hp)))
    act = (hp * (0.5 * (1.0 + th))).astype(BF16)
    slope = 0.5 * (1.0 + th) + (0.5 * hp) * (1.0 - th * th) * (c0 * (1.0 + (3 * 0.044715) * (hp * hp)))
    lead = jnp.where(place[1] == 0, 1.0, 0.0)
    rg_o[:, 0:384] = (dot(act, w_down) + lead * down_b[0]).astype(BF16)
    gd_o[...] = dot(act, g, TN)
    gp = (dot(g, w_down, NT) * slope).astype(BF16)
    gu_o[0:384] = dot(x, gp, TN)
    gu_o[384:392] = jnp.broadcast_to(jnp.sum(gp.astype(F32), axis=0, keepdims=True), (8, 384))
    rg_o[:, 384:768] = dot(gp, w_up, NT).astype(BF16)


def expert_pass(step, place, buf, gates, gbuf, up, down, up_b, down_b, sums, after):
    at = lambda *shape: pl.BlockSpec((1,) + shape, lambda i, p: (p[2 + step],) + (0,) * len(shape))
    return call(
        expert_kernel, "expert_pass", (buf, gates, gbuf, up, down, up_b, down_b, sums),
        [at(CAP, 384), at(CAP, 16), at(CAP, 384), at(384, 384), at(384, 384), at(1, 384), at(1, 384)]
        + [pl.BlockSpec(memory_space=pl.ANY)],
        (sds(392, 384), sds(384, 384), sds(CAP, 768, dtype=BF16), sds(*sums.shape)),
        (whole(392, 384), whole(384, 384), whole(CAP, 768), pl.BlockSpec((1, 8, 384), lambda i, p: (step, 0, 0))),
        scalars=(place,), after=after, aliases={8: 3},
    )


def back_to_tokens(i, place, table, key_row, cot, refs, windows, back):
    experts, step = len(refs), BACK_STEP
    keys = to_column(key_row.astype(F32), ROWS).astype(jnp.int32)
    lane = lane_iota(1, experts * step)
    code = jnp.zeros((1, experts * step), jnp.int32)
    for s in range(experts):
        e = place[2 + s]
        first = table[i, 16 + e]
        windows[s * step : (s + 1) * step, :] = refs[s][pl.ds(pl.multiple_of(first, 16), step), :]
        code = jnp.where(lane >= s * step, e * CAP + first + lane - s * step, code)
    back[...] = dot(jnp.where(code == keys, 1.0, 0.0).astype(BF16), windows[...])

    @pl.when(table[i, 33] > 0)
    def _():
        narrow = lane_iota(1, step)
        for s in range(experts):
            e = place[2 + s]

            def more(r, _):
                first = table[i, 16 + e] + r * step
                base = jnp.minimum(first, CAP - step)
                slot = narrow + base
                hit = (e * CAP + slot == keys) & (slot >= first)
                block = refs[s][pl.ds(pl.multiple_of(base, 16), step), :]
                back[...] = back[...] + dot(jnp.where(hit, 1.0, 0.0).astype(BF16), block)
                return 0

            lax.fori_loop(1, table[i, 24 + e], more, 0)

    tok, gl = back[:, 0:384], back[:, 384:768]
    dots = jnp.sum(tok * cot.astype(F32), axis=-1, keepdims=True)
    mark = jnp.concatenate([to_row(dots, ROWS), jnp.zeros((1, 384 - ROWS), F32)], axis=1)
    return jnp.where(row_iota(ROWS, 384) == LEN + 4, mark, gl), tok


def combine_far_kernel(offset, place, table, rows, cot, r0, r1, r2, r3, r4, r5, r6, r7, gl_o, tok_o, windows, back):
    refs = (r0, r1, r2, r3, r4, r5, r6, r7)
    per = gl_o.shape[0]
    for n in range(per):
        at = pl.program_id(0) * per + n + offset
        gl_o[n], tok_o[n] = back_to_tokens(at, place, table, rows[n, 0:1, :], cot[n], refs, windows.at[n], back.at[n])


def combine_scratch(experts):
    return [pltpu.VMEM((2, experts * BACK_STEP, 768), BF16), pltpu.VMEM((2, ROWS, 768), F32)]


def combine_far(place, table, rows, cot, results, after):
    images = rows.shape[0]
    half = images // 2
    return call(
        functools.partial(combine_far_kernel, half), "combine_far", (rows, cot, *results),
        [each(8, ROWS, per=2, shift=half // 2), each(ROWS, 384, per=2, shift=half // 2)] + [once(CAP, 768)] * len(results),
        (sds(half, ROWS, 384),) * 2, (each(ROWS, 384, per=2),) * 2, scalars=(place, table), grid=(half // 2,),
        scratch=combine_scratch(len(results)), after=after, vmem=20,
    )


def combine_own_kernel(
    place, table, rows, cot, r0, r1, r2, r3, r4, r5, r6, r7, gl_got, tok_got, g0, g1, g2, g3, tok_o, windows, back
):
    i = pl.program_id(0)
    refs = (r0, r1, r2, r3, r4, r5, r6, r7)
    parts = []
    for n in range(2):
        gl, tok = back_to_tokens(2 * i + n, place, table, rows[n, 0:1, :], cot[n], refs, windows.at[n], back.at[n])
        tok_o[n] = tok + tok_got[n]
        parts.append(gl + gl_got[n])
    for c, ref in enumerate((g0, g1, g2, g3)):

        @pl.when(i == c)
        def _():
            ref[0], ref[1] = parts


def combine_own(place, table, rows, cot, results, gl_got, tok_got, after):
    half = gl_got.shape[0]
    return call(
        combine_own_kernel, "combine_own", (rows, cot, *results, gl_got, tok_got),
        [each(8, ROWS, per=2), each(ROWS, 384, per=2)] + [once(CAP, 768)] * len(results) + [each(ROWS, 384, per=2)] * 2,
        (sds(2, ROWS, 384),) * 4 + (sds(half, ROWS, 384),), (whole(2, ROWS, 384),) * 4 + (each(ROWS, 384, per=2),),
        scalars=(place, table), grid=(half // 2,), scratch=combine_scratch(len(results)), after=after, vmem=24,
    )


def backward_kernel(
    first, offset, images, place, count, own, other, cot, rows, h1, low2_r, gate_r, mixt, win_r, qkv, kt, att, x_r,
    w, wt, wot, perm, perm_t, vecs, router_t,
    dw_i, dwo_i, dtb_i, dv_i, dr_i,
    gp_o, dw_o, dwo_o, dtb_o, dv_o, dr_o,
    dqt, dkv,
):
    for src, dst in ((dw_i, dw_o), (dwo_i, dwo_o), (dtb_i, dtb_o), (dv_i, dv_o), (dr_i, dr_o)):
        dst[...] = jnp.zeros(dst.shape, F32) if first else src[...]
    masks = head_masks()
    none = jnp.zeros((WROWS, 256), BF16)
    ones = jnp.ones((16, 256), BF16)

    def add(r, v):
        dv_o[r : r + 1, :] = dv_o[r : r + 1, :] + v

    for n in range(own.shape[0]):
        total = own[n] + other[n]
        gl = jnp.where(row_iota(ROWS, 384) < LEN, total, 0.0)
        gg = total[LEN + 4 : LEN + 5, 0:ROWS]
        at = place[0] * images + offset + n
        grad = cot[n].astype(F32) * jnp.where(at < count[0], 1.0, 0.0)
        probs = gate_r[n, 8:16]
        hot = jnp.where(row_iota(8, ROWS) == rows[n, 1:2, :], 1.0, 0.0)
        gate = jnp.sum(probs * hot, axis=0, keepdims=True)
        glog = jnp.concatenate([probs * (hot - gate) * gg, jnp.zeros((8, ROWS), F32)], axis=0).astype(BF16)
        low2 = low2_r[n].astype(BF16)
        dr_o[...] += dot(glog, low2)
        g2 = gl + dot(glog, router_t[...], TN)
        xhat2, inv2 = layer_norm(h1[n])
        add(3, jnp.sum(g2 * xhat2, axis=0, keepdims=True))
        add(4, jnp.sum(g2, axis=0, keepdims=True))
        gh1 = grad + norm_back(g2 * vecs[3:4], xhat2, inv2)
        gattn = gh1.astype(BF16)
        gwin = dot(perm[...], gattn).astype(BF16)
        add(2, dot(ones, gwin)[0:1])
        dwo_o[...] += dot(mixt[n], gwin)
        gmw = dot(gwin, wot[...]).astype(BF16)
        for g in range(3):
            lanes = lambda c: slice(c * 384 + g * 128, c * 384 + g * 128 + 128)
            table_sum = dtb_o[g]
            for pair in range(2):
                k4 = kt[n, g * 128 : (g + 1) * 128, pair * 128 : (pair + 1) * 128]
                wides = []
                for wi in (2 * pair, 2 * pair + 1):
                    rs = slice(wi * WROWS, (wi + 1) * WROWS)
                    qs = spread(qkv[n, rs, lanes(0)], masks)
                    dms = spread(gmw[rs, g * 128 : (g + 1) * 128], masks)
                    a_low = att[n, rs, g * 256 : (g + 1) * 256]
                    a = a_low.astype(F32)
                    da = dot(qkv[n, rs, lanes(2)], dms, NT)
                    ds = (a * (da - jnp.sum(da * a, axis=0, keepdims=True))).astype(BF16)
                    table_sum = table_sum + ds.astype(F32)
                    dkv[n, rs, g * 128 : (g + 1) * 128] = (SCALE * dot(ds, qs)).astype(BF16)
                    dkv[n, rs, 384 + g * 128 : 512 + g * 128] = dot(a_low, dms).astype(BF16)
                    wides.append(SCALE * dot(k4, jnp.concatenate([ds, none] if wi % 2 == 0 else [none, ds], axis=0)))
                place_diagonal(dqt.at[n], wides, g * 128, pair)
            dtb_o[g] = table_sum
        win = win_r[n]
        dw_o[0:384] += dot(dqt[n], win)
        dw_o[384:1152] += dot(dkv[n], win, TN)
        add(5, dot(ones, dqt[n], NT)[0:1])
        add(6, dot(ones, dkv[n, :, 384:768])[0:1])
        part = dot(dkv[n], wt[384:1152, :])
        hi = part.astype(BF16)
        lo = (part - hi.astype(F32)).astype(BF16)
        part_t = dot(w[:, 0:384], dqt[n])
        hi_t = part_t.astype(BF16)
        lo_t = (part_t - hi_t.astype(F32)).astype(BF16)
        pt = perm_t[...]
        gl1 = dot(pt, hi) + dot(pt, lo) + dot(pt, hi_t, NT) + dot(pt, lo_t, NT)
        xhat1, inv1 = layer_norm(x_r[n].astype(F32))
        add(0, jnp.sum(gl1 * xhat1, axis=0, keepdims=True))
        add(1, jnp.sum(gl1, axis=0, keepdims=True))
        gp_o[n] = gh1 + norm_back(gl1 * vecs[0:1], xhat1, inv1)


def attention_backward(first, c, place, count, own, other, cot, rows, saved, w, wt, wot, consts, acc, after, carry=()):
    per = own.shape[0]
    h1, low2, gates, mixt, win, qkv, kt, att, x = saved
    mine = functools.partial(each, per=per, shift=c)
    accs = [once(*a.shape) for a in acc]
    args = (own, other, cot, rows, h1, low2, gates, mixt, win, qkv, kt, att, x, w, wt, wot, *consts, *acc)
    specs = (
        [each(ROWS, 384, per=per)] * 2
        + [mine(*a.shape[1:]) for a in (cot, rows, h1, low2, gates, mixt, win, qkv, kt, att, x)]
        + [once(*a.shape) for a in (w, wt, wot, *consts)]
        + accs
    )
    lead = 2 + len(args) - len(acc)
    return call(
        functools.partial(backward_kernel, first, c * per, h1.shape[0]), "attention_backward", args, specs,
        (sds(per, ROWS, 384),) + tuple(sds(*a.shape) for a in acc), (each(ROWS, 384, per=per),) + tuple(whole(*a.shape) for a in acc),
        scalars=(place, count), scratch=[pltpu.VMEM((per, 384, 256), BF16), pltpu.VMEM((per, 256, 768), BF16)],
        after=after, carry=carry, vmem=32, aliases={lead + j: 1 + j for j in range(len(acc))},
    )


def add_arrays(a, b, blocks, after=(), carry=()):
    def kernel(x, y, o):
        o[...] = x[...] + y[...]

    rows = a.shape[0] // blocks
    spec = pl.BlockSpec((rows,) + a.shape[1:], lambda i: (i,) + (0,) * (a.ndim - 1))
    return call(kernel, "add", (a, b), [spec, spec], sds(*a.shape), spec, grid=(blocks,), after=after, carry=carry)


def hand_on(after, carry):
    def kernel(o):
        o[...] = jnp.zeros(o.shape, F32)

    return call(kernel, "hand_on", (), (), (sds(8, 128),), (whole(8, 128),), after=after, carry=carry)[1:]


def block_out_kernel(place, count, h1, gates, own, other, rows, o):
    per = o.shape[0]
    for n in range(per):
        i = pl.program_id(0) * per + n
        gate = gates[n, 0:1] + gates[n, 1:2] + gates[n, 2:3]
        weight = to_column(jnp.where(rows[n, 0:1] >= 0, gate, 0.0), ROWS)
        keep = jnp.where(place[0] * pl.num_programs(0) * per + i < count[0], 1.0, 0.0)
        value = keep * (h1[n] + weight * (own[n] + other[n]))
        o[n] = value.astype(BF16).astype(F32)


def block_out_pass(place, count, h1, gates, own, other, rows, after):
    images = h1.shape[0]
    return call(
        block_out_kernel, "block_out", (h1, gates, own, other, rows),
        [each(ROWS, 384, per=2), each(16, ROWS, per=2), each(ROWS, 384, per=2), each(ROWS, 384, per=2), each(8, ROWS, per=2)],
        sds(images, ROWS, 384), each(ROWS, 384, per=2), scalars=(place, count), grid=(images // 2,), after=after,
    )


def join_pass(place, own, other, dtype, after=()):
    images = 2 * sum(a.shape[0] for a in own)
    slab = lambda *lead: pl.BlockSpec(lead + (128,), lambda j, p: (0,) * len(lead) + (j,))

    def kernel(p, *refs):
        out = refs[len(own) + len(other)]
        wide = out if dtype == F32 else refs[-1]
        for side, group in ((0, refs[: len(own)]), (1, refs[len(own) : len(own) + len(other)])):
            at = (p[0] ^ side) * (images // 2)
            for ref in group:
                for n in range(ref.shape[0]):
                    wide[pl.ds(at, LEN, stride=images), :] = ref[n, 0:LEN, :]
                    at = at + 1
        if dtype != F32:
            out[...] = wide[...].astype(dtype)

    return call(
        kernel, "join", (*own, *other), [slab(a.shape[0], ROWS) for a in (*own, *other)],
        sds(LEN * images, 384, dtype=dtype), slab(LEN * images), scalars=(place,), grid=(3,),
        scratch=[] if dtype == F32 else [pltpu.VMEM((LEN * images, 128), F32)], after=after,
    )


def share_kernel(place, dw, dwo, by_offset, vec, router, downs, mine, far):
    for flip, out in ((0, mine), (1, far)):
        t = place[1] ^ flip
        at = pl.multiple_of(t * 96, 32)
        for c in range(3):
            out[c * 96 : (c + 1) * 96, :] = dw[pl.ds(pl.multiple_of(c * 384 + at, 32), 96), :]
        out[288:384, :] = dwo[pl.ds(at, 96), :]
        out[384:448, :] = jnp.zeros((64, 384), F32)
        for k in range(4):

            @pl.when(t == k)
            def _():
                out[384:387, 0:256] = by_offset[3 * k : 3 * k + 3, :]
                out[387:388, 0:96] = vec[5:6, 96 * k : 96 * k + 96]
                out[388:389, 0:96] = vec[6:7, 96 * k : 96 * k + 96]

        out[392:397, :] = vec[0:5, :]
        out[400:408, :] = router[0:8, :]
    for s in range(downs.shape[0]):
        mine[pl.ds(408 + place[2 + s], 1), :] = downs[s, 0:1, :]


def share_pass(place, dw, dwo, by_offset, vec, router, downs):
    args = (dw, dwo, by_offset, vec, router, downs)
    return call(
        share_kernel, "share", args, [once(*a.shape) for a in args],
        (sds(448, 384), sds(448, 384)), (whole(448, 384), whole(448, 384)), scalars=(place,),
    )


def halve_pass(own, got, bit, place, after=()):
    half = own.shape[0] // 2

    def kernel(p, a, b, send, keep):
        up = p[bit] != 0
        low = a[:half] + b[:half]
        high = a[half:] + b[half:]
        send[...] = jnp.where(up, low, high)
        keep[...] = jnp.where(up, high, low)

    return call(
        kernel, "halve", (own, got), [whole(*own.shape)] * 2, (sds(half, 384),) * 2, (whole(half, 384),) * 2,
        scalars=(place,), after=after,
    )


def double_pass(own, got, bit, place, after=()):
    rows = own.shape[0]

    def kernel(p, a, b, o):
        up = p[bit] != 0
        o[:rows] = jnp.where(up, b[...], a[...])
        o[rows:] = jnp.where(up, a[...], b[...])

    return call(
        kernel, "double", (own, got), [whole(*own.shape)] * 2, sds(2 * rows, 384), whole(2 * rows, 384),
        scalars=(place,), after=after,
    )


def gather_pass(place, ups, downs, shift, targets, after=()):
    count, experts = len(ups), 8

    def kernel(p, *refs):
        up_o, down_o, bias_o = refs[-3:]
        for k in range(count):

            @pl.when(pl.program_id(0) == k)
            def _():
                up_o[0] = refs[k][0:384, :]
                down_o[0] = refs[count + k][...]
                bias_o[0] = refs[k][384:392, :]

    at = lambda *shape: pl.BlockSpec((1,) + shape, lambda i, p: (p[2 + lax.rem(i + shift + experts - 1, experts)], 0, 0))
    anywhere = pl.BlockSpec(memory_space=pl.ANY)
    return call(
        kernel, "gather", (*ups, *downs, *targets),
        [once(392, 384)] * count + [once(384, 384)] * count + [anywhere] * len(targets),
        (sds(experts, 384, 384), sds(experts, 384, 384), sds(experts, 8, 384)), (at(384, 384), at(384, 384), at(8, 384)),
        scalars=(place,), grid=(count,), after=after, aliases={1 + 2 * count + j: j for j in range(len(targets))}, vmem=20,
    )


def swap_core(x):
    return lax.ppermute(x, "tensor", [(0, 1), (1, 0), (2, 3), (3, 2)])


def swap_chip(x):
    return lax.ppermute(x, "tensor", [(0, 2), (2, 0), (1, 3), (3, 1)])


def shape_back(values, length, images):
    return values.reshape(length, images, values.shape[-1]).transpose(1, 0, 2)


def on_device(
    n_dp, patches, image_count, routes, slot_index, norm1_gain, norm1_bias, input_proj, query_value_bias,
    position_bias, output_proj, output_bias, norm2_gain, norm2_bias, router_weight, up_weight, up_bias,
    down_weight, down_bias, cotangent,
):
    images, length, width = patches.shape
    half = images // 2
    experts = up_weight.shape[0]
    tensor = lax.axis_index("tensor")
    core = tensor % 2
    ring = n_dp == experts
    cycle = [0, 2, 4, 6, 7, 5, 3, 1]
    where = {d: i for i, d in enumerate(cycle)}
    dp = lax.axis_index("dp")
    spots = np.zeros((4 * n_dp, 16), np.int32)
    for d in range(n_dp):
        for t in range(4):
            rank = 0
            if ring:
                rank = where[d] if t % 2 == 0 else (n_dp - where[d]) % n_dp
            spots[4 * d + t, :13] = [t % 2, t] + [(rank - s) % experts for s in range(experts)] + [d >> b & 1 for b in range(3)]
    place = lax.dynamic_slice(jnp.asarray(spots), (4 * dp + tensor, 0), (1, 16)).reshape(16)
    if ring:
        pairs = []
        for d in range(n_dp):
            for t in range(4):
                to = cycle[(where[d] + (1 if t % 2 == 0 else -1)) % n_dp]
                pairs.append((d * 4 + t, to * 4 + t))
    onward = lambda v: lax.ppermute(v, ("dp", "tensor"), pairs)
    swap_dp = lambda v, bit: lax.ppermute(v, "dp", [(d, d ^ bit) for d in range(n_dp)])
    perm_np, mask_np, relative_np = window_tables()
    perm = jnp.asarray(perm_np, BF16)
    perm_t = jnp.asarray(perm_np.T, BF16)
    mask = jnp.asarray(mask_np)
    hot_np = np.arange(256)[:, None] == relative_np.reshape(1, -1)
    hot = jnp.asarray(hot_np, BF16)

    proj = pack(input_proj.transpose(1, 2, 0).reshape(-1, width), output_proj, position_bias.T, query_value_bias)
    proj_x = swap_chip(proj)
    proj_c = swap_core(proj)
    params = jnp.stack([norm1_gain, norm1_bias, output_bias, norm2_gain, norm2_bias] + [norm1_gain] * 3)
    router_t = jnp.pad(router_weight.T, ((0, 8), (0, 0)))

    rows, table = plan(place, routes, slot_index)
    flat = lambda v: v.transpose(1, 0, 2).reshape(length * images, width)
    gbuf, cot = dispatch_cotangent(place, table, rows, flat(cotangent), experts, ())
    (proj_x,) = hand_on((gbuf,), (proj_x,))
    proj_d = swap_core(proj_x)
    shares = (proj, proj_c, proj_x, proj_d)
    flat_table, vecs, vcol = bias_tables(place, shares, params, hot)
    bias = flat_table[0:12].reshape(3, 4, 64, 64).transpose(0, 2, 1, 3).reshape(3, 64, 256)
    win, qkv, kt, att, mixt, x, h1, low2, gates, w, wt, wo, wot = attention_forward(
        place, flat(patches), rows, shares, bias, mask, perm, perm_t, vecs, vcol, router_t, half, (gbuf,)
    )
    buf, slot_gates = dispatch_low2(table, rows, low2, gates, experts)
    buf, slot_gates = dispatch_low2(table, rows, swap_core(low2), swap_core(gates), experts, (buf, slot_gates))

    results, ups, downs, down_sums = [], [], [], [jnp.zeros((experts, 8, 384), F32)]
    up_b = up_bias.reshape(experts, 1, 384)
    down_b = down_bias.reshape(experts, 1, 384)

    def expert(s, last=None):
        after = () if last is None else (last,)
        gu, gd, rg, gdb = expert_pass(
            s, place, buf, slot_gates, gbuf, up_weight, down_weight, up_b, down_b, down_sums[0], after
        )
        results.append(rg)
        ups.append(gu)
        downs.append(gd)
        down_sums[0] = gdb
        return gdb

    flying, sums = {}, ([], [])
    steps = [0, 0]

    def serve(which, last, carry=(), also=()):
        if not ring:
            return (last, *carry) if carry else last
        steps[which] += 1
        step = steps[which]
        value = flying[which]
        if step < experts:
            value = add_arrays(value, (ups, downs)[which][step], 1 if which == 0 else 2, (last, *also), carry)
            if carry:
                value, *carry = value
        if step >= experts - 1:
            sums[which].append(value)
        if step < 2 * experts - 2:
            flying[which] = onward(value)
        return (value, *carry) if carry else value

    UP, DOWN = 0, 1
    last = expert(0)
    if ring:
        flying = {UP: onward(ups[0]), DOWN: onward(downs[0])}
    last = expert(2, expert(1, last))
    last = serve(UP, last)
    last = expert(3, last)
    last = serve(DOWN, last)
    last = expert(5, expert(4, last))
    last = serve(UP, last)
    last = expert(6, last)
    last = serve(DOWN, last)
    last = expert(7, last)
    gl_far, tok_far = combine_far(place, table, rows, cot, results, (last,))
    last, gl_far, tok_far = serve(UP, gl_far, (gl_far, tok_far))
    gl_got, tok_got = swap_core(gl_far), swap_core(tok_far)
    last = serve(DOWN, last)
    *gl, tok_mine = combine_own(place, table, rows, cot, results, gl_got, tok_got, (last,))
    their = [swap_chip(gl[0])]
    last, gl[1] = serve(UP, tok_mine, (gl[1],))
    their.append(swap_chip(gl[1]))
    last = serve(DOWN, last)
    last, gl[2] = serve(UP, last, (gl[2],), (their[0],))
    their.append(swap_chip(gl[2]))
    last = serve(DOWN, last)
    consts = (perm, perm_t, vecs, router_t)
    saved = (h1, low2, gates, mixt, win, qkv, kt, att, x)
    acc = [
        jnp.zeros((1152, 384), F32), jnp.zeros((384, 384), F32), jnp.zeros((3, 64, 256), F32),
        jnp.zeros((8, 384), F32), jnp.zeros((16, 384), F32),
    ]
    grads = []

    def backward(c, carry):
        gp, *more = attention_backward(
            c == 0, c, place, image_count, gl[c], their[c], cot, rows, saved, w, wt, wot, consts, acc, (last,), carry
        )
        acc[:] = more[:5]
        grads.append(gp)
        return more[5:]

    (gl[3],) = backward(0, (gl[3],))
    their.append(swap_chip(gl[3]))
    last = serve(DOWN, serve(UP, grads[-1]))
    backward(1, ())
    last = serve(DOWN, serve(UP, grads[-1]))
    backward(2, ())
    last = serve(DOWN, serve(UP, grads[-1]))
    (tok_mine,) = backward(3, (tok_mine,))
    tok_their = swap_chip(tok_mine)
    last = serve(DOWN, serve(UP, grads[-1]))
    gp_got = [swap_core(v) for v in grads]

    dw, dwo, dtb, dvec, drouter = acc
    by_offset = offset_sums(dtb.reshape(3, 64, 4, 64).transpose(0, 2, 1, 3).reshape(12, 4096), hot)
    mine, far = share_pass(place, dw, dwo, by_offset, dvec, drouter, down_sums[0])
    got = swap_core(far)
    if ring:
        turns = iter((1, 1, 1, 1, 2, 2))
        turn = 0

        def serve_some(last):
            nonlocal turn
            for _ in range(next(turns)):
                last = serve(turn % 2, last)
                turn += 1
            return last

        for b in range(3):
            send, mine = halve_pass(mine, got, 10 + b, place, (last,))
            got = swap_dp(send, 1 << b)
            last = serve_some(mine)
        total = add_arrays(mine, got, 1, (last,))
        for b in (2, 1, 0):
            got = swap_dp(total, 1 << b)
            last = serve_some(total)
            total = double_pass(total, got, 10 + b, place, (last,))
    else:
        total = lax.psum(mine + got, "dp")
    out_own = block_out_pass(place, image_count, h1, gates, tok_mine, tok_their, rows, (total,))
    grad_patches = join_pass(place, grads, gp_got, F32, (out_own,))
    block_out = join_pass(place, (out_own,), (swap_core(out_own),), BF16, (grad_patches,))
    if ring:
        while steps[DOWN] < 2 * experts - 2:
            last = serve(UP, last) if steps[UP] <= steps[DOWN] else serve(DOWN, last)
    if ring:
        early = 6
        targets = gather_pass(place, sums[UP][:early], sums[DOWN][:early], 0, (), (grad_patches,))
        grad_up, grad_down, bias8 = gather_pass(
            place, sums[UP][early:], sums[DOWN][early:], early, targets, (block_out,)
        )
        grad_up_bias = bias8[:, 0]
    if not ring:
        everything = lax.psum(jnp.concatenate([jnp.stack(ups), jnp.stack(downs)], axis=1), "dp")
        everything = jnp.take(everything, jnp.asarray([(0 - s) % experts for s in range(experts)]), axis=0)
        grad_up, grad_up_bias, grad_down = everything[:, 0:384], everything[:, 384], everything[:, 392:776]
    block_out, grad_patches = (shape_back(v, length, images) for v in (block_out, grad_patches))
    return (
        block_out,
        grad_patches,
        total[392],
        total[393],
        total[0:288].reshape(3, 96, 384).transpose(2, 0, 1),
        total[387:389, 0:96],
        total[384:387, 0:REL].T,
        total[288:384],
        total[394],
        total[395],
        total[396],
        total[400:408].T,
        grad_up,
        grad_up_bias,
        grad_down,
        total[408:416],
    )


def solution(mesh):
    in_specs = (
        P("dp", None, None), P("dp"), P("dp", None), P("dp", None), P(), P(), P(None, None, "tensor"),
        P(None, "tensor"), P(None, "tensor"), P("tensor", None), P(), P(), P(), P(), P(None, None, "tensor"),
        P(None, "tensor"), P(None, "tensor", None), P(), P("dp", None, None),
    )
    out_specs = (
        P("dp", None, None), P("dp", None, None), P(), P(), P(None, None, "tensor"), P(None, "tensor"),
        P(None, "tensor"), P("tensor", None), P(), P(), P(), P(), P(None, None, "tensor"), P(None, "tensor"),
        P(None, "tensor", None), P(),
    )
    return jax.shard_map(
        functools.partial(on_device, mesh.shape["dp"]),
        mesh=mesh, in_specs=in_specs, out_specs=out_specs, check_vma=False,
    )
```
